32 devices in a mesh: dp: 4 (over y, core), head: 2 (over x), blk: 4 (over z).
Axes of the slice: x: 2, y: 2, z: 4, core: 2. Of those that a mesh axis runs over, the one named last changes fastest.
Arguments:
- block_input: bfloat16 [2, 4, 1024, 2048], P(None, 'dp', ('head', 'blk')), may hold values from -6 to 6
- attention_gain: bfloat16 [2048], P(('dp', 'blk')), may hold values from 0.099609375 to 1.8984375
- query_weight: bfloat16 [2048, 2048], P(('dp', 'blk'), 'head'), may hold values from -0.125 to 0.125
- key_weight: bfloat16 [2048, 2048], P(('dp', 'blk'), 'head'), may hold values from -0.125 to 0.125
- value_weight: bfloat16 [2048, 2048], P(('dp', 'blk'), 'head'), may hold values from -0.125 to 0.125
- output_weight: bfloat16 [2048, 2048], P('head', ('dp', 'blk')), may hold values from -0.5 to 0.5
- mlp_gain: bfloat16 [2048], P(('dp', 'blk')), may hold values from 0.099609375 to 1.8984375
- gate_weight: bfloat16 [2048, 8192], P(('dp', 'blk'), 'head'), may hold values from -0.125 to 0.125
- up_weight: bfloat16 [2048, 8192], P(('dp', 'blk'), 'head'), may hold values from -0.125 to 0.125
- down_weight: bfloat16 [8192, 2048], P('head', ('dp', 'blk')), may hold values from -0.09375 to 0.09375
- grad_output: bfloat16 [2, 4, 1024, 2048], P(None, 'dp', ('head', 'blk')), may hold values from -6 to 6
Outputs:
- block_output: bfloat16 [2, 4, 1024, 2048], P(None, 'dp', ('head', 'blk'))
- input_grad: bfloat16 [2, 4, 1024, 2048], P(None, 'dp', ('head', 'blk'))
- attention_gain_grad: float32 [2048], P(('dp', 'blk'))
- query_weight_grad: float32 [2048, 2048], P(('dp', 'blk'), 'head')
- key_weight_grad: float32 [2048, 2048], P(('dp', 'blk'), 'head')
- value_weight_grad: float32 [2048, 2048], P(('dp', 'blk'), 'head')
- output_weight_grad: float32 [2048, 2048], P('head', ('dp', 'blk'))
- mlp_gain_grad: float32 [2048], P(('dp', 'blk'))
- gate_weight_grad: float32 [2048, 8192], P(('dp', 'blk'), 'head')
- up_weight_grad: float32 [2048, 8192], P(('dp', 'blk'), 'head')
- down_weight_grad: float32 [8192, 2048], P('head', ('dp', 'blk'))
The draws below stay inside these ranges and needn't reach their ends.
All inputs are finite; a program needn't handle non-finite values.
Results may differ from the reference program's by a relative error of at most 0.023.
Values may be sent and summed in bfloat16 or wider, within the bound.
A program may use at most 384 MiB of HBM per device.

```python
import math
import jax
import jax.numpy as jnp
from jax import lax

D = 2048
H = 32
HD = 64
FF = 8192
MICRO = 2
BATCH = 4
LENGTH = 1024


def block_scale(stream_key, shape, pieces, least, top_value):
    level = 1.0
    for axis_at, parts in pieces:
        heights = jax.random.uniform(jax.random.fold_in(jax.random.fold_in(stream_key, 6), axis_at), (parts,), jnp.float32, least / len(pieces), top_value / len(pieces))
        level = level * jnp.repeat(jnp.exp(heights), shape[axis_at] // parts).reshape((-1,) + (1,) * (len(shape) - 1 - axis_at))
    return level


def noise(key, dims, scale, limit, cuts=(), kind=jnp.bfloat16):
    drawn = scale * jax.random.normal(key, dims, jnp.float32)
    if cuts:
        drawn = drawn * block_scale(key, dims, cuts, -0.22, 0.18)
    return jnp.clip(drawn, -limit, limit).astype(kind)


def setup_inputs(seed: int = 0) -> dict:
    seeds = jax.random.split(jax.random.key(seed), 12)
    block_input = noise(seeds[0], (MICRO, BATCH, LENGTH, D), 1.0, 6.0, ((1, 4), (2, 8)))
    attention_gain = jnp.clip(1.0 + 0.18 * jax.random.normal(seeds[1], (D,), jnp.float32), 0.099609375, 1.8984375).astype(jnp.bfloat16)
    query_weight = noise(seeds[2], (D, H * HD), D ** -0.5, 0.125, ((0, 16), (1, 2)))
    key_weight = noise(seeds[3], (D, H * HD), D ** -0.5, 0.125, ((0, 16), (1, 2)))
    value_weight = noise(seeds[4], (D, H * HD), D ** -0.5, 0.125, ((0, 16), (1, 2)))
    output_weight = noise(seeds[5], (H * HD, D), (H * HD // 16) ** -0.5, 0.5, ((0, 2), (1, 16)))
    mlp_gain = jnp.clip(1.0 + 0.18 * jax.random.normal(seeds[6], (D,), jnp.float32), 0.099609375, 1.8984375).astype(jnp.bfloat16)
    gate_weight = noise(seeds[7], (D, FF), D ** -0.5, 0.125, ((0, 16), (1, 2)))
    up_weight = noise(seeds[8], (D, FF), D ** -0.5, 0.125, ((0, 16), (1, 2)))
    down_weight = noise(seeds[9], (FF, D), (FF // 2) ** -0.5, 0.09375, ((0, 2), (1, 16)))
    grad_output = noise(seeds[10], (MICRO, BATCH, LENGTH, D), 1.0, 6.0, ((1, 4), (2, 8)))
    return dict(block_input=block_input, attention_gain=attention_gain, query_weight=query_weight, key_weight=key_weight, value_weight=value_weight, output_weight=output_weight, mlp_gain=mlp_gain, gate_weight=gate_weight, up_weight=up_weight, down_weight=down_weight, grad_output=grad_output)


EPSILON = 1e-05
ROPE_BASE = 130000.0
MASKED_SCORE = -1e+30

@jax.custom_vjp
def low(v):
    return lax.optimization_barrier(v.astype(jnp.bfloat16)).astype(jnp.float32)

@jax.custom_vjp
def low_back(v):
    return v

def low_keep(v):
    return (low(v), None)

def low_pass(kept, grad):
    return (grad,)

def back_keep(v):
    return (v, None)

def backward_reduced(kept, grad):
    return (low(grad),)
low.defvjp(low_keep, low_pass)
low_back.defvjp(back_keep, backward_reduced)

def matmul(left_side, right_side):
    return jnp.dot(left_side, right_side, precision=lax.Precision.HIGHEST)

def rotate(flat_rows, positions):
    row_count = flat_rows.shape[0]
    half_width = HD // 2
    frequency = ROPE_BASE ** (-jnp.arange(half_width, dtype=jnp.float32) * 2.0 / HD)
    angles = positions[:, None] * frequency[None, :]
    cosine_table = jnp.cos(angles)[:, None, :]
    sine_table = jnp.sin(angles)[:, None, :]
    heads_view = flat_rows.reshape(row_count, H, HD)
    first_half = heads_view[..., :half_width]
    second_half = heads_view[..., half_width:]
    turned = jnp.concatenate([first_half * cosine_table - second_half * sine_table, second_half * cosine_table + first_half * sine_table], -1)
    return turned.reshape(row_count, H * HD)

def attend(queries, key_rows, value_rows):
    length = queries.shape[0]
    block_rows = math.gcd(512, length)
    key_positions = jnp.arange(length)

    def one_block(block_index):
        query_rows = lax.dynamic_slice_in_dim(queries, block_index * block_rows, block_rows, 0)
        raw_scores = jnp.einsum('qhd,khd->hqk', query_rows, key_rows, precision=lax.Precision.HIGHEST)
        scores = low_back(raw_scores) * HD ** (-0.5)
        query_positions = block_index * block_rows + jnp.arange(block_rows)
        visible = key_positions[None, None, :] <= query_positions[None, :, None]
        scores = jnp.where(visible, scores, MASKED_SCORE)
        row_top = lax.optimization_barrier(jnp.max(scores, -1, keepdims=True))
        exponent = jnp.exp(scores - row_top)
        probabilities = exponent / lax.optimization_barrier(jnp.sum(exponent, -1, keepdims=True))
        return jnp.einsum('hqk,khd->qhd', low(probabilities), value_rows, precision=lax.Precision.HIGHEST)
    attended = lax.map(jax.checkpoint(one_block), jnp.arange(length // block_rows))
    return attended.reshape(length, H * HD)

def layer(parameters, sequence):
    attention_gain, query_weight, key_weight, value_weight, output_weight, mlp_gain, gate_weight, up_weight, down_weight = parameters
    length = sequence.shape[0]
    positions = jnp.arange(length, dtype=jnp.float32)
    scale_one = lax.rsqrt(lax.optimization_barrier(jnp.mean(sequence * sequence, -1, keepdims=True)) + EPSILON)
    normed_one = low(sequence * scale_one * attention_gain)
    queries = low(rotate(low_back(matmul(normed_one, query_weight)), positions)).reshape(length, H, HD)
    key_rows = low(rotate(low_back(matmul(normed_one, key_weight)), positions)).reshape(length, H, HD)
    value_rows = low(low_back(matmul(normed_one, value_weight))).reshape(length, H, HD)
    attended = low(low_back(attend(queries, key_rows, value_rows)))
    mixed = sequence + low_back(matmul(attended, output_weight))
    scale_two = lax.rsqrt(lax.optimization_barrier(jnp.mean(mixed * mixed, -1, keepdims=True)) + EPSILON)
    normed_two = low(mixed * scale_two * mlp_gain)
    gate_lin = low_back(matmul(normed_two, gate_weight))
    up_lin = low_back(matmul(normed_two, up_weight))
    hidden = low(jax.nn.silu(gate_lin) * up_lin)
    return mixed + low_back(matmul(hidden, down_weight))

def reference(block_input, attention_gain, query_weight, key_weight, value_weight, output_weight, mlp_gain, gate_weight, up_weight, down_weight, grad_output):
    parameters = tuple((member.astype(jnp.float32) for member in (attention_gain, query_weight, key_weight, value_weight, output_weight, mlp_gain, gate_weight, up_weight, down_weight)))
    sequences = block_input.astype(jnp.float32).reshape(MICRO * BATCH, LENGTH, D)

    def forward(weights_now, inputs_now):
        return lax.map(jax.checkpoint(lambda sequence: layer(weights_now, sequence)), inputs_now)
    outputs, pullback = jax.vjp(forward, parameters, sequences)
    grads, grad_inputs = pullback(grad_output.astype(jnp.float32).reshape(MICRO * BATCH, LENGTH, D))
    return (outputs.reshape(block_input.shape).astype(jnp.bfloat16), grad_inputs.reshape(block_input.shape).astype(jnp.bfloat16), grads[0], grads[1], grads[2], grads[3], grads[4], grads[5], grads[6], grads[7], grads[8])
```

```python
import functools

import jax
import jax.numpy as jnp
import numpy as np
from jax import lax
from jax.experimental import pallas as pl
from jax.experimental.pallas import tpu as pltpu
from jax.sharding import PartitionSpec as P

HD = 64
EPSILON = 1e-05
ROPE_BASE = 130000.0
MASKED_SCORE = -1e30
F32 = jnp.float32
BF16 = jnp.bfloat16
LANES = 128


def swap(value, axis, bit):
    count = lax.axis_size(axis)
    return lax.ppermute(value, axis, [(i, i ^ bit) for i in range(count)])


def bits_of(count):
    return [1 << i for i in range(count.bit_length() - 1)]


def replica_stages():
    upper = [("blk", bit) for bit in bits_of(lax.axis_size("blk"))[1:]]
    return upper + [("dp", bit) for bit in reversed(bits_of(lax.axis_size("dp")))]


def matmul(left_side, right_side):
    return jnp.dot(left_side, right_side, preferred_element_type=F32)


def matmul_nt(left_side, right_side):
    return lax.dot_general(left_side, right_side, (((1,), (1,)), ((), ())), preferred_element_type=F32)


def matmul_tn(left_side, right_side):
    return lax.dot_general(left_side, right_side, (((0,), (0,)), ((), ())), preferred_element_type=F32)


def feature_order():
    n_blk, n_dp = lax.axis_size("blk"), lax.axis_size("dp")
    order = np.zeros((1,), np.int32)
    for axis, bit in replica_stages():
        order = np.concatenate([order, order ^ (bit if axis == "blk" else bit * n_blk)])
    order = np.concatenate([order, order ^ 1])
    assert order.size == n_blk * n_dp
    mine = lax.axis_index("dp") * n_blk + lax.axis_index("blk")
    back = np.argsort(order).astype(np.int32)
    absolute = jnp.arange(order.size, dtype=jnp.int32) ^ mine
    return jnp.asarray(order) ^ mine, jnp.asarray(back)[absolute]


def reorder_kernel(order_ref, source_ref, target_ref):
    target_ref[...] = source_ref[...]


def reorder(rows, order):
    count, width = rows.shape
    blocks = order.shape[0]
    piece = width // blocks
    if piece % LANES:
        return jnp.take(rows.reshape(count, blocks, piece), order, axis=1).reshape(count, width)
    return pl.pallas_call(
        reorder_kernel,
        grid_spec=pltpu.PrefetchScalarGridSpec(
            num_scalar_prefetch=1,
            grid=(blocks,),
            in_specs=[pl.BlockSpec((count, piece), lambda j, order_ref: (0, order_ref[j]))],
            out_specs=pl.BlockSpec((count, piece), lambda j, order_ref: (0, j)),
        ),
        out_shape=jax.ShapeDtypeStruct(rows.shape, rows.dtype),
    )(order, rows)


def turn_features(rows):
    half = rows.shape[1] // 2
    return jnp.concatenate([rows[:, half:], rows[:, :half]], 1)


def gather_tokens(rows, head_first):
    count = rows.shape[0]
    if head_first:
        other = swap(rows, "head", 1)
        far = swap(turn_features(jnp.concatenate([rows, other], 0)), "blk", 1)
        return jnp.concatenate([rows, far[:count], other, far[count:]], 0)
    both = jnp.concatenate([rows, swap(turn_features(rows), "blk", 1)], 0)
    return jnp.concatenate([both, swap(both, "head", 1)], 0)


def scatter_tokens(partial, head_first):
    partial = partial.astype(BF16)
    count = partial.shape[0] // 4
    if head_first:
        came = swap(partial[2 * count :], "head", 1)
        mine = partial[:count].astype(F32) + came[:count].astype(F32)
        theirs = (partial[count : 2 * count].astype(F32) + came[count:].astype(F32)).astype(BF16)
        return mine + swap(turn_features(theirs), "blk", 1).astype(F32)
    leaving = jnp.concatenate([partial[count : 2 * count], partial[3 * count :]], 0)
    came = swap(turn_features(leaving), "blk", 1)
    mine = partial[:count].astype(F32) + came[:count].astype(F32)
    theirs = (partial[2 * count : 3 * count].astype(F32) + came[count:].astype(F32)).astype(BF16)
    return mine + swap(theirs, "head", 1).astype(F32)


def own_and_other(columns):
    width = columns.shape[1] // 2
    place = lax.axis_index("blk") % 2
    return (
        lax.dynamic_slice_in_dim(columns, place * width, width, 1),
        lax.dynamic_slice_in_dim(columns, (1 - place) * width, width, 1),
    )


def gather_weight(own, other):
    streams = [own, swap(other, "blk", 1)]
    stages = replica_stages()
    for axis, bit in stages[:-1]:
        streams = [jnp.concatenate([held, swap(held, axis, bit)], 0) for held in streams]
    pieces = []
    for held in streams:
        pieces += [held, swap(held, *stages[-1])]
    return jnp.concatenate(pieces, 0)


def scatter_weight_grad(acts, grads):
    quarter = acts.shape[1] // 4
    stages = replica_stages()[::-1]

    def piece(place):
        return matmul_tn(acts[:, place * quarter : (place + 1) * quarter], grads).astype(BF16)

    streams = []
    for first in (2, 0):
        came = swap(piece(first + 1), *stages[0])
        held = piece(first).astype(F32) + came.astype(F32)
        for axis, bit in stages[1:]:
            half = held.shape[0] // 2
            held = held.astype(BF16)
            came = swap(held[half:], axis, bit)
            held = held[:half].astype(F32) + came.astype(F32)
        streams.append(held)
    return streams[1], swap(streams[0].astype(BF16), "blk", 1)


def side_by_side(own, other):
    other = other.astype(F32)
    low = lax.axis_index("blk") % 2 == 0
    return jnp.concatenate([jnp.where(low, own, other), jnp.where(low, other, own)], 1)


def head_groups():
    return lax.axis_size("blk") // 2


def to_sequences(parts):
    groups = head_groups()
    upper = lax.axis_index("blk") // 2
    width = parts[0].shape[1] // groups
    arrived = []
    for r in range(groups):
        chosen = jnp.stack([lax.dynamic_slice_in_dim(part, (upper ^ r) * width, width, 1) for part in parts])
        if r:
            chosen = lax.ppermute(chosen, "blk", [(i, i ^ (2 * r)) for i in range(2 * groups)])
        arrived.append(chosen.reshape(len(parts), 4, -1, width))
    return jnp.concatenate(arrived, 1)


def from_sequences(blocks):
    groups = head_groups()
    upper = lax.axis_index("blk") // 2
    count, _, tokens, width = blocks.shape
    arrived = []
    for r in range(groups):
        chosen = blocks[:, 4 * r : 4 * r + 4]
        if r:
            chosen = lax.ppermute(chosen, "blk", [(i, i ^ (2 * r)) for i in range(2 * groups)])
        arrived.append(chosen.reshape(count, 4 * tokens, width))
    stacked = jnp.stack(arrived)
    ordered = [lax.dynamic_index_in_dim(stacked, h ^ upper, 0, keepdims=False) for h in range(groups)]
    return jnp.concatenate(ordered, 2)


def block_order():
    n_blk, n_head = lax.axis_size("blk"), lax.axis_size("head")
    block = np.arange(n_blk * n_head, dtype=np.int32)
    r_head = (block // n_blk) ^ lax.axis_index("head")
    r_blk = (block % n_blk) ^ lax.axis_index("blk")
    return ((r_blk // 2) * 2 + r_head) * 2 + r_blk % 2


def rope_tables(length, lanes):
    half = HD // 2
    frequency = ROPE_BASE ** (-jnp.arange(half, dtype=F32) * 2.0 / HD)
    angles = jnp.arange(length, dtype=F32)[:, None] * frequency[None, :]
    cosine, sine = jnp.cos(angles), jnp.sin(angles)
    return (
        jnp.tile(cosine, (1, lanes // half)),
        jnp.tile(jnp.concatenate([-sine, sine], 1), (1, lanes // HD)),
    )


def turned(rows, cosine, sine):
    half = HD // 2
    parts = []
    for start in range(0, rows.shape[1], HD):
        parts += [rows[:, start + half : start + HD], rows[:, start : start + half]]
    return rows * cosine + jnp.concatenate(parts, 1) * sine


def load_sequence(order_ref, qkv_ref, cosine_ref, sine_ref, held, tokens, blocks):
    def one(block, carry):
        place = order_ref[block]
        rows = pl.ds(pl.multiple_of(block * tokens, tokens), tokens)
        for part in range(3):
            value = qkv_ref[part, place]
            if part < 2:
                value = turned(value.astype(F32), cosine_ref[rows, :], sine_ref[rows, :]).astype(BF16)
            held[part][rows, :] = value
        return carry

    lax.fori_loop(0, blocks, one, 0)


def softmax_rows(query, keys, first_row):
    scores = matmul_nt(query, keys) * HD ** (-0.5)
    row = first_row + lax.broadcasted_iota(jnp.int32, scores.shape, 0)
    scores = jnp.where(lax.broadcasted_iota(jnp.int32, scores.shape, 1) <= row, scores, MASKED_SCORE)
    weights = jnp.exp(scores - jnp.max(scores, 1, keepdims=True))
    return weights, 1.0 / jnp.sum(weights, 1, keepdims=True)


def attend_kernel(tokens, blocks, rows_at_once, order_ref, qkv_ref, cosine_ref, sine_ref, out_ref, q_s, k_s, v_s):
    lanes = qkv_ref.shape[-1]
    load_sequence(order_ref, qkv_ref, cosine_ref, sine_ref, (q_s, k_s, v_s), tokens, blocks)
    for first in range(0, tokens * blocks, rows_at_once):
        last = first + rows_at_once
        results = []
        for lane in range(0, lanes, HD):
            head = slice(lane, lane + HD)
            weights, inverse = softmax_rows(q_s[first:last, head], k_s[:last, head], first)
            results.append(matmul(weights.astype(BF16), v_s[:last, head]) * inverse)
        result = jnp.concatenate(results, 1).astype(BF16)
        for offset in range(0, rows_at_once, tokens):
            out_ref[order_ref[(first + offset) // tokens]] = result[offset : offset + tokens]


def attend_back_kernel(
    tokens, blocks, rows_at_once, order_ref, qkv_ref, grad_ref, cosine_ref, sine_ref, out_ref,
    q_s, k_s, v_s, dk_s, dv_s,
):
    lanes = qkv_ref.shape[-1]
    load_sequence(order_ref, qkv_ref, cosine_ref, sine_ref, (q_s, k_s, v_s), tokens, blocks)
    dk_s[...] = jnp.zeros_like(dk_s)
    dv_s[...] = jnp.zeros_like(dv_s)
    for first in range(0, tokens * blocks, rows_at_once):
        last = first + rows_at_once
        arrived = [grad_ref[order_ref[row // tokens]] for row in range(first, last, tokens)]
        grad_rows = jnp.concatenate(arrived, 0)
        query_parts, key_parts, value_parts = [], [], []
        for lane in range(0, lanes, HD):
            head = slice(lane, lane + HD)
            query, keys, grad = q_s[first:last, head], k_s[:last, head], grad_rows[:, head]
            weights, inverse = softmax_rows(query, keys, first)
            probabilities = weights * inverse
            grad_prob = matmul_nt(grad, v_s[:last, head])
            row_delta = jnp.sum(probabilities * grad_prob, 1, keepdims=True)
            grad_scores = (probabilities * (grad_prob - row_delta) * HD ** (-0.5)).astype(BF16)
            query_parts.append(matmul(grad_scores, keys))
            key_parts.append(matmul_tn(grad_scores, query))
            value_parts.append(matmul_tn(probabilities.astype(BF16), grad))
        grad_query = jnp.concatenate(query_parts, 1)
        grad_query = turned(grad_query, cosine_ref[first:last, :], -sine_ref[first:last, :]).astype(BF16)
        for offset in range(0, rows_at_once, tokens):
            out_ref[0, order_ref[(first + offset) // tokens]] = grad_query[offset : offset + tokens]
        dk_s[:last, :] += jnp.concatenate(key_parts, 1)
        dv_s[:last, :] += jnp.concatenate(value_parts, 1)

    def one(block, carry):
        place = order_ref[block]
        rows = pl.ds(pl.multiple_of(block * tokens, tokens), tokens)
        out_ref[1, place] = turned(dk_s[rows, :], cosine_ref[rows, :], -sine_ref[rows, :]).astype(BF16)
        out_ref[2, place] = dv_s[rows, :].astype(BF16)
        return carry

    lax.fori_loop(0, blocks, one, 0)


def attention_call(order, qkv, tables, grad=None):
    _, blocks, tokens, width = qkv.shape
    length = blocks * tokens
    lanes = min(LANES, width)
    rows_at_once = min(256, length)
    back = grad is not None

    def fixed(j, order_ref):
        return (0, 0)

    part = pl.BlockSpec((blocks, tokens, lanes), lambda j, order_ref: (0, 0, j))
    three = pl.BlockSpec((3, blocks, tokens, lanes), lambda j, order_ref: (0, 0, 0, j))
    table = pl.BlockSpec((length, lanes), fixed)
    kernel = attend_back_kernel if back else attend_kernel
    scratch = [pltpu.VMEM((length, lanes), BF16)] * 3
    if back:
        scratch += [pltpu.VMEM((length, lanes), F32)] * 2
    products = 5 if back else 2
    return pl.pallas_call(
        functools.partial(kernel, tokens, blocks, rows_at_once),
        grid_spec=pltpu.PrefetchScalarGridSpec(
            num_scalar_prefetch=1,
            grid=(width // lanes,),
            in_specs=[three] + ([part] if back else []) + [table, table],
            out_specs=three if back else part,
            scratch_shapes=scratch,
        ),
        out_shape=jax.ShapeDtypeStruct(qkv.shape if back else qkv.shape[1:], BF16),
        compiler_params=pltpu.CompilerParams(vmem_limit_bytes=48 * 1024 * 1024),
        cost_estimate=pl.CostEstimate(
            flops=products * 4 * length * length * width,
            bytes_accessed=(7 if back else 4) * length * width * 2,
            transcendentals=length * length * (width // HD),
        ),
    )(order, qkv, *([grad] if back else []), *tables)


def scale_of(values):
    return lax.rsqrt(jnp.mean(values * values, -1, keepdims=True) + EPSILON)


def norm_back(grad, values, scale):
    return scale * grad - values * (scale * scale * scale) * jnp.mean(grad * values, -1, keepdims=True)


def on_device(
    block_input,
    attention_gain,
    query_weight,
    key_weight,
    value_weight,
    output_weight,
    mlp_gain,
    gate_weight,
    up_weight,
    down_weight,
    grad_output,
):
    micros, _, tokens, width = block_input.shape
    heads_width = query_weight.shape[1] // 2
    length = tokens * lax.axis_size("blk") * lax.axis_size("head")
    to_own, to_absolute = feature_order()
    order = block_order()
    tables = rope_tables(length, min(LANES, heads_width // head_groups()))
    each = range(micros)
    head_first = [m % 2 == 1 for m in each]

    gain_one = attention_gain.astype(F32)[:, None]
    gain_two = mlp_gain.astype(F32)[:, None]

    def scaled(weight, gain):
        return (weight.astype(F32) * gain).astype(BF16)

    attention_parts = [own_and_other(scaled(w, gain_one)) for w in (query_weight, key_weight, value_weight)]
    qkv_full = gather_weight(*(jnp.concatenate(side, 1) for side in zip(*attention_parts)))
    output_full = gather_weight(*own_and_other(output_weight.T))
    gate_full = gather_weight(*own_and_other(scaled(gate_weight, gain_two)))
    up_full = gather_weight(*own_and_other(scaled(up_weight, gain_two)))
    down_full = gather_weight(*own_and_other(down_weight.T))

    inputs_low = reorder(block_input.reshape(micros * tokens, width), to_own).reshape(micros, tokens, width)
    grad_low = reorder(grad_output.reshape(micros * tokens, width), to_own).reshape(micros, tokens, width)
    inputs = [inputs_low[m].astype(F32) for m in each]
    scale_one = [scale_of(inputs[m]) for m in each]
    normed_one = [gather_tokens((inputs[m] * scale_one[m]).astype(BF16), head_first[m]) for m in each]

    sequences = []
    for m in each:
        qkv = matmul(normed_one[m], qkv_full).astype(BF16)
        parts = [qkv[:, i * heads_width : (i + 1) * heads_width] for i in range(3)]
        sequences.append(to_sequences(parts))
    attended = [from_sequences(attention_call(order, sequences[m], tables)[None])[0] for m in each]
    mixed = [
        inputs[m] + scatter_tokens(matmul_nt(attended[m], output_full), head_first[m]) for m in each
    ]
    scale_two = [scale_of(mixed[m]) for m in each]
    normed_two = [gather_tokens((mixed[m] * scale_two[m]).astype(BF16), head_first[m]) for m in each]
    grad_rows = [gather_tokens(grad_low[m], head_first[m]) for m in each]

    hidden, grad_gate, grad_up, grad_mixed, outputs = [], [], [], [], []
    for m in each:
        gate = matmul(normed_two[m], gate_full)
        up = matmul(normed_two[m], up_full)
        sigmoid = jax.nn.sigmoid(gate)
        activated = gate * sigmoid
        hidden.append((activated * up).astype(BF16))
        grad_hidden = matmul(grad_rows[m], down_full)
        grad_gate.append((grad_hidden * up * sigmoid * (1.0 + gate * (1.0 - sigmoid))).astype(BF16))
        grad_up.append((grad_hidden * activated).astype(BF16))
        grad_normed = matmul_nt(grad_gate[m], gate_full) + matmul_nt(grad_up[m], up_full)
        grad_normed = scatter_tokens(grad_normed, head_first[m])
        grad_mixed.append(grad_low[m].astype(F32) + norm_back(grad_normed, mixed[m], scale_two[m]))
    for m in each:
        outputs.append(
            (mixed[m] + scatter_tokens(matmul_nt(hidden[m], down_full), head_first[m])).astype(BF16)
        )

    def joined(parts):
        return jnp.concatenate(parts, 0)

    normed_two_all = joined(normed_two)
    gate_grad = scatter_weight_grad(normed_two_all, joined(grad_gate))
    up_grad = scatter_weight_grad(normed_two_all, joined(grad_up))
    down_grad = scatter_weight_grad(joined(grad_rows), joined(hidden))

    grad_mixed_rows = [gather_tokens(grad_mixed[m].astype(BF16), head_first[m]) for m in each]
    grad_qkv, input_grads = [], []
    for m in each:
        grad_attended = matmul(grad_mixed_rows[m], output_full).astype(BF16)
        grad_sequences = attention_call(order, sequences[m], tables, to_sequences([grad_attended])[0])
        returned = from_sequences(grad_sequences)
        grad_qkv.append(jnp.concatenate([returned[0], returned[1], returned[2]], 1))
        grad_normed = scatter_tokens(matmul_nt(grad_qkv[m], qkv_full), head_first[m])
        input_grads.append((grad_mixed[m] + norm_back(grad_normed, inputs[m], scale_one[m])).astype(BF16))
    output_grad = scatter_weight_grad(joined(grad_mixed_rows), joined(attended))
    qkv_grad = scatter_weight_grad(joined(normed_one), joined(grad_qkv))

    qkv_grads = [
        side_by_side(*(side[:, i * heads_width : (i + 1) * heads_width] for side in qkv_grad)) for i in range(3)
    ]
    mlp_grads = [side_by_side(*gate_grad), side_by_side(*up_grad)]

    def gain_grad(weights, grads):
        terms = [jnp.sum(w.astype(F32) * g, 1) for w, g in zip(weights, grads)]
        here = functools.reduce(jnp.add, terms)
        return here + swap(here, "head", 1)

    attention_gain_grad = gain_grad((query_weight, key_weight, value_weight), qkv_grads)
    mlp_gain_grad = gain_grad((gate_weight, up_weight), mlp_grads)

    def absolute(parts):
        rows = reorder(joined(parts), to_absolute)
        return rows.reshape(micros, 1, tokens, width)

    return (
        absolute(outputs),
        absolute(input_grads),
        attention_gain_grad,
        qkv_grads[0] * gain_one,
        qkv_grads[1] * gain_one,
        qkv_grads[2] * gain_one,
        side_by_side(*output_grad).T,
        mlp_gain_grad,
        mlp_grads[0] * gain_two,
        mlp_grads[1] * gain_two,
        side_by_side(*down_grad).T,
    )


def solution(mesh):
    rows, row_split = P(None, "dp", ("head", "blk"), None), P(("dp", "blk"), "head")
    column_split, gain = P("head", ("dp", "blk")), P(("dp", "blk"))
    return jax.shard_map(
        on_device,
        mesh=mesh,
        in_specs=(
            rows, gain, row_split, row_split, row_split, column_split, gain, row_split, row_split, column_split, rows,
        ),
        out_specs=(
            rows, rows, gain, row_split, row_split, row_split, column_split, gain, row_split, row_split, column_split,
        ),
        check_vma=False,
    )
```

```python
import functools

import jax
import jax.numpy as jnp
import numpy as np
from jax import lax
from jax.experimental import pallas as pl
from jax.experimental.pallas import tpu as pltpu
from jax.sharding import PartitionSpec as P

HD = 64
EPSILON = 1e-05
ROPE_BASE = 130000.0
MASKED_SCORE = -1e30
F32 = jnp.float32
BF16 = jnp.bfloat16
LANES = 128
MESH = pl.DeviceIdType.MESH


def swap(value, axis, bit):
    count = lax.axis_size(axis)
    return lax.ppermute(value, axis, [(i, i ^ bit) for i in range(count)])


def bits_of(count):
    return [1 << i for i in range(count.bit_length() - 1)]


def replica_stages():
    upper = [("blk", bit) for bit in bits_of(lax.axis_size("blk"))[1:]]
    return upper + [("dp", bit) for bit in reversed(bits_of(lax.axis_size("dp")))]


def matmul(left_side, right_side):
    return jnp.dot(left_side, right_side, preferred_element_type=F32)


def matmul_nt(left_side, right_side):
    return lax.dot_general(left_side, right_side, (((1,), (1,)), ((), ())), preferred_element_type=F32)


def matmul_tn(left_side, right_side):
    return lax.dot_general(left_side, right_side, (((0,), (0,)), ((), ())), preferred_element_type=F32)


def feature_order():
    n_blk, n_dp = lax.axis_size("blk"), lax.axis_size("dp")
    order = np.zeros((1,), np.int32)
    for axis, bit in replica_stages():
        order = np.concatenate([order, order ^ (bit if axis == "blk" else bit * n_blk)])
    order = np.concatenate([order, order ^ 1])
    assert order.size == n_blk * n_dp
    mine = lax.axis_index("dp") * n_blk + lax.axis_index("blk")
    back = np.argsort(order).astype(np.int32)
    absolute = jnp.arange(order.size, dtype=jnp.int32) ^ mine
    return jnp.asarray(order) ^ mine, jnp.asarray(back)[absolute]


def reorder_kernel(order_ref, source_ref, target_ref):
    target_ref[...] = source_ref[...]


def reorder(rows, order):
    count, width = rows.shape
    blocks = order.shape[0]
    piece = width // blocks
    if piece % LANES:
        return jnp.take(rows.reshape(count, blocks, piece), order, axis=1).reshape(count, width)
    return pl.pallas_call(
        reorder_kernel,
        grid_spec=pltpu.PrefetchScalarGridSpec(
            num_scalar_prefetch=1,
            grid=(blocks,),
            in_specs=[pl.BlockSpec((count, piece), lambda j, order_ref: (0, order_ref[j]))],
            out_specs=pl.BlockSpec((count, piece), lambda j, order_ref: (0, j)),
        ),
        out_shape=jax.ShapeDtypeStruct(rows.shape, rows.dtype),
    )(order, rows)


def turn_features(rows):
    half = rows.shape[1] // 2
    return jnp.concatenate([rows[:, half:], rows[:, :half]], 1)


def gather_tokens(rows, head_first):
    count = rows.shape[0]
    if head_first:
        other = swap(rows, "head", 1)
        far = swap(turn_features(jnp.concatenate([rows, other], 0)), "blk", 1)
        return jnp.concatenate([rows, far[:count], other, far[count:]], 0)
    both = jnp.concatenate([rows, swap(turn_features(rows), "blk", 1)], 0)
    return jnp.concatenate([both, swap(both, "head", 1)], 0)


def scatter_tokens(partial, head_first):
    partial = partial.astype(BF16)
    count = partial.shape[0] // 4
    if head_first:
        came = swap(partial[2 * count :], "head", 1)
        mine = partial[:count].astype(F32) + came[:count].astype(F32)
        theirs = (partial[count : 2 * count].astype(F32) + came[count:].astype(F32)).astype(BF16)
        return mine + swap(turn_features(theirs), "blk", 1).astype(F32)
    leaving = jnp.concatenate([partial[count : 2 * count], partial[3 * count :]], 0)
    came = swap(turn_features(leaving), "blk", 1)
    mine = partial[:count].astype(F32) + came[:count].astype(F32)
    theirs = (partial[2 * count : 3 * count].astype(F32) + came[count:].astype(F32)).astype(BF16)
    return mine + swap(theirs, "head", 1).astype(F32)


def own_and_other(columns):
    width = columns.shape[1] // 2
    place = lax.axis_index("blk") % 2
    return (
        lax.dynamic_slice_in_dim(columns, place * width, width, 1),
        lax.dynamic_slice_in_dim(columns, (1 - place) * width, width, 1),
    )


def gather_weight(own, other):
    streams = [own, swap(other, "blk", 1)]
    stages = replica_stages()
    for axis, bit in stages[:-1]:
        streams = [jnp.concatenate([held, swap(held, axis, bit)], 0) for held in streams]
    pieces = []
    for held in streams:
        pieces += [held, swap(held, *stages[-1])]
    return jnp.concatenate(pieces, 0)


def scatter_weight_grad(acts, grads):
    quarter = acts.shape[1] // 4
    stages = replica_stages()[::-1]

    def piece(place):
        return matmul_tn(acts[:, place * quarter : (place + 1) * quarter], grads).astype(BF16)

    streams = []
    for first in (2, 0):
        came = swap(piece(first + 1), *stages[0])
        held = piece(first).astype(F32) + came.astype(F32)
        for axis, bit in stages[1:]:
            half = held.shape[0] // 2
            held = held.astype(BF16)
            came = swap(held[half:], axis, bit)
            held = held[:half].astype(F32) + came.astype(F32)
        streams.append(held)
    return streams[1], swap(streams[0].astype(BF16), "blk", 1)


def side_by_side(own, other):
    other = other.astype(F32)
    low = lax.axis_index("blk") % 2 == 0
    return jnp.concatenate([jnp.where(low, own, other), jnp.where(low, other, own)], 1)


def head_groups():
    return lax.axis_size("blk") // 2


def to_sequences(parts):
    groups = head_groups()
    upper = lax.axis_index("blk") // 2
    width = parts[0].shape[1] // groups
    arrived = []
    for r in range(groups):
        chosen = jnp.stack([lax.dynamic_slice_in_dim(part, (upper ^ r) * width, width, 1) for part in parts])
        if r:
            chosen = lax.ppermute(chosen, "blk", [(i, i ^ (2 * r)) for i in range(2 * groups)])
        arrived.append(chosen.reshape(len(parts), 4, -1, width))
    return jnp.concatenate(arrived, 1)


def from_sequences(blocks):
    groups = head_groups()
    upper = lax.axis_index("blk") // 2
    count, _, tokens, width = blocks.shape
    arrived = []
    for r in range(groups):
        chosen = blocks[:, 4 * r : 4 * r + 4]
        if r:
            chosen = lax.ppermute(chosen, "blk", [(i, i ^ (2 * r)) for i in range(2 * groups)])
        arrived.append(chosen.reshape(count, 4 * tokens, width))
    stacked = jnp.stack(arrived)
    ordered = [lax.dynamic_index_in_dim(stacked, h ^ upper, 0, keepdims=False) for h in range(groups)]
    return jnp.concatenate(ordered, 2)


def block_order():
    n_blk, n_head = lax.axis_size("blk"), lax.axis_size("head")
    block = np.arange(n_blk * n_head, dtype=np.int32)
    r_head = (block // n_blk) ^ lax.axis_index("head")
    r_blk = (block % n_blk) ^ lax.axis_index("blk")
    return ((r_blk // 2) * 2 + r_head) * 2 + r_blk % 2


def rope_tables(length, lanes):
    half = HD // 2
    frequency = ROPE_BASE ** (-jnp.arange(half, dtype=F32) * 2.0 / HD)
    angles = jnp.arange(length, dtype=F32)[:, None] * frequency[None, :]
    cosine, sine = jnp.cos(angles), jnp.sin(angles)
    return (
        jnp.tile(cosine, (1, lanes // half)),
        jnp.tile(jnp.concatenate([-sine, sine], 1), (1, lanes // HD)),
    )


def turned(rows, cosine, sine):
    half = HD // 2
    parts = []
    for start in range(0, rows.shape[1], HD):
        parts += [rows[:, start + half : start + HD], rows[:, start : start + half]]
    return rows * cosine + jnp.concatenate(parts, 1) * sine


def load_sequence(order_ref, qkv_ref, cosine_ref, sine_ref, held, tokens, blocks):
    def one(block, carry):
        place = order_ref[block]
        rows = pl.ds(pl.multiple_of(block * tokens, tokens), tokens)
        for part in range(3):
            value = qkv_ref[part, place]
            if part < 2:
                value = turned(value.astype(F32), cosine_ref[rows, :], sine_ref[rows, :]).astype(BF16)
            held[part][rows, :] = value
        return carry

    lax.fori_loop(0, blocks, one, 0)


def softmax_rows(query, keys, first_row):
    scores = matmul_nt(query, keys) * HD ** (-0.5)
    row = first_row + lax.broadcasted_iota(jnp.int32, scores.shape, 0)
    scores = jnp.where(lax.broadcasted_iota(jnp.int32, scores.shape, 1) <= row, scores, MASKED_SCORE)
    weights = jnp.exp(scores - jnp.max(scores, 1, keepdims=True))
    return weights, 1.0 / jnp.sum(weights, 1, keepdims=True)


def attend_kernel(tokens, blocks, rows_at_once, order_ref, qkv_ref, cosine_ref, sine_ref, out_ref, q_s, k_s, v_s):
    lanes = qkv_ref.shape[-1]
    load_sequence(order_ref, qkv_ref, cosine_ref, sine_ref, (q_s, k_s, v_s), tokens, blocks)
    for first in range(0, tokens * blocks, rows_at_once):
        last = first + rows_at_once
        results = []
        for lane in range(0, lanes, HD):
            head = slice(lane, lane + HD)
            weights, inverse = softmax_rows(q_s[first:last, head], k_s[:last, head], first)
            results.append(matmul(weights.astype(BF16), v_s[:last, head]) * inverse)
        result = jnp.concatenate(results, 1).astype(BF16)
        for offset in range(0, rows_at_once, tokens):
            out_ref[order_ref[(first + offset) // tokens]] = result[offset : offset + tokens]


def attend_back_kernel(
    tokens, blocks, rows_at_once, order_ref, qkv_ref, grad_ref, cosine_ref, sine_ref, out_ref,
    q_s, k_s, v_s, dk_s, dv_s,
):
    lanes = qkv_ref.shape[-1]
    load_sequence(order_ref, qkv_ref, cosine_ref, sine_ref, (q_s, k_s, v_s), tokens, blocks)
    dk_s[...] = jnp.zeros_like(dk_s)
    dv_s[...] = jnp.zeros_like(dv_s)
    for first in range(0, tokens * blocks, rows_at_once):
        last = first + rows_at_once
        arrived = [grad_ref[order_ref[row // tokens]] for row in range(first, last, tokens)]
        grad_rows = jnp.concatenate(arrived, 0)
        query_parts, key_parts, value_parts = [], [], []
        for lane in range(0, lanes, HD):
            head = slice(lane, lane + HD)
            query, keys, grad = q_s[first:last, head], k_s[:last, head], grad_rows[:, head]
            weights, inverse = softmax_rows(query, keys, first)
            probabilities = weights * inverse
            grad_prob = matmul_nt(grad, v_s[:last, head])
            row_delta = jnp.sum(probabilities * grad_prob, 1, keepdims=True)
            grad_scores = (probabilities * (grad_prob - row_delta) * HD ** (-0.5)).astype(BF16)
            query_parts.append(matmul(grad_scores, keys))
            key_parts.append(matmul_tn(grad_scores, query))
            value_parts.append(matmul_tn(probabilities.astype(BF16), grad))
        grad_query = jnp.concatenate(query_parts, 1)
        grad_query = turned(grad_query, cosine_ref[first:last, :], -sine_ref[first:last, :]).astype(BF16)
        for offset in range(0, rows_at_once, tokens):
            out_ref[0, order_ref[(first + offset) // tokens]] = grad_query[offset : offset + tokens]
        dk_s[:last, :] += jnp.concatenate(key_parts, 1)
        dv_s[:last, :] += jnp.concatenate(value_parts, 1)

    def one(block, carry):
        place = order_ref[block]
        rows = pl.ds(pl.multiple_of(block * tokens, tokens), tokens)
        out_ref[1, place] = turned(dk_s[rows, :], cosine_ref[rows, :], -sine_ref[rows, :]).astype(BF16)
        out_ref[2, place] = dv_s[rows, :].astype(BF16)
        return carry

    lax.fori_loop(0, blocks, one, 0)


def attention_call(order, qkv, tables, grad=None):
    _, blocks, tokens, width = qkv.shape
    length = blocks * tokens
    lanes = min(LANES, width)
    rows_at_once = min(256, length) if length <= 2048 else LANES
    back = grad is not None

    def fixed(j, order_ref):
        return (0, 0)

    part = pl.BlockSpec((blocks, tokens, lanes), lambda j, order_ref: (0, 0, j))
    three = pl.BlockSpec((3, blocks, tokens, lanes), lambda j, order_ref: (0, 0, 0, j))
    table = pl.BlockSpec((length, lanes), fixed)
    kernel = attend_back_kernel if back else attend_kernel
    scratch = [pltpu.VMEM((length, lanes), BF16)] * 3
    if back:
        scratch += [pltpu.VMEM((length, lanes), F32)] * 2
    products = 5 if back else 2
    return pl.pallas_call(
        functools.partial(kernel, tokens, blocks, rows_at_once),
        grid_spec=pltpu.PrefetchScalarGridSpec(
            num_scalar_prefetch=1,
            grid=(width // lanes,),
            in_specs=[three] + ([part] if back else []) + [table, table],
            out_specs=three if back else part,
            scratch_shapes=scratch,
        ),
        out_shape=jax.ShapeDtypeStruct(qkv.shape if back else qkv.shape[1:], BF16),
        compiler_params=pltpu.CompilerParams(vmem_limit_bytes=48 * 1024 * 1024),
        cost_estimate=pl.CostEstimate(
            flops=products * 4 * length * length * width,
            bytes_accessed=(7 if back else 4) * length * width * 2,
            transcendentals=length * length * (width // HD),
        ),
    )(order, qkv, *([grad] if back else []), *tables)


def greet():
    masks = [("head", 1)] + [("dp", bit) for bit in bits_of(lax.axis_size("dp"))]
    masks += [("blk", 1)] + [("blk", 2 * r) for r in range(1, head_groups())]
    barrier = pltpu.get_barrier_semaphore()
    for axis, mask in masks:
        pl.semaphore_signal(barrier, inc=1, device_id={axis: flipped(axis, mask)}, device_id_type=MESH)
    pl.semaphore_wait(barrier, len(masks))


def flipped(axis, mask):
    place, other = lax.axis_index(axis), 0
    for bit in bits_of(lax.axis_size(axis)):
        digit = (place // bit) % 2
        other = other + bit * ((1 - digit) if mask & bit else digit)
    return other


class Copies:
    def __init__(self, send, recv, local):
        self.send, self.recv, self.local = send, recv, local
        self.remote_count = self.local_count = 0
        self.sent = []

    def remote(self, source, target, axis, mask):
        k = self.remote_count
        self.remote_count += 1
        copy = pltpu.make_async_remote_copy(
            src_ref=source, dst_ref=target, send_sem=self.send.at[k], recv_sem=self.recv.at[k],
            device_id={axis: flipped(axis, mask)}, device_id_type=MESH,
        )
        copy.start()
        self.sent.append(copy)
        return copy

    def inside(self, source, target):
        copy = pltpu.make_async_copy(source, target, self.local.at[self.local_count])
        self.local_count += 1
        copy.start()
        return copy

    def finish(self):
        for copy in self.sent:
            copy.wait_send()


def halves_turned(rows):
    half = rows.shape[-1] // 2
    return jnp.concatenate([rows[:, half:], rows[:, :half]], 1)


class WeightGather:
    def __init__(self, copies, own, other, full):
        self.copies, self.full, self.stage = copies, full, 0
        self.mine = copies.inside(own, full.at[0, 0])
        self.copy = copies.remote(other, full.at[1, 0], "blk", 1)

    def advance(self):
        if self.mine is not None:
            self.mine.wait()
            self.mine = None
        self.copy.wait_recv()
        stages = replica_stages()
        if self.stage < len(stages):
            held = 1 << self.stage
            self.copy = self.copies.remote(
                self.full.at[:, 0:held], self.full.at[:, held : 2 * held], *stages[self.stage]
            )
        self.stage += 1


class TokenGather:
    def __init__(self, copies, rows, turned_rows, m):
        self.copies, self.rows, self.turned_rows, self.m = copies, rows, turned_rows, m
        self.head_first = m % 2 == 1
        if self.head_first:
            self.copy = copies.remote(rows.at[m, 0, 0], rows.at[m, 1, 0], "head", 1)
        else:
            turned_rows[m, 0] = halves_turned(rows[m, 0, 0])
            self.copy = copies.remote(turned_rows.at[m, 0], rows.at[m, 0, 1], "blk", 1)

    def second(self):
        m, rows, turned_rows = self.m, self.rows, self.turned_rows
        self.copy.wait_recv()
        if self.head_first:
            turned_rows[m, 0] = halves_turned(rows[m, 0, 0])
            turned_rows[m, 1] = halves_turned(rows[m, 1, 0])
            self.copy = self.copies.remote(turned_rows.at[m], rows.at[m, :, 1], "blk", 1)
        else:
            self.copy = self.copies.remote(rows.at[m, 0], rows.at[m, 1], "head", 1)

    def end(self):
        self.copy.wait_recv()


class TokenScatter:
    def __init__(self, copies, partial, leaving, came, passing, last, total, m):
        self.copies, self.partial, self.came, self.passing = copies, partial, came, passing
        self.last, self.total, self.m = last, total, m
        self.head_first = m % 2 == 0
        if self.head_first:
            self.copy = copies.remote(partial.at[m, 1], came.at[m], "head", 1)
        else:
            leaving[m, 0] = halves_turned(partial[m, 0, 1])
            leaving[m, 1] = halves_turned(partial[m, 1, 1])
            self.copy = copies.remote(leaving.at[m], came.at[m], "blk", 1)

    def second(self):
        m, partial = self.m, self.partial
        self.copy.wait_recv()
        kept = partial[m, 0, 1] if self.head_first else partial[m, 1, 0]
        theirs = (kept.astype(F32) + self.came[m, 1].astype(F32)).astype(BF16)
        if self.head_first:
            self.passing[m] = halves_turned(theirs)
            self.copy = self.copies.remote(self.passing.at[m], self.last.at[m], "blk", 1)
        else:
            self.passing[m] = theirs
            self.copy = self.copies.remote(self.passing.at[m], self.last.at[m], "head", 1)
        self.total[m] += partial[m, 0, 0].astype(F32) + self.came[m, 0].astype(F32)

    def end(self):
        self.copy.wait_recv()
        self.total[self.m] += self.last[self.m].astype(F32)


def place_of(block):
    n_blk = lax.axis_size("blk")
    head, blk = block // n_blk, block % n_blk
    near = (blk + lax.axis_index("blk")) % 2
    return blk // 2, ((head + lax.axis_index("head")) % 2) * 2 + near


def load_heads(seq, m, lane, cosine_ref, sine_ref, held):
    tokens = seq.shape[-2]
    lanes = held[0].shape[1]
    blocks = held[0].shape[0] // tokens

    def one(block, carry):
        upper, group = place_of(block)
        rows = pl.ds(pl.multiple_of(block * tokens, tokens), tokens)
        for part in range(3):
            value = seq[m, upper, part, group, :, pl.ds(lane, lanes)]
            if part < 2:
                value = turned(value.astype(F32), cosine_ref[rows, :], sine_ref[rows, :]).astype(BF16)
            held[part][rows, :] = value
        return carry

    lax.fori_loop(0, blocks, one, 0)


def attend(seq, out, m, cosine_ref, sine_ref, held):
    tokens, width = seq.shape[-2:]
    q_s, k_s, v_s = held
    length, lanes = q_s.shape
    rows_at_once = min(256, length) if length <= 2048 else LANES

    def rows_of(first, last, lane):
        results = []
        for start in range(0, lanes, HD):
            head = slice(start, start + HD)
            weights, inverse = softmax_rows(q_s[pl.ds(first, rows_at_once), head], k_s[:last, head], first)
            results.append(matmul(weights.astype(BF16), v_s[:last, head]) * inverse)
        result = jnp.concatenate(results, 1).astype(BF16)
        for offset in range(0, rows_at_once, tokens):
            upper, group = place_of((first + offset) // tokens)
            out[m, upper, group, :, pl.ds(lane, lanes)] = result[offset : offset + tokens]

    def heads(lane):
        load_heads(seq, m, lane, cosine_ref, sine_ref, held)
        over_rows(length, rows_at_once, lambda first, last: rows_of(first, last, lane))

    over_lanes(width, lanes, heads)


def over_rows(length, rows_at_once, body):
    if length // rows_at_once <= 8:
        for first in range(0, length, rows_at_once):
            body(first, first + rows_at_once)
        return

    def one(j, carry):
        body(pl.multiple_of(j * rows_at_once, rows_at_once), length)
        return carry

    lax.fori_loop(0, length // rows_at_once, one, 0)


def over_lanes(width, lanes, body):
    if width == lanes:
        body(0)
        return

    def one(j, carry):
        body(pl.multiple_of(j * lanes, lanes))
        return carry

    lax.fori_loop(0, width // lanes, one, 0)


def store_normed(values, target, at):
    scale = lax.rsqrt(jnp.mean(values * values, -1, keepdims=True) + EPSILON)
    target[at] = (values * scale).astype(BF16)


def front_kernel(sizes, *refs):
    micros, groups, n_att, n_mlp = sizes
    x_ref, att_in, mlp_in, cosine_ref, sine_ref = refs[:5]
    refs = refs[5:]
    w_att, refs = refs[:n_att], refs[n_att:]
    w_mlp, refs = refs[:n_mlp], refs[n_mlp:]
    xg_out, seq_out, attended_out, mixed_out, x2_out = refs[:5]
    (xg, x2, turned_rows, turned_more, w_in, w_out, made, seq, heads_out, attended, partial,
     leaving, came, passing, last, mixed, q_s, k_s, v_s, send, recv, local) = refs[5:]
    held = (q_s, k_s, v_s)
    each = range(micros)
    near = lax.axis_index("blk") % 2
    upper = lax.axis_index("blk") // 2
    width = x_ref.shape[-1]
    tokens = x_ref.shape[-2]
    heads_width = w_in.shape[-1]
    here = heads_width // groups
    copies = Copies(send, recv, local)

    greet()
    att = [WeightGather(copies, att_in.at[i, near], att_in.at[i, 1 - near], w_att[i]) for i in range(n_att)]
    gathers = []
    for m in each:
        store_normed(x_ref[m].astype(F32), xg, (m, 0, 0))
        gathers.append(TokenGather(copies, xg, turned_rows, m))
    for chunk in att:
        chunk.advance()
    per_weight = n_mlp // 3
    order = [(w, j) for j in range(per_weight) for w in range(2)] + [(2, j) for j in range(per_weight)]
    mlp = [
        WeightGather(
            copies, mlp_in.at[w, near * per_weight + j], mlp_in.at[w, (1 - near) * per_weight + j], full
        )
        for (w, j), full in zip(order, w_mlp)
    ]
    for gather in gathers:
        gather.second()
    stages = len(replica_stages())
    steps = [[] for _ in range(stages + n_att)]
    for s in range(stages):
        for i in range(n_att):
            steps[s + i].append(att[i])
    for step in steps:
        for chunk in step:
            if chunk.stage <= stages:
                chunk.advance()

    background = [[] for _ in range(stages + n_mlp + 1)]
    for i, chunk in enumerate(mlp):
        for s in range(stages + 1):
            background[i + s].append(chunk)
    done = [0]

    def pump(count):
        for step in background[done[0] : done[0] + count]:
            for chunk in reversed(step):
                chunk.advance()
        done[0] += count

    for gather in gathers:
        gather.end()
    writes = [copies.inside(xg, xg_out)]
    loads = [copies.inside(w_att[i], w_in.at[i]) for i in range(3)] + [copies.inside(w_att[3], w_out)]
    crossing = [[] for _ in each]
    mine = [[] for _ in each]
    tile = min(256, heads_width)
    for i in range(3):
        loads[i].wait()
        for m in each:
            rows = xg[m].reshape(4 * tokens, width)
            for start in range(0, heads_width, tile):
                columns = w_in[i, :, :, :, start : start + tile].reshape(width, tile)
                product = matmul(rows, columns).astype(BF16)
                for lane in range(0, tile, min(here, tile)):
                    place = (start + lane) // here
                    inner = (start + lane) % here
                    for group in range(4):
                        made[m, place, i, group, :, inner : inner + min(here, tile)] = product[
                            group * tokens : (group + 1) * tokens, lane : lane + min(here, tile)
                        ]
            mine[m].append(copies.inside(made.at[m, upper, i], seq.at[m, upper, i]))
            for r in range(1, groups):
                crossing[m].append(
                    copies.remote(made.at[m, flipped("blk", 2 * r) // 2, i], seq.at[m, upper, i], "blk", 2 * r)
                )
    returning = []
    for m in each:
        pump(1)
        for copy in mine[m]:
            copy.wait()
        for copy in crossing[m]:
            copy.wait_recv()
        attend(seq, heads_out, m, cosine_ref, sine_ref, held)
        back = [copies.inside(heads_out.at[m, upper], attended.at[m, upper])]
        for r in range(1, groups):
            back.append(
                copies.remote(heads_out.at[m, flipped("blk", 2 * r) // 2], attended.at[m, upper], "blk", 2 * r)
            )
        returning.append(back)
    writes.append(copies.inside(seq, seq_out))
    pump(1)
    loads[3].wait()
    scatters = []
    rows_tile = min(256, width)
    for m in each:
        returning[m][0].wait()
        for copy in returning[m][1:]:
            copy.wait_recv()
        rows = jnp.concatenate([attended[m, g].reshape(4 * tokens, here) for g in range(groups)], 1)
        _, replicas, piece, _ = w_out.shape
        for start in range(0, width, rows_tile):
            half, first = start // (replicas * piece), start // piece % replicas
            part = w_out[half, first : first + rows_tile // piece].reshape(rows_tile, heads_width)
            product = matmul_nt(rows, part).astype(BF16)
            for group in range(4):
                partial[m, group // 2, group % 2, :, start : start + rows_tile] = product[
                    group * tokens : (group + 1) * tokens
                ]
        mixed[m] = x_ref[m].astype(F32)
        scatters.append(TokenScatter(copies, partial, leaving, came, passing, last, mixed, m))
    writes.append(copies.inside(attended, attended_out))
    pump(1)
    for scatter in scatters:
        scatter.second()
    pump(1)
    gathers = []
    for m in each:
        scatters[m].end()
        store_normed(mixed[m], x2, (m, 0, 0))
        gathers.append(TokenGather(copies, x2, turned_more, m))
    writes.append(copies.inside(mixed, mixed_out))
    pump(1)
    for gather in gathers:
        gather.second()
    pump(1)
    for gather in gathers:
        gather.end()
    writes.append(copies.inside(x2, x2_out))
    pump(len(background) - done[0])
    for copy in writes:
        copy.wait()
    copies.finish()


def front(x_rows, att_in, mlp_in, tables):
    micros, tokens, width = x_rows.shape
    n_att, _, piece, heads_width = att_in.shape
    n_weights, parts, _, columns = mlp_in.shape
    n_mlp = n_weights * parts // 2
    groups = head_groups()
    here = heads_width // groups
    replicas = width // piece // 2
    length, lanes = tables[0].shape
    any_space = pl.BlockSpec(memory_space=pl.ANY)
    in_vmem = pl.BlockSpec(memory_space=pltpu.VMEM)

    def bf16(*shape):
        return jax.ShapeDtypeStruct(shape, BF16)

    token_rows = (micros, 2, 2, tokens, width)
    outs = [bf16(2, replicas, piece, heads_width)] * n_att + [bf16(2, replicas, piece, columns)] * n_mlp
    outs += [
        bf16(*token_rows),
        bf16(micros, groups, 3, 4, tokens, here),
        bf16(micros, groups, 4, tokens, here),
        jax.ShapeDtypeStruct((micros, tokens, width), F32),
        bf16(*token_rows),
    ]

    def room(*shape):
        return pltpu.VMEM(shape, BF16)

    scratch = [
        room(*token_rows),
        room(*token_rows),
        room(micros, 2, tokens, width),
        room(micros, 2, tokens, width),
        room(3, 2, replicas, piece, heads_width),
        room(2, replicas, piece, heads_width),
        room(micros, groups, 3, 4, tokens, here),
        room(micros, groups, 3, 4, tokens, here),
        room(micros, groups, 4, tokens, here),
        room(micros, groups, 4, tokens, here),
        room(*token_rows),
        room(micros, 2, tokens, width),
        room(micros, 2, tokens, width),
        room(micros, tokens, width),
        room(micros, tokens, width),
        pltpu.VMEM((micros, tokens, width), F32),
        room(length, lanes),
        room(length, lanes),
        room(length, lanes),
        pltpu.SemaphoreType.DMA((192,)),
        pltpu.SemaphoreType.DMA((192,)),
        pltpu.SemaphoreType.DMA((64,)),
    ]
    results = pl.pallas_call(
        functools.partial(front_kernel, (micros, groups, n_att, n_mlp)),
        out_shape=outs,
        in_specs=[in_vmem, any_space, any_space, in_vmem, in_vmem],
        out_specs=[any_space] * len(outs),
        scratch_shapes=scratch,
        compiler_params=pltpu.CompilerParams(
            collective_id=0, has_side_effects=True, vmem_limit_bytes=60 * 1024 * 1024
        ),
    )(x_rows, att_in, mlp_in, *tables)
    w_att, results = results[:n_att], results[n_att:]
    w_mlp, results = results[:n_mlp], results[n_mlp:]
    return [w.reshape(width, -1) for w in w_att], [w.reshape(width, -1) for w in w_mlp], results


def scale_of(values):
    return lax.rsqrt(jnp.mean(values * values, -1, keepdims=True) + EPSILON)


def norm_back(grad, values, scale):
    return scale * grad - values * (scale * scale * scale) * jnp.mean(grad * values, -1, keepdims=True)


def on_device(
    block_input,
    attention_gain,
    query_weight,
    key_weight,
    value_weight,
    output_weight,
    mlp_gain,
    gate_weight,
    up_weight,
    down_weight,
    grad_output,
):
    micros, _, tokens, width = block_input.shape
    heads_width = query_weight.shape[1] // 2
    length = tokens * lax.axis_size("blk") * lax.axis_size("head")
    to_own, to_absolute = feature_order()
    order = block_order()
    tables = rope_tables(length, min(LANES, heads_width // head_groups()))
    each = range(micros)
    head_first = [m % 2 == 1 for m in each]

    gain_one = attention_gain.astype(F32)[:, None]
    gain_two = mlp_gain.astype(F32)[:, None]

    def scaled(weight, gain):
        return (weight.astype(F32) * gain).astype(BF16)

    def joined(parts):
        return jnp.concatenate(parts, 0)

    def columns_of(weight, parts):
        rows, columns = weight.shape
        return weight.reshape(rows, parts, columns // parts).swapaxes(0, 1)

    att_in = jnp.stack(
        [columns_of(scaled(w, gain_one), 2) for w in (query_weight, key_weight, value_weight)]
        + [columns_of(output_weight.T, 2)]
    )
    mlp_in = jnp.stack(
        [columns_of(scaled(w, gain_two), 4) for w in (gate_weight, up_weight)] + [columns_of(down_weight.T, 4)]
    )
    inputs_low = reorder(block_input.reshape(micros * tokens, width), to_own).reshape(micros, tokens, width)
    w_att, w_mlp, held = front(inputs_low, att_in, mlp_in, tables)
    normed_one_all, sequences, attended, mixed, normed_two_all = held
    upper = lax.axis_index("blk") // 2
    sequences = [lax.dynamic_index_in_dim(sequences, upper ^ r, 1, keepdims=False) for r in range(head_groups())]
    sequences = jnp.concatenate(sequences, 2)
    attended = jnp.concatenate([attended[:, g] for g in range(head_groups())], -1)
    attended_all = attended.reshape(micros * 4 * tokens, -1)
    normed_one_all = normed_one_all.reshape(-1, width)
    normed_two_all = normed_two_all.reshape(-1, width)
    gate_parts, up_parts, down_parts = w_mlp[0:4:2], w_mlp[1:4:2], w_mlp[4:]

    grad_low = reorder(grad_output.reshape(micros * tokens, width), to_own).reshape(micros, tokens, width)
    inputs = [inputs_low[m].astype(F32) for m in each]
    scale_one = [scale_of(inputs[m]) for m in each]
    scale_two = [scale_of(mixed[m]) for m in each]
    grad_rows_all = joined([gather_tokens(grad_low[m], head_first[m]) for m in each])

    hidden, grad_gate, grad_up = [], [], []
    grad_normed = produced = 0.0
    for gate_full, up_full, down_full in zip(gate_parts, up_parts, down_parts):
        gate = matmul(normed_two_all, gate_full)
        up = matmul(normed_two_all, up_full)
        sigmoid = jax.nn.sigmoid(gate)
        activated = gate * sigmoid
        hidden.append((activated * up).astype(BF16))
        grad_hidden = matmul(grad_rows_all, down_full)
        grad_gate.append((grad_hidden * up * sigmoid * (1.0 + gate * (1.0 - sigmoid))).astype(BF16))
        grad_up.append((grad_hidden * activated).astype(BF16))
        grad_normed += matmul_nt(grad_gate[-1], gate_full) + matmul_nt(grad_up[-1], up_full)
        produced += matmul_nt(hidden[-1], down_full)

    def split(rows):
        size = rows.shape[0] // micros
        return [rows[m * size : (m + 1) * size] for m in each]

    grad_normed = split(grad_normed)
    grad_mixed = []
    for m in each:
        back = norm_back(scatter_tokens(grad_normed[m], head_first[m]), mixed[m], scale_two[m])
        grad_mixed.append(grad_low[m].astype(F32) + back)
    produced = split(produced)
    outputs = [(mixed[m] + scatter_tokens(produced[m], head_first[m])).astype(BF16) for m in each]

    gate_grad = scatter_weight_grad(normed_two_all, jnp.concatenate(grad_gate, 1))
    up_grad = scatter_weight_grad(normed_two_all, jnp.concatenate(grad_up, 1))
    down_grad = scatter_weight_grad(grad_rows_all, jnp.concatenate(hidden, 1))

    grad_mixed_rows = [gather_tokens(grad_mixed[m].astype(BF16), head_first[m]) for m in each]
    grad_qkv, input_grads = [], []
    for m in each:
        grad_attended = matmul(grad_mixed_rows[m], w_att[3]).astype(BF16)
        grad_sequences = attention_call(order, sequences[m], tables, to_sequences([grad_attended])[0])
        returned = from_sequences(grad_sequences)
        grad_qkv.append(jnp.concatenate([returned[0], returned[1], returned[2]], 1))
        grad_normed = scatter_tokens(functools.reduce(jnp.add, [matmul_nt(returned[i], w_att[i]) for i in range(3)]), head_first[m])
        input_grads.append((grad_mixed[m] + norm_back(grad_normed, inputs[m], scale_one[m])).astype(BF16))
    output_grad = scatter_weight_grad(joined(grad_mixed_rows), attended_all)
    qkv_grad = scatter_weight_grad(normed_one_all, joined(grad_qkv))

    qkv_grads = [
        side_by_side(*(side[:, i * heads_width : (i + 1) * heads_width] for side in qkv_grad)) for i in range(3)
    ]
    mlp_grads = [side_by_side(*gate_grad), side_by_side(*up_grad)]

    def gain_grad(weights, grads):
        terms = [jnp.sum(w.astype(F32) * g, 1) for w, g in zip(weights, grads)]
        here = functools.reduce(jnp.add, terms)
        return here + swap(here, "head", 1)

    attention_gain_grad = gain_grad((query_weight, key_weight, value_weight), qkv_grads)
    mlp_gain_grad = gain_grad((gate_weight, up_weight), mlp_grads)

    def absolute(parts):
        rows = reorder(joined(parts), to_absolute)
        return rows.reshape(micros, 1, tokens, width)

    return (
        absolute(outputs),
        absolute(input_grads),
        attention_gain_grad,
        qkv_grads[0] * gain_one,
        qkv_grads[1] * gain_one,
        qkv_grads[2] * gain_one,
        side_by_side(*output_grad).T,
        mlp_gain_grad,
        mlp_grads[0] * gain_two,
        mlp_grads[1] * gain_two,
        side_by_side(*down_grad).T,
    )


def solution(mesh):
    rows, row_split = P(None, "dp", ("head", "blk"), None), P(("dp", "blk"), "head")
    column_split, gain = P("head", ("dp", "blk")), P(("dp", "blk"))
    return jax.shard_map(
        on_device,
        mesh=mesh,
        in_specs=(
            rows, gain, row_split, row_split, row_split, column_split, gain, row_split, row_split, column_split, rows,
        ),
        out_specs=(
            rows, rows, gain, row_split, row_split, row_split, column_split, gain, row_split, row_split, column_split,
        ),
        check_vma=False,
    )
```

```python
import functools

import jax
import jax.numpy as jnp
import numpy as np
from jax import lax
from jax.experimental import pallas as pl
from jax.experimental.pallas import tpu as pltpu
from jax.sharding import PartitionSpec as P

HD = 64
EPSILON = 1e-05
ROPE_BASE = 130000.0
MASKED_SCORE = -1e30
F32 = jnp.float32
BF16 = jnp.bfloat16
LANES = 128
MESH = pl.DeviceIdType.MESH


def swap(value, axis, bit):
    count = lax.axis_size(axis)
    return lax.ppermute(value, axis, [(i, i ^ bit) for i in range(count)])


def bits_of(count):
    return [1 << i for i in range(count.bit_length() - 1)]


def replica_stages():
    upper = [("blk", bit) for bit in bits_of(lax.axis_size("blk"))[1:]]
    return upper + [("dp", bit) for bit in reversed(bits_of(lax.axis_size("dp")))]


def matmul(left_side, right_side):
    return jnp.dot(left_side, right_side, preferred_element_type=F32)


def matmul_nt(left_side, right_side):
    return lax.dot_general(left_side, right_side, (((1,), (1,)), ((), ())), preferred_element_type=F32)


def matmul_tn(left_side, right_side):
    return lax.dot_general(left_side, right_side, (((0,), (0,)), ((), ())), preferred_element_type=F32)


def feature_order():
    n_blk, n_dp = lax.axis_size("blk"), lax.axis_size("dp")
    order = np.zeros((1,), np.int32)
    for axis, bit in replica_stages():
        order = np.concatenate([order, order ^ (bit if axis == "blk" else bit * n_blk)])
    order = np.concatenate([order, order ^ 1])
    assert order.size == n_blk * n_dp
    mine = lax.axis_index("dp") * n_blk + lax.axis_index("blk")
    back = np.argsort(order).astype(np.int32)
    absolute = jnp.arange(order.size, dtype=jnp.int32) ^ mine
    return jnp.asarray(order) ^ mine, jnp.asarray(back)[absolute]


def reorder_kernel(count, order_ref, *refs):
    for source, target in zip(refs[:count], refs[count:]):
        blocks = order_ref.shape[0]
        piece = source.shape[1] // blocks
        for j in range(blocks):
            start = pl.multiple_of(order_ref[j] * piece, piece)
            target[:, j * piece : (j + 1) * piece] = source[:, pl.ds(start, piece)]


def reorder(order, *arrays):
    count, width = arrays[0].shape
    blocks = order.shape[0]
    piece = width // blocks
    if piece % LANES:
        return [jnp.take(rows.reshape(count, blocks, piece), order, axis=1).reshape(count, width) for rows in arrays]
    in_vmem = pl.BlockSpec(memory_space=pltpu.VMEM)
    return pl.pallas_call(
        functools.partial(reorder_kernel, len(arrays)),
        in_specs=[pl.BlockSpec(memory_space=pltpu.SMEM)] + [in_vmem] * len(arrays),
        out_specs=[in_vmem] * len(arrays),
        out_shape=[jax.ShapeDtypeStruct(rows.shape, rows.dtype) for rows in arrays],
    )(order, *arrays)


def turn_features(rows):
    half = rows.shape[1] // 2
    return jnp.concatenate([rows[:, half:], rows[:, :half]], 1)


def gather_tokens(rows, head_first):
    count = rows.shape[0]
    if head_first:
        other = swap(rows, "head", 1)
        far = swap(turn_features(jnp.concatenate([rows, other], 0)), "blk", 1)
        return jnp.concatenate([rows, far[:count], other, far[count:]], 0)
    both = jnp.concatenate([rows, swap(turn_features(rows), "blk", 1)], 0)
    return jnp.concatenate([both, swap(both, "head", 1)], 0)


def scatter_tokens(partial, head_first):
    partial = partial.astype(BF16)
    count = partial.shape[0] // 4
    if head_first:
        came = swap(partial[2 * count :], "head", 1)
        mine = partial[:count].astype(F32) + came[:count].astype(F32)
        theirs = (partial[count : 2 * count].astype(F32) + came[count:].astype(F32)).astype(BF16)
        return mine + swap(turn_features(theirs), "blk", 1).astype(F32)
    leaving = jnp.concatenate([partial[count : 2 * count], partial[3 * count :]], 0)
    came = swap(turn_features(leaving), "blk", 1)
    mine = partial[:count].astype(F32) + came[:count].astype(F32)
    theirs = (partial[2 * count : 3 * count].astype(F32) + came[count:].astype(F32)).astype(BF16)
    return mine + swap(theirs, "head", 1).astype(F32)


def own_and_other(columns):
    width = columns.shape[1] // 2
    place = lax.axis_index("blk") % 2
    return (
        lax.dynamic_slice_in_dim(columns, place * width, width, 1),
        lax.dynamic_slice_in_dim(columns, (1 - place) * width, width, 1),
    )


def gather_weight(own, other):
    streams = [own, swap(other, "blk", 1)]
    stages = replica_stages()
    for axis, bit in stages[:-1]:
        streams = [jnp.concatenate([held, swap(held, axis, bit)], 0) for held in streams]
    pieces = []
    for held in streams:
        pieces += [held, swap(held, *stages[-1])]
    return jnp.concatenate(pieces, 0)


def scatter_weight_grad(acts, grads):
    quarter = acts.shape[1] // 4
    stages = replica_stages()[::-1]

    def piece(place):
        return matmul_tn(acts[:, place * quarter : (place + 1) * quarter], grads).astype(BF16)

    streams = []
    for first in (2, 0):
        came = swap(piece(first + 1), *stages[0])
        held = piece(first).astype(F32) + came.astype(F32)
        for axis, bit in stages[1:]:
            half = held.shape[0] // 2
            held = held.astype(BF16)
            came = swap(held[half:], axis, bit)
            held = held[:half].astype(F32) + came.astype(F32)
        streams.append(held)
    return streams[1], swap(streams[0].astype(BF16), "blk", 1)


def side_by_side(own, other):
    other = other.astype(F32)
    low = lax.axis_index("blk") % 2 == 0
    return jnp.concatenate([jnp.where(low, own, other), jnp.where(low, other, own)], 1)


def head_groups():
    return lax.axis_size("blk") // 2


def to_sequences(parts):
    groups = head_groups()
    upper = lax.axis_index("blk") // 2
    width = parts[0].shape[1] // groups
    arrived = []
    for r in range(groups):
        chosen = jnp.stack([lax.dynamic_slice_in_dim(part, (upper ^ r) * width, width, 1) for part in parts])
        if r:
            chosen = lax.ppermute(chosen, "blk", [(i, i ^ (2 * r)) for i in range(2 * groups)])
        arrived.append(chosen.reshape(len(parts), 4, -1, width))
    return jnp.concatenate(arrived, 1)


def from_sequences(blocks):
    groups = head_groups()
    upper = lax.axis_index("blk") // 2
    count, _, tokens, width = blocks.shape
    arrived = []
    for r in range(groups):
        chosen = blocks[:, 4 * r : 4 * r + 4]
        if r:
            chosen = lax.ppermute(chosen, "blk", [(i, i ^ (2 * r)) for i in range(2 * groups)])
        arrived.append(chosen.reshape(count, 4 * tokens, width))
    stacked = jnp.stack(arrived)
    ordered = [lax.dynamic_index_in_dim(stacked, h ^ upper, 0, keepdims=False) for h in range(groups)]
    return jnp.concatenate(ordered, 2)


def block_order():
    n_blk, n_head = lax.axis_size("blk"), lax.axis_size("head")
    block = np.arange(n_blk * n_head, dtype=np.int32)
    r_head = (block // n_blk) ^ lax.axis_index("head")
    r_blk = (block % n_blk) ^ lax.axis_index("blk")
    return ((r_blk // 2) * 2 + r_head) * 2 + r_blk % 2


def rope_tables(length, lanes):
    half = HD // 2
    frequency = ROPE_BASE ** (-np.arange(half, dtype=np.float32) * np.float32(2.0 / HD))
    angles = np.arange(length, dtype=np.float32)[:, None] * frequency.astype(np.float32)[None, :]
    cosine, sine = np.cos(angles), np.sin(angles)
    return (
        jnp.asarray(np.tile(cosine, (1, lanes // half)), F32),
        jnp.asarray(np.tile(np.concatenate([-sine, sine], 1), (1, lanes // HD)), F32),
    )


def turned(rows, cosine, sine):
    half = HD // 2
    parts = []
    for start in range(0, rows.shape[1], HD):
        parts += [rows[:, start + half : start + HD], rows[:, start : start + half]]
    return rows * cosine + jnp.concatenate(parts, 1) * sine


def load_sequence(order_ref, qkv_ref, cosine_ref, sine_ref, held, tokens, blocks):
    def one(block, carry):
        place = order_ref[block]
        rows = pl.ds(pl.multiple_of(block * tokens, tokens), tokens)
        for part in range(3):
            value = qkv_ref[part, place]
            if part < 2:
                value = turned(value.astype(F32), cosine_ref[rows, :], sine_ref[rows, :]).astype(BF16)
            held[part][rows, :] = value
        return carry

    lax.fori_loop(0, blocks, one, 0)


def softmax_rows(query, keys, first_row):
    scores = matmul_nt(query, keys) * HD ** (-0.5)
    row = first_row + lax.broadcasted_iota(jnp.int32, scores.shape, 0)
    scores = jnp.where(lax.broadcasted_iota(jnp.int32, scores.shape, 1) <= row, scores, MASKED_SCORE)
    weights = jnp.exp(scores - jnp.max(scores, 1, keepdims=True))
    return weights, 1.0 / jnp.sum(weights, 1, keepdims=True)


def attend_kernel(tokens, blocks, rows_at_once, order_ref, qkv_ref, cosine_ref, sine_ref, out_ref, q_s, k_s, v_s):
    lanes = qkv_ref.shape[-1]
    load_sequence(order_ref, qkv_ref, cosine_ref, sine_ref, (q_s, k_s, v_s), tokens, blocks)
    for first in range(0, tokens * blocks, rows_at_once):
        last = first + rows_at_once
        results = []
        for lane in range(0, lanes, HD):
            head = slice(lane, lane + HD)
            weights, inverse = softmax_rows(q_s[first:last, head], k_s[:last, head], first)
            results.append(matmul(weights.astype(BF16), v_s[:last, head]) * inverse)
        result = jnp.concatenate(results, 1).astype(BF16)
        for offset in range(0, rows_at_once, tokens):
            out_ref[order_ref[(first + offset) // tokens]] = result[offset : offset + tokens]


def attend_back_kernel(
    tokens, blocks, rows_at_once, order_ref, qkv_ref, grad_ref, cosine_ref, sine_ref, out_ref,
    q_s, k_s, v_s, dk_s, dv_s,
):
    lanes = qkv_ref.shape[-1]
    load_sequence(order_ref, qkv_ref, cosine_ref, sine_ref, (q_s, k_s, v_s), tokens, blocks)
    dk_s[...] = jnp.zeros_like(dk_s)
    dv_s[...] = jnp.zeros_like(dv_s)
    for first in range(0, tokens * blocks, rows_at_once):
        last = first + rows_at_once
        arrived = [grad_ref[order_ref[row // tokens]] for row in range(first, last, tokens)]
        grad_rows = jnp.concatenate(arrived, 0)
        query_parts, key_parts, value_parts = [], [], []
        for lane in range(0, lanes, HD):
            head = slice(lane, lane + HD)
            query, keys, grad = q_s[first:last, head], k_s[:last, head], grad_rows[:, head]
            weights, inverse = softmax_rows(query, keys, first)
            probabilities = weights * inverse
            grad_prob = matmul_nt(grad, v_s[:last, head])
            row_delta = jnp.sum(probabilities * grad_prob, 1, keepdims=True)
            grad_scores = (probabilities * (grad_prob - row_delta) * HD ** (-0.5)).astype(BF16)
            query_parts.append(matmul(grad_scores, keys))
            key_parts.append(matmul_tn(grad_scores, query))
            value_parts.append(matmul_tn(probabilities.astype(BF16), grad))
        grad_query = jnp.concatenate(query_parts, 1)
        grad_query = turned(grad_query, cosine_ref[first:last, :], -sine_ref[first:last, :]).astype(BF16)
        for offset in range(0, rows_at_once, tokens):
            out_ref[0, order_ref[(first + offset) // tokens]] = grad_query[offset : offset + tokens]
        dk_s[:last, :] += jnp.concatenate(key_parts, 1)
        dv_s[:last, :] += jnp.concatenate(value_parts, 1)

    def one(block, carry):
        place = order_ref[block]
        rows = pl.ds(pl.multiple_of(block * tokens, tokens), tokens)
        out_ref[1, place] = turned(dk_s[rows, :], cosine_ref[rows, :], -sine_ref[rows, :]).astype(BF16)
        out_ref[2, place] = dv_s[rows, :].astype(BF16)
        return carry

    lax.fori_loop(0, blocks, one, 0)


def attention_call(order, qkv, tables, grad=None):
    _, blocks, tokens, width = qkv.shape
    length = blocks * tokens
    lanes = min(LANES, width)
    rows_at_once = min(256, length) if length <= 2048 else LANES
    back = grad is not None

    def fixed(j, order_ref):
        return (0, 0)

    part = pl.BlockSpec((blocks, tokens, lanes), lambda j, order_ref: (0, 0, j))
    three = pl.BlockSpec((3, blocks, tokens, lanes), lambda j, order_ref: (0, 0, 0, j))
    table = pl.BlockSpec((length, lanes), fixed)
    kernel = attend_back_kernel if back else attend_kernel
    scratch = [pltpu.VMEM((length, lanes), BF16)] * 3
    if back:
        scratch += [pltpu.VMEM((length, lanes), F32)] * 2
    products = 5 if back else 2
    return pl.pallas_call(
        functools.partial(kernel, tokens, blocks, rows_at_once),
        grid_spec=pltpu.PrefetchScalarGridSpec(
            num_scalar_prefetch=1,
            grid=(width // lanes,),
            in_specs=[three] + ([part] if back else []) + [table, table],
            out_specs=three if back else part,
            scratch_shapes=scratch,
        ),
        out_shape=jax.ShapeDtypeStruct(qkv.shape if back else qkv.shape[1:], BF16),
        compiler_params=pltpu.CompilerParams(vmem_limit_bytes=48 * 1024 * 1024),
        cost_estimate=pl.CostEstimate(
            flops=products * 4 * length * length * width,
            bytes_accessed=(7 if back else 4) * length * width * 2,
            transcendentals=length * length * (width // HD),
        ),
    )(order, qkv, *([grad] if back else []), *tables)


def greet():
    masks = [("head", 1)] + [("dp", bit) for bit in bits_of(lax.axis_size("dp"))]
    masks += [("blk", 1)] + [("blk", 2 * r) for r in range(1, head_groups())]
    barrier = pltpu.get_barrier_semaphore()
    for axis, mask in masks:
        pl.semaphore_signal(barrier, inc=1, device_id={axis: flipped(axis, mask)}, device_id_type=MESH)
    pl.semaphore_wait(barrier, len(masks))


def flipped(axis, mask):
    place, other = lax.axis_index(axis), 0
    for bit in bits_of(lax.axis_size(axis)):
        digit = (place // bit) % 2
        other = other + bit * ((1 - digit) if mask & bit else digit)
    return other


class Copies:
    def __init__(self, send, recv, local):
        self.send, self.recv, self.local = send, recv, local
        self.remote_count = self.local_count = 0
        self.sent = []

    def remote(self, source, target, axis, mask):
        k = self.remote_count
        self.remote_count += 1
        copy = pltpu.make_async_remote_copy(
            src_ref=source, dst_ref=target, send_sem=self.send.at[k], recv_sem=self.recv.at[k],
            device_id={axis: flipped(axis, mask)}, device_id_type=MESH,
        )
        copy.start()
        self.sent.append(copy)
        return copy

    def inside(self, source, target):
        copy = pltpu.make_async_copy(source, target, self.local.at[self.local_count])
        self.local_count += 1
        copy.start()
        return copy

    def is_unsent(self, copy):
        return any(copy is other for other in self.sent)

    def wait_sent(self, copy):
        copy.wait_send()
        self.sent = [other for other in self.sent if other is not copy]

    def finish(self):
        for copy in self.sent:
            copy.wait_send()


def halves_turned(rows):
    half = rows.shape[-1] // 2
    return jnp.concatenate([rows[:, half:], rows[:, :half]], 1)


class WeightGather:
    def __init__(self, copies, own, other, full):
        self.copies, self.full, self.stage = copies, full, 0
        self.mine = copies.inside(own, full.at[0, 0])
        self.copy = copies.remote(other, full.at[1, 0], "blk", 1)

    def advance(self):
        if self.mine is not None:
            self.mine.wait()
            self.mine = None
        self.copy.wait_recv()
        stages = replica_stages()
        if self.stage < len(stages):
            held = 1 << self.stage
            self.copy = self.copies.remote(
                self.full.at[:, 0:held], self.full.at[:, held : 2 * held], *stages[self.stage]
            )
        self.stage += 1


class TokenGather:
    def __init__(self, copies, rows, turned_rows, m):
        self.copies, self.rows, self.turned_rows, self.m = copies, rows, turned_rows, m
        self.head_first = m % 2 == 1
        if self.head_first:
            self.copy = copies.remote(rows.at[m, 0, 0], rows.at[m, 1, 0], "head", 1)
        else:
            turned_rows[m, 0] = halves_turned(rows[m, 0, 0])
            self.copy = copies.remote(turned_rows.at[m, 0], rows.at[m, 0, 1], "blk", 1)

    def second(self):
        m, rows, turned_rows = self.m, self.rows, self.turned_rows
        self.copy.wait_recv()
        if self.head_first:
            turned_rows[m, 0] = halves_turned(rows[m, 0, 0])
            turned_rows[m, 1] = halves_turned(rows[m, 1, 0])
            self.copy = self.copies.remote(turned_rows.at[m], rows.at[m, :, 1], "blk", 1)
        else:
            self.copy = self.copies.remote(rows.at[m, 0], rows.at[m, 1], "head", 1)

    def end(self):
        self.copy.wait_recv()


class TokenScatter:
    def __init__(self, copies, partial, leaving, came, passing, last, total, m):
        self.copies, self.partial, self.came, self.passing = copies, partial, came, passing
        self.last, self.total, self.m = last, total, m
        self.head_first = m % 2 == 0
        if self.head_first:
            self.copy = copies.remote(partial.at[m, 1], came.at[m], "head", 1)
        else:
            leaving[m, 0] = halves_turned(partial[m, 0, 1])
            leaving[m, 1] = halves_turned(partial[m, 1, 1])
            self.copy = copies.remote(leaving.at[m], came.at[m], "blk", 1)
        self.first = self.copy

    def second(self):
        m, partial = self.m, self.partial
        self.copy.wait_recv()
        kept = partial[m, 0, 1] if self.head_first else partial[m, 1, 0]
        theirs = (kept.astype(F32) + self.came[m, 1].astype(F32)).astype(BF16)
        if self.head_first:
            self.passing[m] = halves_turned(theirs)
            self.copy = self.copies.remote(self.passing.at[m], self.last.at[m], "blk", 1)
        else:
            self.passing[m] = theirs
            self.copy = self.copies.remote(self.passing.at[m], self.last.at[m], "head", 1)
        self.total[m] += partial[m, 0, 0].astype(F32) + self.came[m, 0].astype(F32)

    def end(self):
        self.copy.wait_recv()
        self.total[self.m] += self.last[self.m].astype(F32)

    def release(self):
        self.copies.wait_sent(self.first)
        self.copies.wait_sent(self.copy)


def place_of(block):
    n_blk = lax.axis_size("blk")
    head, blk = block // n_blk, block % n_blk
    near = (blk + lax.axis_index("blk")) % 2
    return blk // 2, ((head + lax.axis_index("head")) % 2) * 2 + near


def load_heads(seq, m, lane, cosine_ref, sine_ref, held):
    tokens = seq.shape[-2]
    lanes = held[0].shape[1]
    blocks = held[0].shape[0] // tokens

    def one(block, carry):
        upper, group = place_of(block)
        rows = pl.ds(pl.multiple_of(block * tokens, tokens), tokens)
        for part in range(3):
            value = seq[m, upper, part, group, :, pl.ds(lane, lanes)]
            if part < 2:
                value = turned(value.astype(F32), cosine_ref[rows, :], sine_ref[rows, :]).astype(BF16)
            held[part][rows, :] = value
        return carry

    lax.fori_loop(0, blocks, one, 0)


def attend(seq, out, m, cosine_ref, sine_ref, held):
    tokens, width = seq.shape[-2:]
    q_s, k_s, v_s = held
    length, lanes = q_s.shape
    rows_at_once = min(256, length) if length <= 2048 else LANES

    def rows_of(first, last, lane):
        results = []
        for start in range(0, lanes, HD):
            head = slice(start, start + HD)
            weights, inverse = softmax_rows(q_s[pl.ds(first, rows_at_once), head], k_s[:last, head], first)
            results.append(matmul(weights.astype(BF16), v_s[:last, head]) * inverse)
        result = jnp.concatenate(results, 1).astype(BF16)
        for offset in range(0, rows_at_once, tokens):
            upper, group = place_of((first + offset) // tokens)
            out[m, upper, group, :, pl.ds(lane, lanes)] = result[offset : offset + tokens]

    def heads(lane):
        load_heads(seq, m, lane, cosine_ref, sine_ref, held)
        over_rows(length, rows_at_once, lambda first, last: rows_of(first, last, lane))

    over_lanes(width, lanes, heads)


def over_rows(length, rows_at_once, body):
    if length // rows_at_once <= 8:
        for first in range(0, length, rows_at_once):
            body(first, first + rows_at_once)
        return

    def one(j, carry):
        body(pl.multiple_of(j * rows_at_once, rows_at_once), length)
        return carry

    lax.fori_loop(0, length // rows_at_once, one, 0)


def over_lanes(width, lanes, body):
    if width == lanes:
        body(0)
        return

    def one(j, carry):
        body(pl.multiple_of(j * lanes, lanes))
        return carry

    lax.fori_loop(0, width // lanes, one, 0)


def store_normed(values, target, at):
    scale = lax.rsqrt(jnp.mean(values * values, -1, keepdims=True) + EPSILON)
    target[at] = (values * scale).astype(BF16)


def front_kernel(sizes, *refs):
    micros, groups, n_att, n_mlp = sizes
    x_ref, g_in, g_turned, att_in, mlp_in, cosine_ref, sine_ref = refs[:7]
    refs = refs[7:]
    w_att, refs = refs[:n_att], refs[n_att:]
    w_mlp, refs = refs[:n_mlp], refs[n_mlp:]
    xg_out, seq_out, attended_out, mixed_out, x2_out, gg_out = refs[:6]
    (xg, x2, turned_rows, turned_more, w_in, w_out, made, seq, heads_out, attended, partial,
     leaving, came, passing, last, mixed, q_s, k_s, v_s, send, recv, local) = refs[6:]
    held = (q_s, k_s, v_s)
    each = range(micros)
    near = lax.axis_index("blk") % 2
    upper = lax.axis_index("blk") // 2
    width = x_ref.shape[-1]
    tokens = x_ref.shape[-2]
    heads_width = w_in.shape[-1]
    here = heads_width // groups
    copies = Copies(send, recv, local)

    greet()
    att = [WeightGather(copies, att_in.at[i, near], att_in.at[i, 1 - near], w_att[i]) for i in range(n_att)]
    gathers = []
    for m in each:
        store_normed(x_ref[m].astype(F32), xg, (m, 0, 0))
        gathers.append(TokenGather(copies, xg, turned_rows, m))
    for chunk in att:
        chunk.advance()
    per_weight = n_mlp // 3
    order = [(w, j) for j in range(per_weight) for w in range(2)] + [(2, j) for j in range(per_weight)]
    mlp = [
        WeightGather(
            copies, mlp_in.at[w, near * per_weight + j], mlp_in.at[w, (1 - near) * per_weight + j], full
        )
        for (w, j), full in zip(order, w_mlp)
    ]
    for gather in gathers:
        gather.second()
    grad_own = [copies.inside(g_in.at[m], gg_out.at[m, 0, 0]) for m in each]
    grad_rows = [copies.remote(g_turned.at[m], gg_out.at[m, 0, 1], "blk", 1) for m in each]
    stages = len(replica_stages())
    steps = [[] for _ in range(stages + n_att)]
    for s in range(stages):
        for i in range(n_att):
            steps[s + i].append(att[i])
    for step in steps:
        for chunk in step:
            if chunk.stage <= stages:
                chunk.advance()

    background = [[] for _ in range(stages + n_mlp + 1)]
    for i, chunk in enumerate(mlp):
        for s in range(stages + 1):
            background[i + s].append(chunk)
    done = [0]

    def pump(count):
        for step in background[done[0] : done[0] + count]:
            for chunk in reversed(step):
                chunk.advance()
        done[0] += count

    for gather in gathers:
        gather.end()
    writes = [copies.inside(xg, xg_out)]
    loads = [copies.inside(w_att[i], w_in.at[i]) for i in range(3)] + [copies.inside(w_att[3], w_out)]
    crossing = [[] for _ in each]
    mine = [[] for _ in each]
    tile = min(256, heads_width)
    for i in range(3):
        loads[i].wait()
        for m in each:
            rows = xg[m].reshape(4 * tokens, width)
            for start in range(0, heads_width, tile):
                columns = w_in[i, :, :, :, start : start + tile].reshape(width, tile)
                product = matmul(rows, columns).astype(BF16)
                for lane in range(0, tile, min(here, tile)):
                    place = (start + lane) // here
                    inner = (start + lane) % here
                    for group in range(4):
                        made[m, place, i, group, :, inner : inner + min(here, tile)] = product[
                            group * tokens : (group + 1) * tokens, lane : lane + min(here, tile)
                        ]
            mine[m].append(copies.inside(made.at[m, upper, i], seq.at[m, upper, i]))
            for r in range(1, groups):
                crossing[m].append(
                    copies.remote(made.at[m, flipped("blk", 2 * r) // 2, i], seq.at[m, upper, i], "blk", 2 * r)
                )
    for m in each:
        grad_own[m].wait()
        grad_rows[m].wait_recv()
        grad_rows[m] = copies.remote(gg_out.at[m, 0], gg_out.at[m, 1], "head", 1)
    returning = []
    for m in each:
        pump(1)
        for copy in mine[m]:
            copy.wait()
        for copy in crossing[m]:
            copy.wait_recv()
        attend(seq, heads_out, m, cosine_ref, sine_ref, held)
        back = [copies.inside(heads_out.at[m, upper], attended.at[m, upper])]
        for r in range(1, groups):
            back.append(
                copies.remote(heads_out.at[m, flipped("blk", 2 * r) // 2], attended.at[m, upper], "blk", 2 * r)
            )
        returning.append(back)
    writes.append(copies.inside(seq, seq_out))
    pump(1)
    loads[3].wait()
    scatters = []
    rows_tile = min(256, width)
    for m in each:
        returning[m][0].wait()
        for copy in returning[m][1:]:
            copy.wait_recv()
        rows = jnp.concatenate([attended[m, g].reshape(4 * tokens, here) for g in range(groups)], 1)
        _, replicas, piece, _ = w_out.shape
        for start in range(0, width, rows_tile):
            half, first = start // (replicas * piece), start // piece % replicas
            part = w_out[half, first : first + rows_tile // piece].reshape(rows_tile, heads_width)
            product = matmul_nt(rows, part).astype(BF16)
            for group in range(4):
                partial[m, group // 2, group % 2, :, start : start + rows_tile] = product[
                    group * tokens : (group + 1) * tokens
                ]
        mixed[m] = x_ref[m].astype(F32)
        scatters.append(TokenScatter(copies, partial, leaving, came, passing, last, mixed, m))
    writes.append(copies.inside(attended, attended_out))
    pump(1)
    for scatter in scatters:
        scatter.second()
    pump(1)
    gathers = []
    for m in each:
        scatters[m].end()
        store_normed(mixed[m], x2, (m, 0, 0))
        gathers.append(TokenGather(copies, x2, turned_more, m))
    writes.append(copies.inside(mixed, mixed_out))
    pump(1)
    for gather in gathers:
        gather.second()
    pump(1)
    for gather in gathers:
        gather.end()
    writes.append(copies.inside(x2, x2_out))
    pump(len(background) - done[0])
    for copy in grad_rows:
        copy.wait_recv()
    for copy in writes:
        copy.wait()
    copies.finish()


def front(x_rows, grad_rows, grad_turned, att_in, mlp_in, tables):
    micros, tokens, width = x_rows.shape
    n_att, _, piece, heads_width = att_in.shape
    n_weights, parts, _, columns = mlp_in.shape
    n_mlp = n_weights * parts // 2
    groups = head_groups()
    here = heads_width // groups
    replicas = width // piece // 2
    length, lanes = tables[0].shape
    any_space = pl.BlockSpec(memory_space=pl.ANY)
    in_vmem = pl.BlockSpec(memory_space=pltpu.VMEM)

    def bf16(*shape):
        return jax.ShapeDtypeStruct(shape, BF16)

    token_rows = (micros, 2, 2, tokens, width)
    outs = [bf16(2, replicas, piece, heads_width)] * n_att + [bf16(2, replicas, piece, columns)] * n_mlp
    outs += [
        bf16(*token_rows),
        bf16(micros, groups, 3, 4, tokens, here),
        bf16(micros, groups, 4, tokens, here),
        jax.ShapeDtypeStruct((micros, tokens, width), F32),
        bf16(*token_rows),
        bf16(*token_rows),
    ]

    def room(*shape):
        return pltpu.VMEM(shape, BF16)

    scratch = [
        room(*token_rows),
        room(*token_rows),
        room(micros, 2, tokens, width),
        room(micros, 2, tokens, width),
        room(3, 2, replicas, piece, heads_width),
        room(2, replicas, piece, heads_width),
        room(micros, groups, 3, 4, tokens, here),
        room(micros, groups, 3, 4, tokens, here),
        room(micros, groups, 4, tokens, here),
        room(micros, groups, 4, tokens, here),
        room(*token_rows),
        room(micros, 2, tokens, width),
        room(micros, 2, tokens, width),
        room(micros, tokens, width),
        room(micros, tokens, width),
        pltpu.VMEM((micros, tokens, width), F32),
        room(length, lanes),
        room(length, lanes),
        room(length, lanes),
        pltpu.SemaphoreType.DMA((192,)),
        pltpu.SemaphoreType.DMA((192,)),
        pltpu.SemaphoreType.DMA((64,)),
    ]
    results = pl.pallas_call(
        functools.partial(front_kernel, (micros, groups, n_att, n_mlp)),
        out_shape=outs,
        in_specs=[in_vmem] + [any_space] * 4 + [in_vmem, in_vmem],
        out_specs=[any_space] * len(outs),
        scratch_shapes=scratch,
        compiler_params=pltpu.CompilerParams(
            collective_id=0, has_side_effects=True, vmem_limit_bytes=60 * 1024 * 1024
        ),
    )(x_rows, grad_rows, grad_turned, att_in, mlp_in, *tables)
    w_att, results = results[:n_att], results[n_att:]
    w_mlp, results = results[:n_mlp], results[n_mlp:]
    return w_att, [w.reshape(width, -1) for w in w_mlp], results


class GradScatter:
    def __init__(self, copies, kept, first_copy, landed, room, final, own, other):
        self.copies, self.kept, self.copy, self.landed = copies, kept, first_copy, landed
        self.room, self.final, self.own, self.other = room, final, own, other
        self.stage = 0

    def advance(self):
        copies, kept, stage = self.copies, self.kept, self.stage
        stages = replica_stages()[::-1]
        self.copy.wait_recv()
        self.stage += 1
        if stage == len(stages):
            return
        count = kept.shape[1] >> stage
        columns = kept.shape[-1]
        mine, came = (part.at[:, 0:count, :, 0:columns] for part in self.room)
        loads = [copies.inside(kept.at[:, 0:count], mine), copies.inside(self.landed[stage], came)]
        for load in loads:
            load.wait()
        if stage == len(stages) - 1:
            self.final[:, 0:columns] = mine[0, 0].astype(F32) + came[0, 0].astype(F32)
            mine[1, 0] = (mine[1, 0].astype(F32) + came[1, 0].astype(F32)).astype(BF16)
            stores = [
                copies.inside(self.final.at[:, 0:columns], self.own),
                copies.inside(mine.at[1, 0], kept.at[1, 0]),
            ]
            for store in stores:
                store.wait()
            self.copy = copies.remote(kept.at[1, 0], self.other, "blk", 1)
            return

        def one(i, carry):
            half, row = i // count, i % count
            mine[half, row] = (mine[half, row].astype(F32) + came[half, row].astype(F32)).astype(BF16)
            return carry

        lax.fori_loop(0, 2 * count, one, 0)
        copies.inside(mine, kept.at[:, 0:count]).wait()
        self.copy = copies.remote(
            kept.at[:, count // 2 : count], self.landed[stage + 1], *stages[stage + 1]
        )


def attend_back(seq, seq_at, grad, out, m, cosine_ref, sine_ref, held, sums):
    tokens, width = seq.shape[-2:]
    q_s, k_s, v_s = held
    dk_s, dv_s = sums
    length, lanes = q_s.shape
    rows_at_once = min(256, length)

    def rows_of(first, last, lane):
        places = [place_of((first + offset) // tokens) for offset in range(0, rows_at_once, tokens)]
        grad_rows = jnp.concatenate([grad[m, u, g, :, pl.ds(lane, lanes)] for u, g in places], 0)
        rows = pl.ds(first, rows_at_once)
        query_parts, key_parts, value_parts = [], [], []
        for start in range(0, lanes, HD):
            head = slice(start, start + HD)
            query, keys, grad_part = q_s[rows, head], k_s[:last, head], grad_rows[:, head]
            weights, inverse = softmax_rows(query, keys, first)
            probabilities = weights * inverse
            grad_prob = matmul_nt(grad_part, v_s[:last, head])
            row_delta = jnp.sum(probabilities * grad_prob, 1, keepdims=True)
            grad_scores = (probabilities * (grad_prob - row_delta) * HD ** (-0.5)).astype(BF16)
            query_parts.append(matmul(grad_scores, keys))
            key_parts.append(matmul_tn(grad_scores, query))
            value_parts.append(matmul_tn(probabilities.astype(BF16), grad_part))
        grad_query = jnp.concatenate(query_parts, 1)
        grad_query = turned(grad_query, cosine_ref[rows, :], -sine_ref[rows, :]).astype(BF16)
        for i, (u, g) in enumerate(places):
            out[m, u, 0, g, :, pl.ds(lane, lanes)] = grad_query[i * tokens : (i + 1) * tokens]
        dk_s[:last, :] += jnp.concatenate(key_parts, 1)
        dv_s[:last, :] += jnp.concatenate(value_parts, 1)

    def heads(lane):
        load_heads(seq, seq_at, lane, cosine_ref, sine_ref, held)
        dk_s[...] = jnp.zeros_like(dk_s)
        dv_s[...] = jnp.zeros_like(dv_s)
        over_rows(length, rows_at_once, lambda first, last: rows_of(first, last, lane))

        def one(block, carry):
            u, g = place_of(block)
            rows = pl.ds(pl.multiple_of(block * tokens, tokens), tokens)
            grad_key = turned(dk_s[rows, :], cosine_ref[rows, :], -sine_ref[rows, :])
            out[m, u, 1, g, :, pl.ds(lane, lanes)] = grad_key.astype(BF16)
            out[m, u, 2, g, :, pl.ds(lane, lanes)] = dv_s[rows, :].astype(BF16)
            return carry

        lax.fori_loop(0, length // tokens, one, 0)

    over_lanes(width, lanes, heads)


def back_kernel(sizes, *refs):
    micros, groups, n_mlp, n_att = sizes
    stages = len(replica_stages())

    def take(count):
        nonlocal refs
        taken, refs = refs[:count], refs[count:]
        return taken

    e_in, mixed_in, x2_in, gg_in, xg_in, attended_in, seq_in, g_ref, x_ref, cosine_ref, sine_ref = take(11)
    grads_in, w_att = take(n_mlp), take(n_att)
    own_mlp, other_mlp, own_att, other_att = take(n_mlp), take(n_mlp), take(n_att), take(n_att)
    (input_out,) = take(1)
    kept_mlp, kept_att = take(n_mlp), take(n_att)
    landed_mlp = [take(stages) for _ in range(n_mlp)]
    landed_att = [take(stages) for _ in range(n_att)]
    (partial, leaving, came, passing, last, came_c, last_c, total, total_c, rows_g,
     turned_g, leaves, room_a, room_b, final, made_o, arrived_o, made_b, rows_b, rows_o,
     acts, weights, seq, q_s, k_s, v_s, dk_s, dv_s, send, recv, local) = refs
    each = range(micros)
    upper = lax.axis_index("blk") // 2
    tokens, width = x_ref.shape[-2:]
    here = made_o.shape[-1]
    heads_width = here * groups
    _, kept_pieces, piece, _ = kept_mlp[0].shape
    copies = Copies(send, recv, local)
    count = 4 * tokens
    tile = 256

    greet()
    loads = [copies.inside(e_in, partial), copies.inside(mixed_in, total_c)]
    for load in loads:
        load.wait()
    for m in each:
        total[m] = jnp.zeros_like(total[m])
    scatters = [TokenScatter(copies, partial, leaving, came, passing, last, total, m) for m in each]

    busy = []

    def weight_grad(acts, grads, kept, landed, own, other):
        part_columns = grads[0].shape[-1]
        columns = part_columns * len(grads)
        for copy in busy:
            copies.wait_sent(copy)
        busy.clear()
        per_half = kept_pieces * piece // tile
        pieces = tile // piece
        for side in (1, 0):
            side_room = leaves if side else room_a

            def one(i, carry, side=side, side_room=side_room):
                low, part = i // per_half, i % per_half
                start = low * (2 * kept_pieces * piece) + side * (kept_pieces * piece) + part * tile
                lanes = pl.ds(pl.multiple_of(start, tile), tile)
                left = acts[:, :, :, :, lanes].reshape(micros * count, tile)
                for j, right in enumerate(grads):
                    product = matmul_tn(left, right[...].reshape(micros * count, part_columns)).astype(BF16)
                    columns_here = slice(j * part_columns, (j + 1) * part_columns)
                    side_room[low, pl.ds(part * pieces, pieces), :, columns_here] = product.reshape(
                        pieces, piece, part_columns
                    )
                return carry

            lax.fori_loop(0, 2 * per_half, one, 0)
            source = side_room.at[:, :, :, 0:columns]
            if side:
                first = copies.remote(source, landed[0], *replica_stages()[-1])
                busy.append(first)
            else:
                copies.inside(source, kept).wait()
        return GradScatter(copies, kept, first, landed, (room_a, room_b), final, own, other)

    chunks = []

    def pump():
        for chunk in reversed(chunks):
            if chunk.stage <= stages:
                chunk.advance()

    def load_grads(k):
        loads = []
        for half_of in range(2):
            lanes = slice(half_of * heads_width, (half_of + 1) * heads_width)
            for row in range(2 * kept_pieces):
                source = grads_in[k].at[row * piece : (row + 1) * piece, lanes]
                loads.append(copies.inside(source, weights.at[k % 2, half_of, row]))
        return loads

    acts_load = copies.inside(x2_in, acts)
    slots = [load_grads(0)]

    def mlp_chunk(k):
        for load in slots[k]:
            load.wait()
        if k + 1 < n_mlp:
            slots.append(load_grads(k + 1))
        parts = [weights.at[k % 2, half] for half in range(2)]
        return weight_grad(acts, parts, kept_mlp[k], landed_mlp[k], own_mlp[k], other_mlp[k])

    acts_load.wait()
    chunks.append(mlp_chunk(0))
    chunks.append(mlp_chunk(1))
    for scatter in scatters:
        scatter.second()
    pump()
    chunks.append(mlp_chunk(2))
    gathers = []
    for m in each:
        scatters[m].end()
        mixed = total_c[m]
        scale = lax.rsqrt(jnp.mean(mixed * mixed, -1, keepdims=True) + EPSILON)
        total[m] = g_ref[m].astype(F32) + norm_back(total[m], mixed, scale)
        rows_g[m, 0, 0] = total[m].astype(BF16)
        gathers.append(TokenGather(copies, rows_g, turned_g, m))
    pump()
    chunks.append(mlp_chunk(3))
    acts_load = copies.inside(gg_in, acts)
    for gather in gathers:
        gather.second()
    acts_load.wait()
    chunks.append(mlp_chunk(4))
    pump()
    chunks.append(mlp_chunk(5))
    for gather in gathers:
        gather.end()

    for scatter in scatters:
        scatter.release()
    w_loads = [copies.inside(w_att[i], weights.at[slot]) for i, slot in ((3, 0), (0, 1), (1, 2))]
    seq_load = copies.inside(seq_in.at[0], seq.at[0])
    att_loads = [
        copies.inside(attended_in.at[m, place], rows_o.at[4 * m : 4 * m + 4, :, place * here : (place + 1) * here])
        for m in each
        for place in range(groups)
    ]
    w_loads[0].wait()
    crossing = []
    for m in each:
        rows = rows_g[m].reshape(count, width)
        product = matmul(rows, weights[0].reshape(width, heads_width)).astype(BF16)
        for place in range(groups):
            for group in range(4):
                made_o[m, place, group] = product[
                    group * tokens : (group + 1) * tokens, place * here : (place + 1) * here
                ]
        moves = [copies.inside(made_o.at[m, upper], arrived_o.at[m, upper])]
        for r in range(1, groups):
            source = made_o.at[m, flipped("blk", 2 * r) // 2]
            moves.append(copies.remote(source, arrived_o.at[m, upper], "blk", 2 * r))
        crossing.append(moves)
    w_loads.append(copies.inside(w_att[2], weights.at[0]))
    for load in att_loads:
        load.wait()
    chunks.append(weight_grad(rows_g, [rows_o], kept_att[3], landed_att[3], own_att[3], other_att[3]))
    returning = []
    own_lanes = pl.ds(pl.multiple_of(upper * here, here), here)
    for m in each:
        seq_load.wait()
        crossing[m][0].wait()
        for copy in crossing[m][1:]:
            copy.wait_recv()
        attend_back(seq, 0, arrived_o, made_b, m, cosine_ref, sine_ref, (q_s, k_s, v_s), (dk_s, dv_s))
        if m + 1 < micros:
            seq_load = copies.inside(seq_in.at[m + 1], seq.at[0])
        moves = ([], [])
        for i in range(3):
            target = rows_b.at[i, 4 * m : 4 * m + 4, :, own_lanes]
            moves[0].append(copies.inside(made_b.at[m, upper, i], target))
            for r in range(1, groups):
                source = made_b.at[m, flipped("blk", 2 * r) // 2, i]
                moves[1].append(copies.remote(source, target, "blk", 2 * r))
        returning.append(moves)
        pump()
    for load in w_loads[1:]:
        load.wait()
    started = []
    for m in each:
        for copy in returning[m][0]:
            copy.wait()
        for copy in returning[m][1]:
            copy.wait_recv()
        pieces = tile // piece
        for start in range(0, width, tile):
            low, first = start // (2 * kept_pieces * piece), start // piece % (2 * kept_pieces)
            product = functools.reduce(
                jnp.add,
                [
                    matmul_nt(
                        rows_b[i, 4 * m : 4 * m + 4].reshape(count, heads_width),
                        weights[(i + 1) % 3, low, first : first + pieces].reshape(tile, heads_width),
                    )
                    for i in range(3)
                ],
            ).astype(BF16)
            for group in range(4):
                partial[m, group // 2, group % 2, :, start : start + tile] = product[
                    group * tokens : (group + 1) * tokens
                ]
        total_c[m] = jnp.zeros_like(total_c[m])
        started.append(TokenScatter(copies, partial, leaving, came_c, passing, last_c, total_c, m))

    copies.inside(xg_in, acts).wait()
    for i in range(3):
        chunks.append(weight_grad(acts, [rows_b.at[i]], kept_att[i], landed_att[i], own_att[i], other_att[i]))
    pump()
    for scatter in started:
        scatter.second()
    pump()
    for m in each:
        started[m].end()
        started[m].release()
        values = x_ref[m].astype(F32)
        scale = lax.rsqrt(jnp.mean(values * values, -1, keepdims=True) + EPSILON)
        passing[m] = (total[m] + norm_back(total_c[m], values, scale)).astype(BF16)
    copies.inside(passing, input_out).wait()
    while any(chunk.stage <= stages for chunk in chunks):
        pump()
    copies.finish()


def back(partial, mixed, x2, grad_rows, normed_one, attended, sequences, g_rows, x_rows, tables, grads, w_att):
    micros, tokens, width = x_rows.shape
    n_mlp, n_att = len(grads), len(w_att)
    columns = grads[0].shape[1]
    _, replicas, piece, heads_width = w_att[0].shape
    groups = head_groups()
    here = heads_width // groups
    stages = len(replica_stages())
    any_space = pl.BlockSpec(memory_space=pl.ANY)
    in_vmem = pl.BlockSpec(memory_space=pltpu.VMEM)

    def bf16(*shape):
        return jax.ShapeDtypeStruct(shape, BF16)

    def room(*shape):
        return pltpu.VMEM(shape, BF16)

    def f32_room(*shape):
        return pltpu.VMEM(shape, F32)

    widths = [columns] * n_mlp + [heads_width] * n_att
    outs = [jax.ShapeDtypeStruct((piece, columns), F32)] * n_mlp + [bf16(piece, columns)] * n_mlp
    outs += [jax.ShapeDtypeStruct((piece, heads_width), F32)] * n_att + [bf16(piece, heads_width)] * n_att
    outs += [bf16(micros, tokens, width)]
    outs += [bf16(2, replicas // 2, piece, w) for w in widths]
    outs += [bf16(2, replicas >> (s + 1), piece, w) for w in widths for s in range(stages)]
    token_rows = (micros, 2, 2, tokens, width)
    half_room = (2, replicas // 2, piece, max(columns, heads_width))
    scratch = [
        room(*token_rows),
        room(micros, 2, tokens, width),
        room(micros, 2, tokens, width),
        room(micros, tokens, width),
        room(micros, tokens, width),
        room(micros, 2, tokens, width),
        room(micros, tokens, width),
        f32_room(micros, tokens, width),
        f32_room(micros, tokens, width),
        room(*token_rows),
        room(micros, 2, tokens, width),
        room(*half_room),
        room(*half_room),
        room(*half_room),
        f32_room(piece, max(columns, heads_width)),
        room(micros, groups, 4, tokens, here),
        room(micros, groups, 4, tokens, here),
        room(micros, groups, 3, 4, tokens, here),
        room(3, micros * 4, tokens, heads_width),
        room(micros * 4, tokens, heads_width),
        room(*token_rows),
        room(3, 2, replicas, piece, heads_width),
        room(1, groups, 3, 4, tokens, here),
        *[room(*tables[0].shape)] * 3,
        *[f32_room(*tables[0].shape)] * 2,
        pltpu.SemaphoreType.DMA((128,)),
        pltpu.SemaphoreType.DMA((128,)),
        pltpu.SemaphoreType.DMA((384,)),
    ]
    results = pl.pallas_call(
        functools.partial(back_kernel, (micros, groups, n_mlp, n_att)),
        out_shape=outs,
        in_specs=[any_space] * 7 + [in_vmem] * 4 + [any_space] * (n_mlp + n_att),
        out_specs=[any_space] * len(outs),
        scratch_shapes=scratch,
        compiler_params=pltpu.CompilerParams(
            collective_id=1, has_side_effects=True, vmem_limit_bytes=63 * 1024 * 1024
        ),
    )(partial, mixed, x2, grad_rows, normed_one, attended, sequences, g_rows, x_rows, *tables, *grads, *w_att)
    own_mlp, results = results[:n_mlp], results[n_mlp:]
    other_mlp, results = results[:n_mlp], results[n_mlp:]
    own_att, results = results[:n_att], results[n_att:]
    other_att, results = results[:n_att], results[n_att:]
    return list(zip(own_mlp, other_mlp)), list(zip(own_att, other_att)), results[0]


def scale_of(values):
    return lax.rsqrt(jnp.mean(values * values, -1, keepdims=True) + EPSILON)


def norm_back(grad, values, scale):
    return scale * grad - values * (scale * scale * scale) * jnp.mean(grad * values, -1, keepdims=True)


def on_device(
    block_input,
    attention_gain,
    query_weight,
    key_weight,
    value_weight,
    output_weight,
    mlp_gain,
    gate_weight,
    up_weight,
    down_weight,
    grad_output,
):
    micros, _, tokens, width = block_input.shape
    heads_width = query_weight.shape[1] // 2
    length = tokens * lax.axis_size("blk") * lax.axis_size("head")
    to_own, to_absolute = feature_order()
    order = block_order()
    tables = rope_tables(length, min(LANES, heads_width // head_groups()))
    each = range(micros)
    head_first = [m % 2 == 1 for m in each]

    gain_one = attention_gain.astype(F32)[:, None]
    gain_two = mlp_gain.astype(F32)[:, None]

    def scaled(weight, gain):
        return (weight.astype(F32) * gain).astype(BF16)

    def joined(parts):
        return jnp.concatenate(parts, 0)

    def columns_of(weight, parts):
        rows, columns = weight.shape
        return weight.reshape(rows, parts, columns // parts).swapaxes(0, 1)

    att_in = jnp.stack(
        [columns_of(scaled(w, gain_one), 2) for w in (query_weight, key_weight, value_weight)]
        + [columns_of(output_weight.T, 2)]
    )
    mlp_in = jnp.stack(
        [columns_of(scaled(w, gain_two), 4) for w in (gate_weight, up_weight)] + [columns_of(down_weight.T, 4)]
    )
    block_rows = [array.reshape(micros * tokens, width) for array in (block_input, grad_output)]
    inputs_low, grad_low = (rows.reshape(micros, tokens, width) for rows in reorder(to_own, *block_rows))
    grad_turned = turn_features(grad_low.reshape(micros * tokens, width)).reshape(micros, tokens, width)
    w_att, w_mlp, held = front(inputs_low, grad_low, grad_turned, att_in, mlp_in, tables)
    normed_one, sequences, attended, mixed, normed_two, grad_rows = held
    normed_two_all = normed_two.reshape(-1, width)
    grad_rows_all = grad_rows.reshape(-1, width)
    gate_parts, up_parts, down_parts = w_mlp[0:4:2], w_mlp[1:4:2], w_mlp[4:]

    hidden, grad_gate, grad_up = [], [], []
    grad_normed = produced = 0.0
    for gate_full, up_full, down_full in zip(gate_parts, up_parts, down_parts):
        gate = matmul(normed_two_all, gate_full)
        up = matmul(normed_two_all, up_full)
        sigmoid = jax.nn.sigmoid(gate)
        activated = gate * sigmoid
        hidden.append((activated * up).astype(BF16))
        grad_hidden = matmul(grad_rows_all, down_full)
        grad_gate.append((grad_hidden * up * sigmoid * (1.0 + gate * (1.0 - sigmoid))).astype(BF16))
        grad_up.append((grad_hidden * activated).astype(BF16))
        grad_normed += matmul_nt(grad_gate[-1], gate_full) + matmul_nt(grad_up[-1], up_full)
        produced += matmul_nt(hidden[-1], down_full)

    def split(rows):
        size = rows.shape[0] // micros
        return [rows[m * size : (m + 1) * size] for m in each]

    produced = split(produced)
    outputs = [(mixed[m] + scatter_tokens(produced[m], head_first[m])).astype(BF16) for m in each]

    if sequences.shape[-1] % LANES == 0 and micros * 4 * tokens == width // 2:
        mlp_pairs, att_pairs, input_grads = back(
            grad_normed.astype(BF16).reshape(normed_two.shape), mixed, normed_two, grad_rows, normed_one, attended,
            sequences, grad_low, inputs_low, tables,
            [grad_gate[0], grad_up[0], grad_gate[1], grad_up[1], hidden[0], hidden[1]], w_att,
        )
        input_grads = [input_grads[m] for m in each]

        def beside(pairs):
            return tuple(jnp.concatenate(side, 1) for side in zip(*pairs))

        gate_grad, up_grad, down_grad = beside(mlp_pairs[0:4:2]), beside(mlp_pairs[1:4:2]), beside(mlp_pairs[4:])
        output_grad = att_pairs[3]
        qkv_grads = [side_by_side(*pair) for pair in att_pairs[:3]]
    else:
        upper = lax.axis_index("blk") // 2
        w_att = [w.reshape(width, -1) for w in w_att]
        normed_one_all = normed_one.reshape(-1, width)
        sequences = [lax.dynamic_index_in_dim(sequences, upper ^ r, 1, keepdims=False) for r in range(head_groups())]
        sequences = jnp.concatenate(sequences, 2)
        attended = jnp.concatenate([attended[:, g] for g in range(head_groups())], -1)
        attended_all = attended.reshape(micros * 4 * tokens, -1)
        grad_normed = split(grad_normed)
        grad_mixed = []
        for m in each:
            back_rows = norm_back(scatter_tokens(grad_normed[m], head_first[m]), mixed[m], scale_of(mixed[m]))
            grad_mixed.append(grad_low[m].astype(F32) + back_rows)
        gate_grad = scatter_weight_grad(normed_two_all, jnp.concatenate(grad_gate, 1))
        up_grad = scatter_weight_grad(normed_two_all, jnp.concatenate(grad_up, 1))
        down_grad = scatter_weight_grad(grad_rows_all, jnp.concatenate(hidden, 1))
        grad_mixed_rows = [gather_tokens(grad_mixed[m].astype(BF16), head_first[m]) for m in each]
        grad_qkv, input_grads = [], []
        for m in each:
            grad_attended = matmul(grad_mixed_rows[m], w_att[3]).astype(BF16)
            grad_sequences = attention_call(order, sequences[m], tables, to_sequences([grad_attended])[0])
            returned = from_sequences(grad_sequences)
            grad_qkv.append(jnp.concatenate([returned[0], returned[1], returned[2]], 1))
            terms = [matmul_nt(returned[i], w_att[i]) for i in range(3)]
            grad_normed_one = scatter_tokens(functools.reduce(jnp.add, terms), head_first[m])
            inputs = inputs_low[m].astype(F32)
            back_rows = norm_back(grad_normed_one, inputs, scale_of(inputs))
            input_grads.append((grad_mixed[m] + back_rows).astype(BF16))
        output_grad = scatter_weight_grad(joined(grad_mixed_rows), attended_all)
        qkv_grad = scatter_weight_grad(normed_one_all, joined(grad_qkv))
        qkv_grads = [
            side_by_side(*(side[:, i * heads_width : (i + 1) * heads_width] for side in qkv_grad)) for i in range(3)
        ]
    mlp_grads = [side_by_side(*gate_grad), side_by_side(*up_grad)]

    def gain_grad(weights, grads):
        terms = [jnp.sum(w.astype(F32) * g, 1) for w, g in zip(weights, grads)]
        here = functools.reduce(jnp.add, terms)
        return here + swap(here, "head", 1)

    attention_gain_grad = gain_grad((query_weight, key_weight, value_weight), qkv_grads)
    mlp_gain_grad = gain_grad((gate_weight, up_weight), mlp_grads)
    block_output, input_grad = reorder(to_absolute, joined(outputs), joined(input_grads))

    return (
        block_output.reshape(micros, 1, tokens, width),
        input_grad.reshape(micros, 1, tokens, width),
        attention_gain_grad,
        qkv_grads[0] * gain_one,
        qkv_grads[1] * gain_one,
        qkv_grads[2] * gain_one,
        side_by_side(*output_grad).T,
        mlp_gain_grad,
        mlp_grads[0] * gain_two,
        mlp_grads[1] * gain_two,
        side_by_side(*down_grad).T,
    )


def solution(mesh):
    rows, row_split = P(None, "dp", ("head", "blk"), None), P(("dp", "blk"), "head")
    column_split, gain = P("head", ("dp", "blk")), P(("dp", "blk"))
    return jax.shard_map(
        on_device,
        mesh=mesh,
        in_specs=(
            rows, gain, row_split, row_split, row_split, column_split, gain, row_split, row_split, column_split, rows,
        ),
        out_specs=(
            rows, rows, gain, row_split, row_split, row_split, column_split, gain, row_split, row_split, column_split,
        ),
        check_vma=False,
    )
```

```python
import functools

import jax
import jax.numpy as jnp
import numpy as np
from jax import lax
from jax.experimental import pallas as pl
from jax.experimental.pallas import tpu as pltpu
from jax.sharding import PartitionSpec as P

HD = 64
EPSILON = 1e-05
ROPE_BASE = 130000.0
MASKED_SCORE = -1e30
F32 = jnp.float32
BF16 = jnp.bfloat16
LANES = 128
MESH = pl.DeviceIdType.MESH


def swap(value, axis, bit):
    count = lax.axis_size(axis)
    return lax.ppermute(value, axis, [(i, i ^ bit) for i in range(count)])


def bits_of(count):
    return [1 << i for i in range(count.bit_length() - 1)]


def replica_stages():
    upper = [("blk", bit) for bit in bits_of(lax.axis_size("blk"))[1:]]
    return upper + [("dp", bit) for bit in reversed(bits_of(lax.axis_size("dp")))]


def matmul(left_side, right_side):
    return jnp.dot(left_side, right_side, preferred_element_type=F32)


def matmul_nt(left_side, right_side):
    return lax.dot_general(left_side, right_side, (((1,), (1,)), ((), ())), preferred_element_type=F32)


def matmul_tn(left_side, right_side):
    return lax.dot_general(left_side, right_side, (((0,), (0,)), ((), ())), preferred_element_type=F32)


def feature_order():
    n_blk, n_dp = lax.axis_size("blk"), lax.axis_size("dp")
    order = np.zeros((1,), np.int32)
    for axis, bit in replica_stages():
        order = np.concatenate([order, order ^ (bit if axis == "blk" else bit * n_blk)])
    order = np.concatenate([order, order ^ 1])
    assert order.size == n_blk * n_dp
    mine = lax.axis_index("dp") * n_blk + lax.axis_index("blk")
    back = np.argsort(order).astype(np.int32)
    absolute = jnp.arange(order.size, dtype=jnp.int32) ^ mine
    return jnp.asarray(order) ^ mine, jnp.asarray(back)[absolute]


def reorder_kernel(count, order_ref, *refs):
    for source, target in zip(refs[:count], refs[count:]):
        blocks = order_ref.shape[0]
        piece = source.shape[1] // blocks
        for j in range(blocks):
            start = pl.multiple_of(order_ref[j] * piece, piece)
            target[:, j * piece : (j + 1) * piece] = source[:, pl.ds(start, piece)]


def reorder(order, *arrays):
    count, width = arrays[0].shape
    blocks = order.shape[0]
    piece = width // blocks
    if piece % LANES:
        return [jnp.take(rows.reshape(count, blocks, piece), order, axis=1).reshape(count, width) for rows in arrays]
    in_vmem = pl.BlockSpec(memory_space=pltpu.VMEM)
    return pl.pallas_call(
        functools.partial(reorder_kernel, len(arrays)),
        in_specs=[pl.BlockSpec(memory_space=pltpu.SMEM)] + [in_vmem] * len(arrays),
        out_specs=[in_vmem] * len(arrays),
        out_shape=[jax.ShapeDtypeStruct(rows.shape, rows.dtype) for rows in arrays],
    )(order, *arrays)


def turn_features(rows):
    half = rows.shape[1] // 2
    return jnp.concatenate([rows[:, half:], rows[:, :half]], 1)


def gather_tokens(rows, head_first):
    count = rows.shape[0]
    if head_first:
        other = swap(rows, "head", 1)
        far = swap(turn_features(jnp.concatenate([rows, other], 0)), "blk", 1)
        return jnp.concatenate([rows, far[:count], other, far[count:]], 0)
    both = jnp.concatenate([rows, swap(turn_features(rows), "blk", 1)], 0)
    return jnp.concatenate([both, swap(both, "head", 1)], 0)


def scatter_tokens(partial, head_first):
    partial = partial.astype(BF16)
    count = partial.shape[0] // 4
    if head_first:
        came = swap(partial[2 * count :], "head", 1)
        mine = partial[:count].astype(F32) + came[:count].astype(F32)
        theirs = (partial[count : 2 * count].astype(F32) + came[count:].astype(F32)).astype(BF16)
        return mine + swap(turn_features(theirs), "blk", 1).astype(F32)
    leaving = jnp.concatenate([partial[count : 2 * count], partial[3 * count :]], 0)
    came = swap(turn_features(leaving), "blk", 1)
    mine = partial[:count].astype(F32) + came[:count].astype(F32)
    theirs = (partial[2 * count : 3 * count].astype(F32) + came[count:].astype(F32)).astype(BF16)
    return mine + swap(theirs, "head", 1).astype(F32)


def own_and_other(columns):
    width = columns.shape[1] // 2
    place = lax.axis_index("blk") % 2
    return (
        lax.dynamic_slice_in_dim(columns, place * width, width, 1),
        lax.dynamic_slice_in_dim(columns, (1 - place) * width, width, 1),
    )


def gather_weight(own, other):
    streams = [own, swap(other, "blk", 1)]
    stages = replica_stages()
    for axis, bit in stages[:-1]:
        streams = [jnp.concatenate([held, swap(held, axis, bit)], 0) for held in streams]
    pieces = []
    for held in streams:
        pieces += [held, swap(held, *stages[-1])]
    return jnp.concatenate(pieces, 0)


def scatter_weight_grad(acts, grads):
    quarter = acts.shape[1] // 4
    stages = replica_stages()[::-1]

    def piece(place):
        return matmul_tn(acts[:, place * quarter : (place + 1) * quarter], grads).astype(BF16)

    streams = []
    for first in (2, 0):
        came = swap(piece(first + 1), *stages[0])
        held = piece(first).astype(F32) + came.astype(F32)
        for axis, bit in stages[1:]:
            half = held.shape[0] // 2
            held = held.astype(BF16)
            came = swap(held[half:], axis, bit)
            held = held[:half].astype(F32) + came.astype(F32)
        streams.append(held)
    return streams[1], swap(streams[0].astype(BF16), "blk", 1)


def side_by_side(own, other):
    other = other.astype(F32)
    low = lax.axis_index("blk") % 2 == 0
    return jnp.concatenate([jnp.where(low, own, other), jnp.where(low, other, own)], 1)


def head_groups():
    return lax.axis_size("blk") // 2


def to_sequences(parts):
    groups = head_groups()
    upper = lax.axis_index("blk") // 2
    width = parts[0].shape[1] // groups
    arrived = []
    for r in range(groups):
        chosen = jnp.stack([lax.dynamic_slice_in_dim(part, (upper ^ r) * width, width, 1) for part in parts])
        if r:
            chosen = lax.ppermute(chosen, "blk", [(i, i ^ (2 * r)) for i in range(2 * groups)])
        arrived.append(chosen.reshape(len(parts), 4, -1, width))
    return jnp.concatenate(arrived, 1)


def from_sequences(blocks):
    groups = head_groups()
    upper = lax.axis_index("blk") // 2
    count, _, tokens, width = blocks.shape
    arrived = []
    for r in range(groups):
        chosen = blocks[:, 4 * r : 4 * r + 4]
        if r:
            chosen = lax.ppermute(chosen, "blk", [(i, i ^ (2 * r)) for i in range(2 * groups)])
        arrived.append(chosen.reshape(count, 4 * tokens, width))
    stacked = jnp.stack(arrived)
    ordered = [lax.dynamic_index_in_dim(stacked, h ^ upper, 0, keepdims=False) for h in range(groups)]
    return jnp.concatenate(ordered, 2)


def block_order():
    n_blk, n_head = lax.axis_size("blk"), lax.axis_size("head")
    block = np.arange(n_blk * n_head, dtype=np.int32)
    r_head = (block // n_blk) ^ lax.axis_index("head")
    r_blk = (block % n_blk) ^ lax.axis_index("blk")
    return ((r_blk // 2) * 2 + r_head) * 2 + r_blk % 2


def rope_tables(length, lanes):
    half = HD // 2
    frequency = ROPE_BASE ** (-np.arange(half, dtype=np.float32) * np.float32(2.0 / HD))
    angles = np.arange(length, dtype=np.float32)[:, None] * frequency.astype(np.float32)[None, :]
    cosine, sine = np.cos(angles), np.sin(angles)
    return (
        jnp.asarray(np.tile(cosine, (1, lanes // half)), F32),
        jnp.asarray(np.tile(np.concatenate([-sine, sine], 1), (1, lanes // HD)), F32),
    )


def turned(rows, cosine, sine):
    half = HD // 2
    parts = []
    for start in range(0, rows.shape[1], HD):
        parts += [rows[:, start + half : start + HD], rows[:, start : start + half]]
    return rows * cosine + jnp.concatenate(parts, 1) * sine


def load_sequence(order_ref, qkv_ref, cosine_ref, sine_ref, held, tokens, blocks):
    def one(block, carry):
        place = order_ref[block]
        rows = pl.ds(pl.multiple_of(block * tokens, tokens), tokens)
        for part in range(3):
            value = qkv_ref[part, place]
            if part < 2:
                value = turned(value.astype(F32), cosine_ref[rows, :], sine_ref[rows, :]).astype(BF16)
            held[part][rows, :] = value
        return carry

    lax.fori_loop(0, blocks, one, 0)


def softmax_rows(query, keys, first_row):
    scores = matmul_nt(query, keys) * HD ** (-0.5)
    row = first_row + lax.broadcasted_iota(jnp.int32, scores.shape, 0)
    scores = jnp.where(lax.broadcasted_iota(jnp.int32, scores.shape, 1) <= row, scores, MASKED_SCORE)
    weights = jnp.exp(scores - jnp.max(scores, 1, keepdims=True))
    return weights, 1.0 / jnp.sum(weights, 1, keepdims=True)


def attend_kernel(tokens, blocks, rows_at_once, order_ref, qkv_ref, cosine_ref, sine_ref, out_ref, q_s, k_s, v_s):
    lanes = qkv_ref.shape[-1]
    load_sequence(order_ref, qkv_ref, cosine_ref, sine_ref, (q_s, k_s, v_s), tokens, blocks)
    for first in range(0, tokens * blocks, rows_at_once):
        last = first + rows_at_once
        results = []
        for lane in range(0, lanes, HD):
            head = slice(lane, lane + HD)
            weights, inverse = softmax_rows(q_s[first:last, head], k_s[:last, head], first)
            results.append(matmul(weights.astype(BF16), v_s[:last, head]) * inverse)
        result = jnp.concatenate(results, 1).astype(BF16)
        for offset in range(0, rows_at_once, tokens):
            out_ref[order_ref[(first + offset) // tokens]] = result[offset : offset + tokens]


def attend_back_kernel(
    tokens, blocks, rows_at_once, order_ref, qkv_ref, grad_ref, cosine_ref, sine_ref, out_ref,
    q_s, k_s, v_s, dk_s, dv_s,
):
    lanes = qkv_ref.shape[-1]
    load_sequence(order_ref, qkv_ref, cosine_ref, sine_ref, (q_s, k_s, v_s), tokens, blocks)
    dk_s[...] = jnp.zeros_like(dk_s)
    dv_s[...] = jnp.zeros_like(dv_s)
    for first in range(0, tokens * blocks, rows_at_once):
        last = first + rows_at_once
        arrived = [grad_ref[order_ref[row // tokens]] for row in range(first, last, tokens)]
        grad_rows = jnp.concatenate(arrived, 0)
        query_parts, key_parts, value_parts = [], [], []
        for lane in range(0, lanes, HD):
            head = slice(lane, lane + HD)
            query, keys, grad = q_s[first:last, head], k_s[:last, head], grad_rows[:, head]
            weights, inverse = softmax_rows(query, keys, first)
            probabilities = weights * inverse
            grad_prob = matmul_nt(grad, v_s[:last, head])
            row_delta = jnp.sum(probabilities * grad_prob, 1, keepdims=True)
            grad_scores = (probabilities * (grad_prob - row_delta) * HD ** (-0.5)).astype(BF16)
            query_parts.append(matmul(grad_scores, keys))
            key_parts.append(matmul_tn(grad_scores, query))
            value_parts.append(matmul_tn(probabilities.astype(BF16), grad))
        grad_query = jnp.concatenate(query_parts, 1)
        grad_query = turned(grad_query, cosine_ref[first:last, :], -sine_ref[first:last, :]).astype(BF16)
        for offset in range(0, rows_at_once, tokens):
            out_ref[0, order_ref[(first + offset) // tokens]] = grad_query[offset : offset + tokens]
        dk_s[:last, :] += jnp.concatenate(key_parts, 1)
        dv_s[:last, :] += jnp.concatenate(value_parts, 1)

    def one(block, carry):
        place = order_ref[block]
        rows = pl.ds(pl.multiple_of(block * tokens, tokens), tokens)
        out_ref[1, place] = turned(dk_s[rows, :], cosine_ref[rows, :], -sine_ref[rows, :]).astype(BF16)
        out_ref[2, place] = dv_s[rows, :].astype(BF16)
        return carry

    lax.fori_loop(0, blocks, one, 0)


def attention_call(order, qkv, tables, grad=None):
    _, blocks, tokens, width = qkv.shape
    length = blocks * tokens
    lanes = min(LANES, width)
    rows_at_once = min(256, length) if length <= 2048 else LANES
    back = grad is not None

    def fixed(j, order_ref):
        return (0, 0)

    part = pl.BlockSpec((blocks, tokens, lanes), lambda j, order_ref: (0, 0, j))
    three = pl.BlockSpec((3, blocks, tokens, lanes), lambda j, order_ref: (0, 0, 0, j))
    table = pl.BlockSpec((length, lanes), fixed)
    kernel = attend_back_kernel if back else attend_kernel
    scratch = [pltpu.VMEM((length, lanes), BF16)] * 3
    if back:
        scratch += [pltpu.VMEM((length, lanes), F32)] * 2
    products = 5 if back else 2
    return pl.pallas_call(
        functools.partial(kernel, tokens, blocks, rows_at_once),
        grid_spec=pltpu.PrefetchScalarGridSpec(
            num_scalar_prefetch=1,
            grid=(width // lanes,),
            in_specs=[three] + ([part] if back else []) + [table, table],
            out_specs=three if back else part,
            scratch_shapes=scratch,
        ),
        out_shape=jax.ShapeDtypeStruct(qkv.shape if back else qkv.shape[1:], BF16),
        compiler_params=pltpu.CompilerParams(vmem_limit_bytes=48 * 1024 * 1024),
        cost_estimate=pl.CostEstimate(
            flops=products * 4 * length * length * width,
            bytes_accessed=(7 if back else 4) * length * width * 2,
            transcendentals=length * length * (width // HD),
        ),
    )(order, qkv, *([grad] if back else []), *tables)


def greet():
    masks = [("head", 1)] + [("dp", bit) for bit in bits_of(lax.axis_size("dp"))]
    masks += [("blk", 1)] + [("blk", 2 * r) for r in range(1, head_groups())]
    barrier = pltpu.get_barrier_semaphore()
    for axis, mask in masks:
        pl.semaphore_signal(barrier, inc=1, device_id={axis: flipped(axis, mask)}, device_id_type=MESH)
    pl.semaphore_wait(barrier, len(masks))


def flipped(axis, mask):
    place, other = lax.axis_index(axis), 0
    for bit in bits_of(lax.axis_size(axis)):
        digit = (place // bit) % 2
        other = other + bit * ((1 - digit) if mask & bit else digit)
    return other


class Copies:
    def __init__(self, send, recv, local):
        self.send, self.recv, self.local = send, recv, local
        self.remote_count = self.local_count = 0
        self.sent = []

    def remote(self, source, target, axis, mask):
        k = self.remote_count
        self.remote_count += 1
        copy = pltpu.make_async_remote_copy(
            src_ref=source, dst_ref=target, send_sem=self.send.at[k], recv_sem=self.recv.at[k],
            device_id={axis: flipped(axis, mask)}, device_id_type=MESH,
        )
        copy.start()
        self.sent.append(copy)
        return copy

    def inside(self, source, target):
        copy = pltpu.make_async_copy(source, target, self.local.at[self.local_count])
        self.local_count += 1
        copy.start()
        return copy

    def is_unsent(self, copy):
        return any(copy is other for other in self.sent)

    def wait_sent(self, copy):
        copy.wait_send()
        self.sent = [other for other in self.sent if other is not copy]

    def finish(self):
        for copy in self.sent:
            copy.wait_send()


def halves_turned(rows):
    half = rows.shape[-1] // 2
    return jnp.concatenate([rows[:, half:], rows[:, :half]], 1)


class WeightGather:
    def __init__(self, copies, own, other, full):
        self.copies, self.full, self.stage = copies, full, 0
        self.mine = copies.inside(own, full.at[0, 0])
        self.copy = copies.remote(other, full.at[1, 0], "blk", 1)

    def advance(self):
        if self.mine is not None:
            self.mine.wait()
            self.mine = None
        self.copy.wait_recv()
        stages = replica_stages()
        if self.stage < len(stages):
            held = 1 << self.stage
            self.copy = self.copies.remote(
                self.full.at[:, 0:held], self.full.at[:, held : 2 * held], *stages[self.stage]
            )
        self.stage += 1


class TokenGather:
    def __init__(self, copies, rows, turned_rows, m, head_first=None):
        self.copies, self.rows, self.turned_rows, self.m = copies, rows, turned_rows, m
        self.head_first = m % 2 == 1 if head_first is None else head_first
        if self.head_first:
            self.copy = copies.remote(rows.at[m, 0, 0], rows.at[m, 1, 0], "head", 1)
        else:
            turned_rows[m, 0] = halves_turned(rows[m, 0, 0])
            self.copy = copies.remote(turned_rows.at[m, 0], rows.at[m, 0, 1], "blk", 1)
        self.first = self.copy

    def second(self):
        m, rows, turned_rows = self.m, self.rows, self.turned_rows
        self.copy.wait_recv()
        if self.head_first:
            turned_rows[m, 0] = halves_turned(rows[m, 0, 0])
            turned_rows[m, 1] = halves_turned(rows[m, 1, 0])
            self.copy = self.copies.remote(turned_rows.at[m], rows.at[m, :, 1], "blk", 1)
        else:
            self.copy = self.copies.remote(rows.at[m, 0], rows.at[m, 1], "head", 1)

    def end(self):
        self.copy.wait_recv()

    def release(self):
        self.copies.wait_sent(self.first)
        self.copies.wait_sent(self.copy)


class TokenScatter:
    def __init__(self, copies, partial, leaving, came, passing, last, total, m, head_first=None):
        self.copies, self.partial, self.came, self.passing = copies, partial, came, passing
        self.last, self.total, self.m = last, total, m
        self.head_first = m % 2 == 0 if head_first is None else head_first
        if self.head_first:
            self.copy = copies.remote(partial.at[m, 1], came.at[m], "head", 1)
        else:
            leaving[m, 0] = halves_turned(partial[m, 0, 1])
            leaving[m, 1] = halves_turned(partial[m, 1, 1])
            self.copy = copies.remote(leaving.at[m], came.at[m], "blk", 1)
        self.first = self.copy

    def second(self):
        m, partial = self.m, self.partial
        self.copy.wait_recv()
        kept = partial[m, 0, 1] if self.head_first else partial[m, 1, 0]
        theirs = (kept.astype(F32) + self.came[m, 1].astype(F32)).astype(BF16)
        if self.head_first:
            self.passing[m] = halves_turned(theirs)
            self.copy = self.copies.remote(self.passing.at[m], self.last.at[m], "blk", 1)
        else:
            self.passing[m] = theirs
            self.copy = self.copies.remote(self.passing.at[m], self.last.at[m], "head", 1)
        self.total[m] += partial[m, 0, 0].astype(F32) + self.came[m, 0].astype(F32)

    def end(self):
        self.copy.wait_recv()
        self.total[self.m] += self.last[self.m].astype(F32)

    def release(self):
        self.copies.wait_sent(self.first)
        self.copies.wait_sent(self.copy)


def place_of(block):
    n_blk = lax.axis_size("blk")
    head, blk = block // n_blk, block % n_blk
    near = (blk + lax.axis_index("blk")) % 2
    return blk // 2, ((head + lax.axis_index("head")) % 2) * 2 + near


def load_heads(seq, m, lane, cosine_ref, sine_ref, held):
    tokens = seq.shape[-2]
    lanes = held[0].shape[1]
    blocks = held[0].shape[0] // tokens

    def one(block, carry):
        upper, group = place_of(block)
        rows = pl.ds(pl.multiple_of(block * tokens, tokens), tokens)
        for part in range(3):
            value = seq[m, upper, part, group, :, pl.ds(lane, lanes)]
            if part < 2:
                value = turned(value.astype(F32), cosine_ref[rows, :], sine_ref[rows, :]).astype(BF16)
            held[part][rows, :] = value
        return carry

    lax.fori_loop(0, blocks, one, 0)


def attend(seq, out, m, cosine_ref, sine_ref, held):
    tokens, width = seq.shape[-2:]
    q_s, k_s, v_s = held
    length, lanes = q_s.shape
    rows_at_once = min(256, length) if length <= 2048 else LANES

    def rows_of(first, last, lane):
        results = []
        for start in range(0, lanes, HD):
            head = slice(start, start + HD)
            weights, inverse = softmax_rows(q_s[pl.ds(first, rows_at_once), head], k_s[:last, head], first)
            results.append(matmul(weights.astype(BF16), v_s[:last, head]) * inverse)
        result = jnp.concatenate(results, 1).astype(BF16)
        for offset in range(0, rows_at_once, tokens):
            upper, group = place_of((first + offset) // tokens)
            out[m, upper, group, :, pl.ds(lane, lanes)] = result[offset : offset + tokens]

    def heads(lane):
        load_heads(seq, m, lane, cosine_ref, sine_ref, held)
        over_rows(length, rows_at_once, lambda first, last: rows_of(first, last, lane))

    over_lanes(width, lanes, heads)


def over_rows(length, rows_at_once, body):
    if length // rows_at_once <= 8:
        for first in range(0, length, rows_at_once):
            body(first, first + rows_at_once)
        return

    def one(j, carry):
        body(pl.multiple_of(j * rows_at_once, rows_at_once), length)
        return carry

    lax.fori_loop(0, length // rows_at_once, one, 0)


def over_lanes(width, lanes, body):
    if width == lanes:
        body(0)
        return

    def one(j, carry):
        body(pl.multiple_of(j * lanes, lanes))
        return carry

    lax.fori_loop(0, width // lanes, one, 0)


def store_normed(values, target, at):
    scale = lax.rsqrt(jnp.mean(values * values, -1, keepdims=True) + EPSILON)
    target[at] = (values * scale).astype(BF16)


def front_kernel(sizes, *refs):
    micros, groups, n_att, n_mlp = sizes
    x_ref, g_in, g_turned, att_in, mlp_in, cosine_ref, sine_ref = refs[:7]
    refs = refs[7:]
    w_att, refs = refs[:n_att], refs[n_att:]
    w_mlp, refs = refs[:n_mlp], refs[n_mlp:]
    xg_out, seq_out, attended_out, mixed_out, x2_out, gg_out = refs[:6]
    (xg, x2, turned_rows, turned_more, w_in, w_out, made, seq, heads_out, attended, partial,
     leaving, came, passing, last, mixed, q_s, k_s, v_s, send, recv, local) = refs[6:]
    held = (q_s, k_s, v_s)
    each = range(micros)
    near = lax.axis_index("blk") % 2
    upper = lax.axis_index("blk") // 2
    width = x_ref.shape[-1]
    tokens = x_ref.shape[-2]
    heads_width = w_in.shape[-1]
    here = heads_width // groups
    copies = Copies(send, recv, local)

    greet()
    att = [WeightGather(copies, att_in.at[i, near], att_in.at[i, 1 - near], w_att[i]) for i in range(n_att)]
    gathers = []
    for m in each:
        store_normed(x_ref[m].astype(F32), xg, (m, 0, 0))
        gathers.append(TokenGather(copies, xg, turned_rows, m))
    for chunk in att:
        chunk.advance()
    per_weight = n_mlp // 3
    order = [(w, j) for j in range(per_weight) for w in range(2)] + [(2, j) for j in range(per_weight)]
    mlp = [
        WeightGather(
            copies, mlp_in.at[w, near * per_weight + j], mlp_in.at[w, (1 - near) * per_weight + j], full
        )
        for (w, j), full in zip(order, w_mlp)
    ]
    for gather in gathers:
        gather.second()
    grad_own = [copies.inside(g_in.at[m], gg_out.at[m, 0, 0]) for m in each]
    grad_rows = [copies.remote(g_turned.at[m], gg_out.at[m, 0, 1], "blk", 1) for m in each]
    stages = len(replica_stages())
    steps = [[] for _ in range(stages + n_att)]
    for s in range(stages):
        for i in range(n_att):
            steps[s + i].append(att[i])
    for step in steps:
        for chunk in step:
            if chunk.stage <= stages:
                chunk.advance()

    background = [[] for _ in range(stages + n_mlp + 1)]
    for i, chunk in enumerate(mlp):
        for s in range(stages + 1):
            background[i + s].append(chunk)
    done = [0]

    def pump(count):
        for step in background[done[0] : done[0] + count]:
            for chunk in reversed(step):
                chunk.advance()
        done[0] += count

    for gather in gathers:
        gather.end()
    writes = [copies.inside(xg, xg_out)]
    loads = [copies.inside(w_att[i], w_in.at[i]) for i in range(3)] + [copies.inside(w_att[3], w_out)]
    crossing = [[] for _ in each]
    mine = [[] for _ in each]
    tile = min(256, heads_width)
    for i in range(3):
        loads[i].wait()
        for m in each:
            rows = xg[m].reshape(4 * tokens, width)
            for start in range(0, heads_width, tile):
                columns = w_in[i, :, :, :, start : start + tile].reshape(width, tile)
                product = matmul(rows, columns).astype(BF16)
                for lane in range(0, tile, min(here, tile)):
                    place = (start + lane) // here
                    inner = (start + lane) % here
                    for group in range(4):
                        made[m, place, i, group, :, inner : inner + min(here, tile)] = product[
                            group * tokens : (group + 1) * tokens, lane : lane + min(here, tile)
                        ]
            mine[m].append(copies.inside(made.at[m, upper, i], seq.at[m, upper, i]))
            for r in range(1, groups):
                crossing[m].append(
                    copies.remote(made.at[m, flipped("blk", 2 * r) // 2, i], seq.at[m, upper, i], "blk", 2 * r)
                )
    for m in each:
        grad_own[m].wait()
        grad_rows[m].wait_recv()
        grad_rows[m] = copies.remote(gg_out.at[m, 0], gg_out.at[m, 1], "head", 1)
    returning = []
    for m in each:
        pump(1)
        for copy in mine[m]:
            copy.wait()
        for copy in crossing[m]:
            copy.wait_recv()
        attend(seq, heads_out, m, cosine_ref, sine_ref, held)
        back = [copies.inside(heads_out.at[m, upper], attended.at[m, upper])]
        for r in range(1, groups):
            back.append(
                copies.remote(heads_out.at[m, flipped("blk", 2 * r) // 2], attended.at[m, upper], "blk", 2 * r)
            )
        returning.append(back)
    writes.append(copies.inside(seq, seq_out))
    pump(1)
    loads[3].wait()
    scatters = []
    rows_tile = min(256, width)
    for m in each:
        returning[m][0].wait()
        for copy in returning[m][1:]:
            copy.wait_recv()
        rows = jnp.concatenate([attended[m, g].reshape(4 * tokens, here) for g in range(groups)], 1)
        _, replicas, piece, _ = w_out.shape
        for start in range(0, width, rows_tile):
            half, first = start // (replicas * piece), start // piece % replicas
            part = w_out[half, first : first + rows_tile // piece].reshape(rows_tile, heads_width)
            product = matmul_nt(rows, part).astype(BF16)
            for group in range(4):
                partial[m, group // 2, group % 2, :, start : start + rows_tile] = product[
                    group * tokens : (group + 1) * tokens
                ]
        mixed[m] = x_ref[m].astype(F32)
        scatters.append(TokenScatter(copies, partial, leaving, came, passing, last, mixed, m))
    writes.append(copies.inside(attended, attended_out))
    pump(1)
    for scatter in scatters:
        scatter.second()
    pump(1)
    gathers = []
    for m in each:
        scatters[m].end()
        store_normed(mixed[m], x2, (m, 0, 0))
        gathers.append(TokenGather(copies, x2, turned_more, m))
    writes.append(copies.inside(mixed, mixed_out))
    pump(1)
    for gather in gathers:
        gather.second()
    pump(1)
    for gather in gathers:
        gather.end()
    writes.append(copies.inside(x2, x2_out))
    pump(len(background) - done[0])
    for copy in grad_rows:
        copy.wait_recv()
    for copy in writes:
        copy.wait()
    copies.finish()


def front(x_rows, grad_rows, grad_turned, att_in, mlp_in, tables):
    micros, tokens, width = x_rows.shape
    n_att, _, piece, heads_width = att_in.shape
    n_weights, parts, _, columns = mlp_in.shape
    n_mlp = n_weights * parts // 2
    groups = head_groups()
    here = heads_width // groups
    replicas = width // piece // 2
    length, lanes = tables[0].shape
    any_space = pl.BlockSpec(memory_space=pl.ANY)
    in_vmem = pl.BlockSpec(memory_space=pltpu.VMEM)

    def bf16(*shape):
        return jax.ShapeDtypeStruct(shape, BF16)

    token_rows = (micros, 2, 2, tokens, width)
    outs = [bf16(2, replicas, piece, heads_width)] * n_att + [bf16(2, replicas, piece, columns)] * n_mlp
    outs += [
        bf16(*token_rows),
        bf16(micros, groups, 3, 4, tokens, here),
        bf16(micros, groups, 4, tokens, here),
        jax.ShapeDtypeStruct((micros, tokens, width), F32),
        bf16(*token_rows),
        bf16(*token_rows),
    ]

    def room(*shape):
        return pltpu.VMEM(shape, BF16)

    scratch = [
        room(*token_rows),
        room(*token_rows),
        room(micros, 2, tokens, width),
        room(micros, 2, tokens, width),
        room(3, 2, replicas, piece, heads_width),
        room(2, replicas, piece, heads_width),
        room(micros, groups, 3, 4, tokens, here),
        room(micros, groups, 3, 4, tokens, here),
        room(micros, groups, 4, tokens, here),
        room(micros, groups, 4, tokens, here),
        room(*token_rows),
        room(micros, 2, tokens, width),
        room(micros, 2, tokens, width),
        room(micros, tokens, width),
        room(micros, tokens, width),
        pltpu.VMEM((micros, tokens, width), F32),
        room(length, lanes),
        room(length, lanes),
        room(length, lanes),
        pltpu.SemaphoreType.DMA((192,)),
        pltpu.SemaphoreType.DMA((192,)),
        pltpu.SemaphoreType.DMA((64,)),
    ]
    results = pl.pallas_call(
        functools.partial(front_kernel, (micros, groups, n_att, n_mlp)),
        out_shape=outs,
        in_specs=[in_vmem] + [any_space] * 4 + [in_vmem, in_vmem],
        out_specs=[any_space] * len(outs),
        scratch_shapes=scratch,
        compiler_params=pltpu.CompilerParams(
            collective_id=0, has_side_effects=True, vmem_limit_bytes=60 * 1024 * 1024
        ),
    )(x_rows, grad_rows, grad_turned, att_in, mlp_in, *tables)
    w_att, results = results[:n_att], results[n_att:]
    w_mlp, results = results[:n_mlp], results[n_mlp:]
    return w_att, [w.reshape(width, -1) for w in w_mlp], results


def absolute_block(place):
    stages = replica_stages()
    n_blk = lax.axis_size("blk")
    bits = [("blk", 1, place >> len(stages) & 1)] + [(a, bit, place >> s & 1) for s, (a, bit) in enumerate(stages)]
    block = 0
    for axis, bit, here in bits:
        digit = (lax.axis_index(axis) // bit) % 2
        block = block + bit * ((1 - digit) if here else digit) * (1 if axis == "blk" else n_blk)
    return block


def feature_lanes(place, piece):
    return pl.ds(pl.multiple_of(absolute_block(place) * piece, piece), piece)


def to_own_order(read, width, piece):
    return jnp.concatenate([read(feature_lanes(j, piece)) for j in range(width // piece)], 1)


def to_absolute_order(rows, target, at, piece):
    for j in range(rows.shape[1] // piece):
        target[at, :, feature_lanes(j, piece)] = rows[:, j * piece : (j + 1) * piece]


def part_of(block):
    n_blk = lax.axis_size("blk")
    head, blk = block // n_blk, block % n_blk
    mine = lax.axis_index("blk")
    near = (blk + mine) % 2
    return (blk // 2 + mine // 2) % 2, ((head + lax.axis_index("head")) % 2) * 2 + near


def load_pair_heads(seq, lane, cosine_ref, sine_ref, held):
    tokens = seq.shape[-2]
    lanes = held[0].shape[1]
    blocks = held[0].shape[0] // tokens

    def one(block, carry):
        part, group = part_of(block)
        rows = pl.ds(pl.multiple_of(block * tokens, tokens), tokens)
        for i in range(3):
            value = seq[i, part, group, :, pl.ds(lane, lanes)]
            if i < 2:
                value = turned(value.astype(F32), cosine_ref[rows, :], sine_ref[rows, :]).astype(BF16)
            held[i][rows, :] = value
        return carry

    lax.fori_loop(0, blocks, one, 0)


def attend_pair(seq, out, lane, cosine_ref, sine_ref, held):
    tokens = seq.shape[-2]
    q_s, k_s, v_s = held
    length, lanes = q_s.shape
    rows_at_once = min(256, length)
    load_pair_heads(seq, lane, cosine_ref, sine_ref, held)
    for first in range(0, length, rows_at_once):
        last = first + rows_at_once
        results = []
        for start in range(0, lanes, HD):
            head = slice(start, start + HD)
            weights, inverse = softmax_rows(q_s[first:last, head], k_s[:last, head], first)
            results.append(matmul(weights.astype(BF16), v_s[:last, head]) * inverse)
        result = jnp.concatenate(results, 1).astype(BF16)
        for offset in range(0, rows_at_once, tokens):
            part, group = part_of((first + offset) // tokens)
            out[part, group, :, pl.ds(lane, lanes)] = result[offset : offset + tokens]


def attend_pair_back(seq, grad, out, lane, cosine_ref, sine_ref, held, sums):
    tokens = seq.shape[-2]
    q_s, k_s, v_s = held
    dk_s, dv_s = sums
    length, lanes = q_s.shape
    rows_at_once = min(256, length)
    load_pair_heads(seq, lane, cosine_ref, sine_ref, held)
    dk_s[...] = jnp.zeros_like(dk_s)
    dv_s[...] = jnp.zeros_like(dv_s)
    for first in range(0, length, rows_at_once):
        last = first + rows_at_once
        places = [part_of((first + offset) // tokens) for offset in range(0, rows_at_once, tokens)]
        grad_rows = jnp.concatenate([grad[p, g, :, pl.ds(lane, lanes)] for p, g in places], 0)
        query_parts, key_parts, value_parts = [], [], []
        for start in range(0, lanes, HD):
            head = slice(start, start + HD)
            query, keys, grad_part = q_s[first:last, head], k_s[:last, head], grad_rows[:, head]
            weights, inverse = softmax_rows(query, keys, first)
            probabilities = weights * inverse
            grad_prob = matmul_nt(grad_part, v_s[:last, head])
            row_delta = jnp.sum(probabilities * grad_prob, 1, keepdims=True)
            grad_scores = (probabilities * (grad_prob - row_delta) * HD ** (-0.5)).astype(BF16)
            query_parts.append(matmul(grad_scores, keys))
            key_parts.append(matmul_tn(grad_scores, query))
            value_parts.append(matmul_tn(probabilities.astype(BF16), grad_part))
        grad_query = jnp.concatenate(query_parts, 1)
        grad_query = turned(grad_query, cosine_ref[first:last, :], -sine_ref[first:last, :]).astype(BF16)
        for i, (p, g) in enumerate(places):
            out[0, p * 4 + g, :, pl.ds(lane, lanes)] = grad_query[i * tokens : (i + 1) * tokens]
        dk_s[:last, :] += jnp.concatenate(key_parts, 1)
        dv_s[:last, :] += jnp.concatenate(value_parts, 1)

    def one(block, carry):
        p, g = part_of(block)
        rows = pl.ds(pl.multiple_of(block * tokens, tokens), tokens)
        grad_key = turned(dk_s[rows, :], cosine_ref[rows, :], -sine_ref[rows, :])
        out[1, p * 4 + g, :, pl.ds(lane, lanes)] = grad_key.astype(BF16)
        out[2, p * 4 + g, :, pl.ds(lane, lanes)] = dv_s[rows, :].astype(BF16)
        return carry

    lax.fori_loop(0, length // tokens, one, 0)


def greet_pairs():
    masks = [("head", 1)] + [(axis, bit) for axis in ("blk", "dp") for bit in bits_of(lax.axis_size(axis))]
    barrier = pltpu.get_barrier_semaphore()
    for axis, mask in masks:
        pl.semaphore_signal(barrier, inc=1, device_id={axis: flipped(axis, mask)}, device_id_type=MESH)
    pl.semaphore_wait(barrier, len(masks))


def up_to(chunk, stage):
    while chunk.stage < stage:
        chunk.advance()


def store_product(product, target, part, columns):
    tokens = target.shape[-2]
    for group in range(4):
        target[part, group // 2, group % 2, :, columns] = product[group * tokens : (group + 1) * tokens]


def pair_front_kernel(sizes, *refs):
    n_att, n_mlp = sizes
    x_in, g_in, att_in, mlp_in, cosine_ref, sine_ref = refs[:6]
    refs = refs[6:]
    w_att, refs = refs[:n_att], refs[n_att:]
    (w_gu, w_down, grads_out, hidden_out), refs = refs[:4], refs[4:]
    xg_out, seq_out, attended_out, mixed_out, x2_out, gg_out, x_out, g_out = refs[:8]
    (x_raw, g_raw, x_own, g_own, g_turned, xg, x2, turned_rows, turned_more, w_in, w_out, seq, attended, partial,
     leaving, came, passing, last, mixed, slopes, activated, q_s, k_s, v_s, send, recv, local) = refs[8:]
    held = (q_s, k_s, v_s)
    near = lax.axis_index("blk") % 2
    upper = lax.axis_index("blk") // 2
    tokens, width = x_own.shape[-2:]
    heads_width = w_in.shape[-1]
    count = 4 * tokens
    piece = w_in.shape[-2]
    copies = Copies(send, recv, local)
    stages = len(replica_stages())

    loads = [copies.inside(x_in.at[upper, 0], x_raw.at[0]), copies.inside(g_in.at[upper, 0], g_raw.at[0])]
    greet_pairs()
    trade = copies.remote(x_in.at[1 - upper, 0], x_raw.at[1], "blk", 2)

    def att_chunk(i):
        return lambda: WeightGather(copies, att_in.at[i, near], att_in.at[i, 1 - near], w_att[i])

    def mlp_chunk(i):
        per_weight = n_mlp // 3
        w, j = (i % 2, i // 2) if i < 2 * per_weight else (2, i - 2 * per_weight)
        size = mlp_in.shape[-1]
        if w < 2:
            full = w_gu.at[:, :, :, i * size : (i + 1) * size]
        else:
            full = w_down.at[:, :, :, j * size : (j + 1) * size]
        own, other = near * per_weight + j, (1 - near) * per_weight + j
        return lambda: WeightGather(copies, mlp_in.at[w, own], mlp_in.at[w, other], full)

    makers = [att_chunk(i) for i in range(n_att)] + [mlp_chunk(i) for i in range(n_mlp)]
    chunks = []

    def reach(k, stage):
        if 0 <= k < len(makers):
            while len(chunks) <= k:
                chunks.append(makers[len(chunks)]())
            up_to(chunks[k], stage)

    def step(k):
        reach(k - 2, stages + 1)
        reach(k - 1, 3)
        reach(k, 2)
        reach(k + ahead[0], 1)
        reach(k + 3, 0)

    ahead = [1]

    reach(n_att - 1, 0)
    reach(0, 1)

    def own_rows(p):
        x_own[p] = to_own_order(lambda lanes: x_raw[p, :, lanes], width, piece)
        store_normed(x_own[p].astype(F32), xg, (p, 0, 0))
        return TokenGather(copies, xg, turned_rows, p, False)

    loads[0].wait()
    gathers = [own_rows(0)]
    step(0)
    gathers[0].second()
    step(1)
    trade.wait_recv()
    gathers.append(own_rows(1))
    step(2)
    w_loads = []

    def load_weight(i):
        reach(i, stages + 1)
        w_loads.append(copies.inside(w_att[i], w_in.at[i] if i < 3 else w_out))

    def project(i, p):
        rows = xg[p].reshape(count, width)
        for start in range(0, heads_width, 256):
            columns = w_in[i, :, :, :, start : start + 256].reshape(width, 256)
            product = matmul(rows, columns).astype(BF16)
            for group in range(4):
                seq[i, p, group, :, start : start + 256] = product[group * tokens : (group + 1) * tokens]

    gathers[1].second()
    step(3)
    trade = copies.remote(g_in.at[1 - upper, 0], g_raw.at[1], "blk", 2)
    loads[1].wait()
    for i in range(3):
        load_weight(i)
    gathers[0].end()
    for i in range(3):
        w_loads[i].wait()
        project(i, 0)
    gathers[1].end()
    for i in range(3):
        project(i, 1)
    store_xg = copies.inside(xg, xg_out)
    writes = [copies.inside(seq, seq_out), copies.inside(x_own, x_out)]
    first_gathers = gathers
    trade.wait_recv()
    ahead[0] = 2
    reach(5, 1)
    grad_rows = []
    for p in range(2):
        g_own[p] = to_own_order(lambda lanes, p=p: g_raw[p, :, lanes], width, piece)
        g_turned[p] = halves_turned(g_own[p])
        mine = copies.inside(g_own.at[p], gg_out.at[p, 0, 0])
        grad_rows.append((mine, copies.remote(g_turned.at[p], gg_out.at[p, 0, 1], "blk", 1)))
    writes.append(copies.inside(g_own, g_out))
    lanes = q_s.shape[1]
    for at, lane in enumerate(range(0, heads_width, lanes)):
        attend_pair(seq, attended, lane, cosine_ref, sine_ref, held)
        if at == 1:
            step(4)
    load_weight(3)
    w_loads[3].wait()
    scatters = []
    for p in range(2):
        rows = attended[p].reshape(count, heads_width)
        for start in range(0, width, 256):
            half, first = start // (width // 2), start // piece % (width // piece // 2)
            part = w_out[half, first : first + 256 // piece].reshape(256, heads_width)
            store_product(matmul_nt(rows, part).astype(BF16), partial, p, slice(start, start + 256))
        mixed[p] = x_own[p].astype(F32)
        scatters.append(TokenScatter(copies, partial, leaving, came, passing, last, mixed, p))
    writes.append(copies.inside(attended, attended_out))
    step(5)
    for scatter in scatters:
        scatter.second()
    far = []
    for p, (mine, turned_copy) in enumerate(grad_rows):
        mine.wait()
        turned_copy.wait_recv()
        far.append(copies.remote(gg_out.at[p, 0], gg_out.at[p, 1], "head", 1))
    gathers = []
    for p in range(2):
        scatters[p].end()
        store_normed(mixed[p], x2, (p, 0, 0))
        gathers.append(TokenGather(copies, x2, turned_more, p))
    writes.append(copies.inside(mixed, mixed_out))
    step(6)
    for gather in gathers:
        gather.second()
    step(7)
    for gather in gathers:
        gather.end()
    writes.append(copies.inside(x2, x2_out))
    store_xg.wait()
    for gather in first_gathers:
        gather.release()
    for scatter in scatters:
        scatter.release()
    for copy in far:
        copy.wait_recv()
    load_rows = [copies.inside(gg_out, xg)]
    hidden = partial
    quarters = range(0, 2 * heads_width, heads_width)
    size = 2 * heads_width

    def tiles(body):
        def one(i, carry):
            body(i // 2, i % 2)
            return carry

        lax.fori_loop(0, 4, one, 0)

    def forward(j):
        for lane in quarters:
            sources = [w_gu.at[:, :, :, (2 * j + w) * size + lane : (2 * j + w) * size + lane + heads_width] for w in (0, 1)]
            loads = [copies.inside(source, w_in.at[w]) for w, source in enumerate(sources)]
            for load in loads:
                load.wait()
            lanes = slice(j * size + lane, j * size + lane + heads_width)

            def body(p, head, lanes=lanes):
                rows = x2[p, head].reshape(2 * tokens, width)
                gate = matmul(rows, w_in[0].reshape(width, heads_width))
                up = matmul(rows, w_in[1].reshape(width, heads_width))
                sigmoid = jax.nn.sigmoid(gate)
                active = gate * sigmoid
                slope = up * sigmoid * (1.0 + gate * (1.0 - sigmoid))
                shape = (2, tokens, heads_width)
                slopes[p, head, :, :, lanes] = slope.astype(BF16).reshape(shape)
                activated[p, head, :, :, lanes] = active.astype(BF16).reshape(shape)
                hidden[p, head, :, :, lanes] = (active * up).astype(BF16).reshape(shape)

            tiles(body)
        here = slice(j * size, (j + 1) * size)
        writes.append(copies.inside(hidden.at[:, :, :, :, here], hidden_out.at[:, :, :, :, here]))

    def backward(j):
        for lane in quarters:
            lanes = slice(j * size + lane, j * size + lane + heads_width)
            copies.inside(w_down.at[:, :, :, lanes], w_in.at[2]).wait()

            def body(p, head, lanes=lanes):
                rows = xg[p, head].reshape(2 * tokens, width)
                grad_hidden = matmul(rows, w_in[2].reshape(width, heads_width)).reshape(2, tokens, heads_width)
                slopes[p, head, :, :, lanes] = (grad_hidden * slopes[p, head, :, :, lanes].astype(F32)).astype(BF16)
                activated[p, head, :, :, lanes] = (
                    grad_hidden * activated[p, head, :, :, lanes].astype(F32)
                ).astype(BF16)

            tiles(body)
        here = slice(j * size, (j + 1) * size)
        for w, made in enumerate((slopes, activated)):
            there = slice((2 * j + w) * size, (2 * j + w + 1) * size)
            writes.append(copies.inside(made.at[:, :, :, :, here], grads_out.at[:, :, :, :, there]))

    reach(n_att + 1, stages + 1)
    forward(0)
    step(8)
    reach(n_att + 3, stages + 1)
    forward(1)
    for load in load_rows:
        load.wait()
    step(9)
    reach(n_att + 4, stages + 1)
    backward(0)
    step(10)
    step(11)
    backward(1)
    for copy in writes:
        copy.wait()
    copies.finish()


def pair_front(block_input, grad_output, att_in, mlp_in, tables):
    _, _, tokens, width = block_input.shape
    n_att, _, piece, heads_width = att_in.shape
    n_weights, parts, _, columns = mlp_in.shape
    n_mlp = n_weights * parts // 2
    replicas = width // piece // 2
    length, lanes = tables[0].shape
    any_space = pl.BlockSpec(memory_space=pl.ANY)
    in_vmem = pl.BlockSpec(memory_space=pltpu.VMEM)

    def bf16(*shape):
        return jax.ShapeDtypeStruct(shape, BF16)

    def room(*shape):
        return pltpu.VMEM(shape, BF16)

    token_rows = (2, 2, 2, tokens, width)
    outs = [bf16(2, replicas, piece, heads_width)] * n_att
    hidden_width = n_mlp // 3 * columns
    outs += [bf16(2, replicas, piece, 2 * hidden_width), bf16(2, replicas, piece, hidden_width)]
    outs += [bf16(2, 2, 2, tokens, 2 * hidden_width), bf16(2, 2, 2, tokens, hidden_width)]
    outs += [
        bf16(*token_rows),
        bf16(3, 2, 4, tokens, heads_width),
        bf16(2, 4, tokens, heads_width),
        jax.ShapeDtypeStruct((2, tokens, width), F32),
        bf16(*token_rows),
        bf16(*token_rows),
        bf16(2, tokens, width),
        bf16(2, tokens, width),
    ]
    own, pair = (2, tokens, width), (2, 2, tokens, width)
    scratch = [room(*shape) for shape in [own] * 5 + [token_rows] * 2 + [pair] * 2]
    scratch += [
        room(3, 2, replicas, piece, heads_width),
        room(2, replicas, piece, heads_width),
        room(3, 2, 4, tokens, heads_width),
        room(2, 4, tokens, heads_width),
        room(*token_rows),
        room(*pair),
        room(*pair),
        room(*own),
        room(*own),
        pltpu.VMEM(own, F32),
        room(2, 2, 2, tokens, hidden_width),
        room(2, 2, 2, tokens, hidden_width),
        *[room(length, lanes)] * 3,
        pltpu.SemaphoreType.DMA((96,)),
        pltpu.SemaphoreType.DMA((96,)),
        pltpu.SemaphoreType.DMA((64,)),
    ]
    results = pl.pallas_call(
        functools.partial(pair_front_kernel, (n_att, n_mlp)),
        out_shape=outs,
        in_specs=[any_space] * 4 + [in_vmem] * 2,
        out_specs=[any_space] * len(outs),
        scratch_shapes=scratch,
        compiler_params=pltpu.CompilerParams(
            collective_id=2, has_side_effects=True, vmem_limit_bytes=63 * 1024 * 1024
        ),
    )(block_input, grad_output, att_in, mlp_in, *tables)
    w_att, results = results[:n_att], results[n_att:]
    return w_att, results[:2], results[2:4], results[4:]


class GradHalving:
    def __init__(self, copies, kept, first_copy, landed, room, final, own, other):
        self.copies, self.kept, self.copy, self.landed = copies, kept, first_copy, landed
        self.room, self.final, self.own, self.other = room, final, own, other
        self.stages = replica_stages()[::-1]
        self.stage, self.state = 0, "sent"

    def reach(self, stage, state):
        order = ("sent", "here", "added")
        while (self.stage, order.index(self.state)) < (stage, order.index(state)):
            if self.state == "sent":
                self.copy.wait_recv()
                self.state = "here"
            elif self.state == "here":
                self.add()
                self.state = "added"
            else:
                self.stage += 1
                self.send()
                self.state = "sent"

    def send(self):
        copies, kept, stage = self.copies, self.kept, self.stage
        if stage == len(self.stages):
            self.copy = copies.remote(kept.at[1, 0], self.other, "blk", 1)
            return
        count = kept.shape[1] >> (stage - 1)
        self.copy = copies.remote(
            kept.at[:, count // 2 : count], self.landed[stage], *self.stages[stage]
        )

    def add(self):
        copies, kept, stage = self.copies, self.kept, self.stage
        if stage == len(self.stages):
            return
        count = kept.shape[1] >> stage
        columns = kept.shape[-1]
        mine, came = (part.at[:, 0:count, :, 0:columns] for part in self.room)
        loads = [copies.inside(kept.at[:, 0:count], mine), copies.inside(self.landed[stage], came)]
        for load in loads:
            load.wait()
        if stage == len(self.stages) - 1:
            self.final[:, 0:columns] = mine[0, 0].astype(F32) + came[0, 0].astype(F32)
            mine[1, 0] = (mine[1, 0].astype(F32) + came[1, 0].astype(F32)).astype(BF16)
            stores = [
                copies.inside(self.final.at[:, 0:columns], self.own),
                copies.inside(mine.at[1, 0], kept.at[1, 0]),
            ]
            for store in stores:
                store.wait()
            return

        def one(i, carry):
            half, row = i // count, i % count
            mine[half, row] = (mine[half, row].astype(F32) + came[half, row].astype(F32)).astype(BF16)
            return carry

        lax.fori_loop(0, 2 * count, one, 0)
        copies.inside(mine, kept.at[:, 0:count]).wait()


def pair_back_kernel(sizes, *refs):
    n_mlp, n_att = sizes
    stages = len(replica_stages())

    def take(number):
        nonlocal refs
        taken, refs = refs[:number], refs[number:]
        return taken

    e_in, produced_in, mixed_in, x2_in, gg_in, xg_in, attended_in, seq_in = take(8)
    g_ref, x_ref, cosine_ref, sine_ref = take(4)
    (grads_in, hidden_in), w_att = take(2), take(n_att)
    own_mlp, other_mlp, own_att, other_att = take(n_mlp), take(n_mlp), take(n_att), take(n_att)
    output_out, input_out = take(2)
    kept_mlp, kept_att = take(n_mlp), take(n_att)
    landed_mlp = [take(stages) for _ in range(n_mlp)]
    landed_att = [take(stages) for _ in range(n_att)]
    (partial, leaving, came, passing, last, came_o, last_o, came_c, last_c, total, total_c, rows_g,
     turned_g, leaves, room_a, room_b, final, grad_heads, rows_b, rows_o,
     acts, weights, seq, ready, q_s, k_s, v_s, dk_s, dv_s, send, recv, local) = refs
    parts = range(2)
    upper = lax.axis_index("blk") // 2
    tokens, width = x_ref.shape[-2:]
    heads_width = rows_o.shape[-1]
    _, kept_pieces, piece, _ = kept_mlp[0].shape
    copies = Copies(send, recv, local)
    count = 4 * tokens
    tile = 256

    load_e = copies.inside(e_in, partial)
    load_mixed = copies.inside(mixed_in, total_c)
    acts_load = copies.inside(x2_in, acts)
    greet_pairs()
    load_e.wait()
    for p in parts:
        total[p] = jnp.zeros_like(total[p])
    scatters = [TokenScatter(copies, partial, leaving, came, passing, last, total, p) for p in parts]

    busy = []

    def weight_grad(acts, grads, kept, landed, own, other):
        part_columns = grads[0].shape[-1]
        columns = part_columns * len(grads)
        for copy in busy:
            copies.wait_sent(copy)
        busy.clear()
        per_half = kept_pieces * piece // tile
        pieces = tile // piece
        for side in (1, 0):
            side_room = leaves if side else room_a

            def one(i, carry, side=side, side_room=side_room):
                low, part = i // per_half, i % per_half
                start = low * (2 * kept_pieces * piece) + side * (kept_pieces * piece) + part * tile
                lanes = pl.ds(pl.multiple_of(start, tile), tile)
                left = acts[:, :, :, :, lanes].reshape(2 * count, tile)
                for j, right in enumerate(grads):
                    product = matmul_tn(left, right[...].reshape(2 * count, part_columns)).astype(BF16)
                    columns_here = slice(j * part_columns, (j + 1) * part_columns)
                    side_room[low, pl.ds(part * pieces, pieces), :, columns_here] = product.reshape(
                        pieces, piece, part_columns
                    )
                return carry

            lax.fori_loop(0, 2 * per_half, one, 0)
            source = side_room.at[:, :, :, 0:columns]
            if side:
                first = copies.remote(source, landed[0], *replica_stages()[-1])
                busy.append(first)
            else:
                copies.inside(source, kept).wait()
        chunks.append(GradHalving(copies, kept, first, landed, (room_a, room_b), final, own, other))

    chunks = []

    def reach(k, stage, state):
        if 0 <= k < len(chunks):
            chunks[k].reach(stage, state)

    done = [0]

    def step():
        k = done[0]
        done[0] += 1
        reach(k + 1, 1, "sent")
        reach(k, 2, "sent")
        reach(k - 1, 3, "sent")
        reach(k - 2, 3, "here")

    def load_grads(k):
        loads = []
        for half_of in range(2):
            for row in range(2 * kept_pieces):
                source = grads_in if k < 2 * n_mlp // 3 else hidden_in
                first = k % (2 * n_mlp // 3) * 2 * heads_width + half_of * heads_width
                source = source.at[row // 4, row // 2 % 2, row % 2, :, first : first + heads_width]
                loads.append(copies.inside(source, weights.at[k % 2, half_of, row]))
        return loads

    slots = [load_grads(0)]

    def mlp_chunk(k):
        for load in slots[k]:
            load.wait()
        if k + 1 < n_mlp:
            slots.append(load_grads(k + 1))
        halves = [weights.at[k % 2, half_of] for half_of in range(2)]
        weight_grad(acts, halves, kept_mlp[k], landed_mlp[k], own_mlp[k], other_mlp[k])

    acts_load.wait()
    mlp_chunk(0)
    mlp_chunk(1)
    reach(0, 1, "sent")
    for scatter in scatters:
        scatter.second()
    load_mixed.wait()
    mlp_chunk(2)
    gathers = []
    for p in parts:
        scatters[p].end()
        scatters[p].release()
        mixed = total_c[p]
        scale = lax.rsqrt(jnp.mean(mixed * mixed, -1, keepdims=True) + EPSILON)
        total[p] = g_ref[p].astype(F32) + norm_back(total[p], mixed, scale)
        rows_g[p, 0, 0] = total[p].astype(BF16)
        gathers.append(TokenGather(copies, rows_g, turned_g, p))
    load_produced = copies.inside(produced_in, partial)
    step()
    mlp_chunk(3)
    acts_load = copies.inside(gg_in, acts)
    for gather in gathers:
        gather.second()
    acts_load.wait()
    mlp_chunk(4)
    step()
    mlp_chunk(5)
    w_loads = [copies.inside(w_att[i], weights.at[slot]) for i, slot in ((3, 0), (0, 1), (1, 2))]
    load_seq = copies.inside(seq_in, seq)
    load_rows_o = [copies.inside(attended_in.at[p], rows_o.at[4 * p : 4 * p + 4]) for p in parts]
    for gather in gathers:
        gather.end()
    load_produced.wait()
    scatters = [TokenScatter(copies, partial, leaving, came_o, passing, last_o, total_c, p, True) for p in parts]
    w_loads[0].wait()
    for p in parts:
        rows = rows_g[p].reshape(count, width)
        product = matmul(rows, weights[0].reshape(width, heads_width)).astype(BF16)
        for group in range(4):
            grad_heads[p, group] = product[group * tokens : (group + 1) * tokens]
    w_loads.append(copies.inside(w_att[2], weights.at[0]))
    for load in load_rows_o:
        load.wait()
    weight_grad(rows_g, [rows_o], kept_att[3], landed_att[3], own_att[3], other_att[3])
    step()
    load_seq.wait()
    lanes = cosine_ref.shape[1]
    for at, lane in enumerate(range(0, heads_width, lanes)):
        attend_pair_back(seq, grad_heads, rows_b, lane, cosine_ref, sine_ref, (q_s, k_s, v_s), (dk_s, dv_s))
        if at == 0:
            for scatter in scatters:
                scatter.second()
        step()
    trades = []
    for p in parts:
        scatters[p].end()
        scatters[p].release()
        to_absolute_order(total_c[p].astype(BF16), ready, p, piece)
    stores = [copies.inside(ready.at[0], output_out.at[upper])]
    trades.append(copies.remote(ready.at[1], output_out.at[upper], "blk", 2))
    acts_load = copies.inside(xg_in, acts)
    for load in w_loads[1:]:
        load.wait()
    scatters = []
    for p in parts:
        pieces = tile // piece
        for start in range(0, width, tile):
            low, first = start // (2 * kept_pieces * piece), start // piece % (2 * kept_pieces)
            terms = []
            for i in range(3):
                weight = weights[(i + 1) % 3, low, first : first + pieces].reshape(tile, heads_width)
                terms.append(matmul_nt(rows_b[i, 4 * p : 4 * p + 4].reshape(count, heads_width), weight))
            product = functools.reduce(jnp.add, terms).astype(BF16)
            store_product(product, partial, p, slice(start, start + tile))
        total_c[p] = jnp.zeros_like(total_c[p])
        scatters.append(TokenScatter(copies, partial, leaving, came_c, passing, last_c, total_c, p))
    acts_load.wait()
    for i in range(3):
        weight_grad(acts, [rows_b.at[i]], kept_att[i], landed_att[i], own_att[i], other_att[i])
    step()
    for scatter in scatters:
        scatter.second()
    step()
    for store in stores:
        store.wait()
    copies.wait_sent(trades[0])
    for p in parts:
        scatters[p].end()
        scatters[p].release()
        values = x_ref[p].astype(F32)
        scale = lax.rsqrt(jnp.mean(values * values, -1, keepdims=True) + EPSILON)
        rows = (total[p] + norm_back(total_c[p], values, scale)).astype(BF16)
        to_absolute_order(rows, ready, p, piece)
    store = copies.inside(ready.at[0], input_out.at[upper])
    trades.append(copies.remote(ready.at[1], input_out.at[upper], "blk", 2))
    while done[0] < len(chunks) + 2:
        step()
    store.wait()
    for trade in trades:
        trade.wait_recv()
    copies.finish()


def pair_back(partial, produced, held, tables, grads, w_att):
    normed_one, sequences, attended, mixed, normed_two, grad_rows, x_rows, g_rows = held
    _, tokens, width = x_rows.shape
    _, replicas, piece, heads_width = w_att[0].shape
    columns = 2 * heads_width
    n_mlp, n_att = sum(g.shape[-1] for g in grads) // columns, len(w_att)
    stages = len(replica_stages())
    any_space = pl.BlockSpec(memory_space=pl.ANY)
    in_vmem = pl.BlockSpec(memory_space=pltpu.VMEM)

    def bf16(*shape):
        return jax.ShapeDtypeStruct(shape, BF16)

    def f32(*shape):
        return jax.ShapeDtypeStruct(shape, F32)

    def room(*shape):
        return pltpu.VMEM(shape, BF16)

    widths = [columns] * n_mlp + [heads_width] * n_att
    outs = [f32(piece, columns)] * n_mlp + [bf16(piece, columns)] * n_mlp
    outs += [f32(piece, heads_width)] * n_att + [bf16(piece, heads_width)] * n_att
    outs += [bf16(2, tokens, width)] * 2
    outs += [bf16(2, replicas // 2, piece, w) for w in widths]
    outs += [bf16(2, replicas >> (s + 1), piece, w) for w in widths for s in range(stages)]
    token_rows, own, pair = (2, 2, 2, tokens, width), (2, tokens, width), (2, 2, tokens, width)
    widest = max(columns, heads_width)
    half_room = (2, replicas // 2, piece, widest)
    scratch = [
        room(*token_rows),
        room(*pair),
        room(*pair),
        room(*own),
        room(*own),
        room(*pair),
        room(*own),
        room(*pair),
        room(*own),
        pltpu.VMEM(own, F32),
        pltpu.VMEM(own, F32),
        room(*token_rows),
        room(*pair),
        room(*half_room),
        room(*half_room),
        room(*half_room),
        pltpu.VMEM((piece, widest), F32),
        room(2, 4, tokens, heads_width),
        room(3, 8, tokens, heads_width),
        room(8, tokens, heads_width),
        room(*token_rows),
        room(3, 2, replicas, piece, heads_width),
        room(3, 2, 4, tokens, heads_width),
        room(*own),
        *[room(*tables[0].shape)] * 3,
        *[pltpu.VMEM(tables[0].shape, F32)] * 2,
        pltpu.SemaphoreType.DMA((96,)),
        pltpu.SemaphoreType.DMA((96,)),
        pltpu.SemaphoreType.DMA((384,)),
    ]
    results = pl.pallas_call(
        functools.partial(pair_back_kernel, (n_mlp, n_att)),
        out_shape=outs,
        in_specs=[any_space] * 8 + [in_vmem] * 4 + [any_space] * (2 + n_att),
        out_specs=[any_space] * len(outs),
        scratch_shapes=scratch,
        compiler_params=pltpu.CompilerParams(
            collective_id=3, has_side_effects=True, vmem_limit_bytes=63 * 1024 * 1024
        ),
    )(
        partial, produced, mixed, normed_two, grad_rows, normed_one, attended, sequences, g_rows, x_rows,
        *tables, *grads, *w_att,
    )
    own_mlp, results = results[:n_mlp], results[n_mlp:]
    other_mlp, results = results[:n_mlp], results[n_mlp:]
    own_att, results = results[:n_att], results[n_att:]
    other_att, results = results[:n_att], results[n_att:]
    return list(zip(own_mlp, other_mlp)), list(zip(own_att, other_att)), results[0], results[1]


def scale_of(values):
    return lax.rsqrt(jnp.mean(values * values, -1, keepdims=True) + EPSILON)


def norm_back(grad, values, scale):
    return scale * grad - values * (scale * scale * scale) * jnp.mean(grad * values, -1, keepdims=True)


def on_device(
    block_input,
    attention_gain,
    query_weight,
    key_weight,
    value_weight,
    output_weight,
    mlp_gain,
    gate_weight,
    up_weight,
    down_weight,
    grad_output,
):
    micros, _, tokens, width = block_input.shape
    heads_width = query_weight.shape[1] // 2
    length = tokens * lax.axis_size("blk") * lax.axis_size("head")
    to_own, to_absolute = feature_order()
    order = block_order()
    tables = rope_tables(length, min(LANES, heads_width // head_groups()))
    each = range(micros)
    head_first = [m % 2 == 1 for m in each]

    gain_one = attention_gain.astype(F32)[:, None]
    gain_two = mlp_gain.astype(F32)[:, None]

    def scaled(weight, gain):
        return (weight.astype(F32) * gain).astype(BF16)

    def joined(parts):
        return jnp.concatenate(parts, 0)

    def columns_of(weight, parts):
        rows, columns = weight.shape
        return weight.reshape(rows, parts, columns // parts).swapaxes(0, 1)

    att_in = jnp.stack(
        [columns_of(scaled(w, gain_one), 2) for w in (query_weight, key_weight, value_weight)]
        + [columns_of(output_weight.T, 2)]
    )
    mlp_in = jnp.stack(
        [columns_of(scaled(w, gain_two), 4) for w in (gate_weight, up_weight)] + [columns_of(down_weight.T, 4)]
    )
    paired = micros == 2 and lax.axis_size("blk") == 4 and heads_width % LANES == 0 and 8 * tokens == width // 2
    paired = paired and mlp_in.shape[-1] == 2 * heads_width == width // 2 and mlp_in.shape[-2] == tokens
    hidden, grad_gate, grad_up = [], [], []
    grad_normed = produced = 0.0
    if paired:
        w_att, w_mlp, made, held = pair_front(block_input, grad_output, att_in, mlp_in, tables)
        grad_normed, produced = (
            matmul_nt(rows.reshape(-1, rows.shape[-1]), weight.reshape(width, -1)) for rows, weight in zip(made, w_mlp)
        )
    else:
        block_rows = [array.reshape(micros * tokens, width) for array in (block_input, grad_output)]
        inputs_low, grad_low = (rows.reshape(micros, tokens, width) for rows in reorder(to_own, *block_rows))
        grad_turned = turn_features(grad_low.reshape(micros * tokens, width)).reshape(micros, tokens, width)
        w_att, w_mlp, held = front(inputs_low, grad_low, grad_turned, att_in, mlp_in, tables)
        normed_one, sequences, attended, mixed, normed_two, grad_rows = held
        normed_two_all = normed_two.reshape(-1, width)
        grad_rows_all = grad_rows.reshape(-1, width)
        for gate_full, up_full, down_full in zip(w_mlp[0:4:2], w_mlp[1:4:2], w_mlp[4:]):
            gate = matmul(normed_two_all, gate_full)
            up = matmul(normed_two_all, up_full)
            sigmoid = jax.nn.sigmoid(gate)
            activated = gate * sigmoid
            hidden.append((activated * up).astype(BF16))
            grad_hidden = matmul(grad_rows_all, down_full)
            grad_gate.append((grad_hidden * up * sigmoid * (1.0 + gate * (1.0 - sigmoid))).astype(BF16))
            grad_up.append((grad_hidden * activated).astype(BF16))
            grad_normed += matmul_nt(grad_gate[-1], gate_full) + matmul_nt(grad_up[-1], up_full)
            produced += matmul_nt(hidden[-1], down_full)

    def split(rows):
        size = rows.shape[0] // micros
        return [rows[m * size : (m + 1) * size] for m in each]

    if paired:
        partials = [rows.astype(BF16).reshape(held[4].shape) for rows in (grad_normed, produced)]
        mlp_pairs, att_pairs, block_output, input_grad = pair_back(*partials, held, tables, made, w_att)

        def beside(pairs):
            return tuple(jnp.concatenate(side, 1) for side in zip(*pairs))

        gate_grad, up_grad, down_grad = beside(mlp_pairs[0:4:2]), beside(mlp_pairs[1:4:2]), beside(mlp_pairs[4:])
        output_grad = att_pairs[3]
        qkv_grads = [side_by_side(*pair) for pair in att_pairs[:3]]
    else:
        produced = split(produced)
        outputs = [(mixed[m] + scatter_tokens(produced[m], head_first[m])).astype(BF16) for m in each]
        upper = lax.axis_index("blk") // 2
        w_att = [w.reshape(width, -1) for w in w_att]
        normed_one_all = normed_one.reshape(-1, width)
        sequences = [lax.dynamic_index_in_dim(sequences, upper ^ r, 1, keepdims=False) for r in range(head_groups())]
        sequences = jnp.concatenate(sequences, 2)
        attended = jnp.concatenate([attended[:, g] for g in range(head_groups())], -1)
        attended_all = attended.reshape(micros * 4 * tokens, -1)
        grad_normed = split(grad_normed)
        grad_mixed = []
        for m in each:
            back_rows = norm_back(scatter_tokens(grad_normed[m], head_first[m]), mixed[m], scale_of(mixed[m]))
            grad_mixed.append(grad_low[m].astype(F32) + back_rows)
        gate_grad = scatter_weight_grad(normed_two_all, jnp.concatenate(grad_gate, 1))
        up_grad = scatter_weight_grad(normed_two_all, jnp.concatenate(grad_up, 1))
        down_grad = scatter_weight_grad(grad_rows_all, jnp.concatenate(hidden, 1))
        grad_mixed_rows = [gather_tokens(grad_mixed[m].astype(BF16), head_first[m]) for m in each]
        grad_qkv, input_grads = [], []
        for m in each:
            grad_attended = matmul(grad_mixed_rows[m], w_att[3]).astype(BF16)
            grad_sequences = attention_call(order, sequences[m], tables, to_sequences([grad_attended])[0])
            returned = from_sequences(grad_sequences)
            grad_qkv.append(jnp.concatenate([returned[0], returned[1], returned[2]], 1))
            terms = [matmul_nt(returned[i], w_att[i]) for i in range(3)]
            grad_normed_one = scatter_tokens(functools.reduce(jnp.add, terms), head_first[m])
            inputs = inputs_low[m].astype(F32)
            back_rows = norm_back(grad_normed_one, inputs, scale_of(inputs))
            input_grads.append((grad_mixed[m] + back_rows).astype(BF16))
        output_grad = scatter_weight_grad(joined(grad_mixed_rows), attended_all)
        qkv_grad = scatter_weight_grad(normed_one_all, joined(grad_qkv))
        qkv_grads = [
            side_by_side(*(side[:, i * heads_width : (i + 1) * heads_width] for side in qkv_grad)) for i in range(3)
        ]
        block_output, input_grad = reorder(to_absolute, joined(outputs), joined(input_grads))
    mlp_grads = [side_by_side(*gate_grad), side_by_side(*up_grad)]

    def gain_grad(weights, grads):
        terms = [jnp.sum(w.astype(F32) * g, 1) for w, g in zip(weights, grads)]
        here = functools.reduce(jnp.add, terms)
        return here + swap(here, "head", 1)

    attention_gain_grad = gain_grad((query_weight, key_weight, value_weight), qkv_grads)
    mlp_gain_grad = gain_grad((gate_weight, up_weight), mlp_grads)

    return (
        block_output.reshape(micros, 1, tokens, width),
        input_grad.reshape(micros, 1, tokens, width),
        attention_gain_grad,
        qkv_grads[0] * gain_one,
        qkv_grads[1] * gain_one,
        qkv_grads[2] * gain_one,
        side_by_side(*output_grad).T,
        mlp_gain_grad,
        mlp_grads[0] * gain_two,
        mlp_grads[1] * gain_two,
        side_by_side(*down_grad).T,
    )


def solution(mesh):
    rows, row_split = P(None, "dp", ("head", "blk"), None), P(("dp", "blk"), "head")
    column_split, gain = P("head", ("dp", "blk")), P(("dp", "blk"))
    return jax.shard_map(
        on_device,
        mesh=mesh,
        in_specs=(
            rows, gain, row_split, row_split, row_split, column_split, gain, row_split, row_split, column_split, rows,
        ),
        out_specs=(
            rows, rows, gain, row_split, row_split, row_split, column_split, gain, row_split, row_split, column_split,
        ),
        check_vma=False,
    )
```

```python
import functools

import jax
import jax.numpy as jnp
import numpy as np
from jax import lax
from jax.experimental import pallas as pl
from jax.experimental.pallas import tpu as pltpu
from jax.sharding import PartitionSpec as P

HD = 64
EPSILON = 1e-05
ROPE_BASE = 130000.0
MASKED_SCORE = -1e30
F32 = jnp.float32
BF16 = jnp.bfloat16
LANES = 128
MESH = pl.DeviceIdType.MESH


def swap(value, axis, bit):
    count = lax.axis_size(axis)
    return lax.ppermute(value, axis, [(i, i ^ bit) for i in range(count)])


def bits_of(count):
    return [1 << i for i in range(count.bit_length() - 1)]


def replica_stages():
    upper = [("blk", bit) for bit in bits_of(lax.axis_size("blk"))[1:]]
    return upper + [("dp", bit) for bit in reversed(bits_of(lax.axis_size("dp")))]


def matmul(left_side, right_side):
    return jnp.dot(left_side, right_side, preferred_element_type=F32)


def matmul_nt(left_side, right_side):
    return lax.dot_general(left_side, right_side, (((1,), (1,)), ((), ())), preferred_element_type=F32)


def matmul_tn(left_side, right_side):
    return lax.dot_general(left_side, right_side, (((0,), (0,)), ((), ())), preferred_element_type=F32)


def feature_order():
    n_blk, n_dp = lax.axis_size("blk"), lax.axis_size("dp")
    order = np.zeros((1,), np.int32)
    for axis, bit in replica_stages():
        order = np.concatenate([order, order ^ (bit if axis == "blk" else bit * n_blk)])
    order = np.concatenate([order, order ^ 1])
    assert order.size == n_blk * n_dp
    mine = lax.axis_index("dp") * n_blk + lax.axis_index("blk")
    back = np.argsort(order).astype(np.int32)
    absolute = jnp.arange(order.size, dtype=jnp.int32) ^ mine
    return jnp.asarray(order) ^ mine, jnp.asarray(back)[absolute]


def reorder_kernel(count, order_ref, *refs):
    for source, target in zip(refs[:count], refs[count:]):
        blocks = order_ref.shape[0]
        piece = source.shape[1] // blocks
        for j in range(blocks):
            start = pl.multiple_of(order_ref[j] * piece, piece)
            target[:, j * piece : (j + 1) * piece] = source[:, pl.ds(start, piece)]


def reorder(order, *arrays):
    count, width = arrays[0].shape
    blocks = order.shape[0]
    piece = width // blocks
    if piece % LANES:
        return [jnp.take(rows.reshape(count, blocks, piece), order, axis=1).reshape(count, width) for rows in arrays]
    in_vmem = pl.BlockSpec(memory_space=pltpu.VMEM)
    return pl.pallas_call(
        functools.partial(reorder_kernel, len(arrays)),
        in_specs=[pl.BlockSpec(memory_space=pltpu.SMEM)] + [in_vmem] * len(arrays),
        out_specs=[in_vmem] * len(arrays),
        out_shape=[jax.ShapeDtypeStruct(rows.shape, rows.dtype) for rows in arrays],
    )(order, *arrays)


def turn_features(rows):
    half = rows.shape[1] // 2
    return jnp.concatenate([rows[:, half:], rows[:, :half]], 1)


def gather_tokens(rows, head_first):
    count = rows.shape[0]
    if head_first:
        other = swap(rows, "head", 1)
        far = swap(turn_features(jnp.concatenate([rows, other], 0)), "blk", 1)
        return jnp.concatenate([rows, far[:count], other, far[count:]], 0)
    both = jnp.concatenate([rows, swap(turn_features(rows), "blk", 1)], 0)
    return jnp.concatenate([both, swap(both, "head", 1)], 0)


def scatter_tokens(partial, head_first):
    partial = partial.astype(BF16)
    count = partial.shape[0] // 4
    if head_first:
        came = swap(partial[2 * count :], "head", 1)
        mine = partial[:count].astype(F32) + came[:count].astype(F32)
        theirs = (partial[count : 2 * count].astype(F32) + came[count:].astype(F32)).astype(BF16)
        return mine + swap(turn_features(theirs), "blk", 1).astype(F32)
    leaving = jnp.concatenate([partial[count : 2 * count], partial[3 * count :]], 0)
    came = swap(turn_features(leaving), "blk", 1)
    mine = partial[:count].astype(F32) + came[:count].astype(F32)
    theirs = (partial[2 * count : 3 * count].astype(F32) + came[count:].astype(F32)).astype(BF16)
    return mine + swap(theirs, "head", 1).astype(F32)


def own_and_other(columns):
    width = columns.shape[1] // 2
    place = lax.axis_index("blk") % 2
    return (
        lax.dynamic_slice_in_dim(columns, place * width, width, 1),
        lax.dynamic_slice_in_dim(columns, (1 - place) * width, width, 1),
    )


def gather_weight(own, other):
    streams = [own, swap(other, "blk", 1)]
    stages = replica_stages()
    for axis, bit in stages[:-1]:
        streams = [jnp.concatenate([held, swap(held, axis, bit)], 0) for held in streams]
    pieces = []
    for held in streams:
        pieces += [held, swap(held, *stages[-1])]
    return jnp.concatenate(pieces, 0)


def scatter_weight_grad(acts, grads):
    quarter = acts.shape[1] // 4
    stages = replica_stages()[::-1]

    def piece(place):
        return matmul_tn(acts[:, place * quarter : (place + 1) * quarter], grads).astype(BF16)

    streams = []
    for first in (2, 0):
        came = swap(piece(first + 1), *stages[0])
        held = piece(first).astype(F32) + came.astype(F32)
        for axis, bit in stages[1:]:
            half = held.shape[0] // 2
            held = held.astype(BF16)
            came = swap(held[half:], axis, bit)
            held = held[:half].astype(F32) + came.astype(F32)
        streams.append(held)
    return streams[1], swap(streams[0].astype(BF16), "blk", 1)


def side_by_side(own, other):
    other = other.astype(F32)
    low = lax.axis_index("blk") % 2 == 0
    return jnp.concatenate([jnp.where(low, own, other), jnp.where(low, other, own)], 1)


def head_groups():
    return lax.axis_size("blk") // 2


def to_sequences(parts):
    groups = head_groups()
    upper = lax.axis_index("blk") // 2
    width = parts[0].shape[1] // groups
    arrived = []
    for r in range(groups):
        chosen = jnp.stack([lax.dynamic_slice_in_dim(part, (upper ^ r) * width, width, 1) for part in parts])
        if r:
            chosen = lax.ppermute(chosen, "blk", [(i, i ^ (2 * r)) for i in range(2 * groups)])
        arrived.append(chosen.reshape(len(parts), 4, -1, width))
    return jnp.concatenate(arrived, 1)


def from_sequences(blocks):
    groups = head_groups()
    upper = lax.axis_index("blk") // 2
    count, _, tokens, width = blocks.shape
    arrived = []
    for r in range(groups):
        chosen = blocks[:, 4 * r : 4 * r + 4]
        if r:
            chosen = lax.ppermute(chosen, "blk", [(i, i ^ (2 * r)) for i in range(2 * groups)])
        arrived.append(chosen.reshape(count, 4 * tokens, width))
    stacked = jnp.stack(arrived)
    ordered = [lax.dynamic_index_in_dim(stacked, h ^ upper, 0, keepdims=False) for h in range(groups)]
    return jnp.concatenate(ordered, 2)


def block_order():
    n_blk, n_head = lax.axis_size("blk"), lax.axis_size("head")
    block = np.arange(n_blk * n_head, dtype=np.int32)
    r_head = (block // n_blk) ^ lax.axis_index("head")
    r_blk = (block % n_blk) ^ lax.axis_index("blk")
    return ((r_blk // 2) * 2 + r_head) * 2 + r_blk % 2


def rope_tables(length, lanes):
    half = HD // 2
    frequency = ROPE_BASE ** (-np.arange(half, dtype=np.float32) * np.float32(2.0 / HD))
    angles = np.arange(length, dtype=np.float32)[:, None] * frequency.astype(np.float32)[None, :]
    cosine, sine = np.cos(angles), np.sin(angles)
    return (
        jnp.asarray(np.tile(cosine, (1, lanes // half)), F32),
        jnp.asarray(np.tile(np.concatenate([-sine, sine], 1), (1, lanes // HD)), F32),
    )


def turned(rows, cosine, sine):
    half = HD // 2
    parts = []
    for start in range(0, rows.shape[1], HD):
        parts += [rows[:, start + half : start + HD], rows[:, start : start + half]]
    return rows * cosine + jnp.concatenate(parts, 1) * sine


def load_sequence(order_ref, qkv_ref, cosine_ref, sine_ref, held, tokens, blocks):
    def one(block, carry):
        place = order_ref[block]
        rows = pl.ds(pl.multiple_of(block * tokens, tokens), tokens)
        for part in range(3):
            value = qkv_ref[part, place]
            if part < 2:
                value = turned(value.astype(F32), cosine_ref[rows, :], sine_ref[rows, :]).astype(BF16)
            held[part][rows, :] = value
        return carry

    lax.fori_loop(0, blocks, one, 0)


def softmax_rows(query, keys, first_row):
    scores = matmul_nt(query, keys) * HD ** (-0.5)
    row = first_row + lax.broadcasted_iota(jnp.int32, scores.shape, 0)
    scores = jnp.where(lax.broadcasted_iota(jnp.int32, scores.shape, 1) <= row, scores, MASKED_SCORE)
    weights = jnp.exp(scores - jnp.max(scores, 1, keepdims=True))
    return weights, 1.0 / jnp.sum(weights, 1, keepdims=True)


def attend_kernel(tokens, blocks, rows_at_once, order_ref, qkv_ref, cosine_ref, sine_ref, out_ref, q_s, k_s, v_s):
    lanes = qkv_ref.shape[-1]
    load_sequence(order_ref, qkv_ref, cosine_ref, sine_ref, (q_s, k_s, v_s), tokens, blocks)
    for first in range(0, tokens * blocks, rows_at_once):
        last = first + rows_at_once
        results = []
        for lane in range(0, lanes, HD):
            head = slice(lane, lane + HD)
            weights, inverse = softmax_rows(q_s[first:last, head], k_s[:last, head], first)
            results.append(matmul(weights.astype(BF16), v_s[:last, head]) * inverse)
        result = jnp.concatenate(results, 1).astype(BF16)
        for offset in range(0, rows_at_once, tokens):
            out_ref[order_ref[(first + offset) // tokens]] = result[offset : offset + tokens]


def attend_back_kernel(
    tokens, blocks, rows_at_once, order_ref, qkv_ref, grad_ref, cosine_ref, sine_ref, out_ref,
    q_s, k_s, v_s, dk_s, dv_s,
):
    lanes = qkv_ref.shape[-1]
    load_sequence(order_ref, qkv_ref, cosine_ref, sine_ref, (q_s, k_s, v_s), tokens, blocks)
    dk_s[...] = jnp.zeros_like(dk_s)
    dv_s[...] = jnp.zeros_like(dv_s)
    for first in range(0, tokens * blocks, rows_at_once):
        last = first + rows_at_once
        arrived = [grad_ref[order_ref[row // tokens]] for row in range(first, last, tokens)]
        grad_rows = jnp.concatenate(arrived, 0)
        query_parts, key_parts, value_parts = [], [], []
        for lane in range(0, lanes, HD):
            head = slice(lane, lane + HD)
            query, keys, grad = q_s[first:last, head], k_s[:last, head], grad_rows[:, head]
            weights, inverse = softmax_rows(query, keys, first)
            probabilities = weights * inverse
            grad_prob = matmul_nt(grad, v_s[:last, head])
            row_delta = jnp.sum(probabilities * grad_prob, 1, keepdims=True)
            grad_scores = (probabilities * (grad_prob - row_delta) * HD ** (-0.5)).astype(BF16)
            query_parts.append(matmul(grad_scores, keys))
            key_parts.append(matmul_tn(grad_scores, query))
            value_parts.append(matmul_tn(probabilities.astype(BF16), grad))
        grad_query = jnp.concatenate(query_parts, 1)
        grad_query = turned(grad_query, cosine_ref[first:last, :], -sine_ref[first:last, :]).astype(BF16)
        for offset in range(0, rows_at_once, tokens):
            out_ref[0, order_ref[(first + offset) // tokens]] = grad_query[offset : offset + tokens]
        dk_s[:last, :] += jnp.concatenate(key_parts, 1)
        dv_s[:last, :] += jnp.concatenate(value_parts, 1)

    def one(block, carry):
        place = order_ref[block]
        rows = pl.ds(pl.multiple_of(block * tokens, tokens), tokens)
        out_ref[1, place] = turned(dk_s[rows, :], cosine_ref[rows, :], -sine_ref[rows, :]).astype(BF16)
        out_ref[2, place] = dv_s[rows, :].astype(BF16)
        return carry

    lax.fori_loop(0, blocks, one, 0)


def attention_call(order, qkv, tables, grad=None):
    _, blocks, tokens, width = qkv.shape
    length = blocks * tokens
    lanes = min(LANES, width)
    rows_at_once = min(256, length) if length <= 2048 else LANES
    back = grad is not None

    def fixed(j, order_ref):
        return (0, 0)

    part = pl.BlockSpec((blocks, tokens, lanes), lambda j, order_ref: (0, 0, j))
    three = pl.BlockSpec((3, blocks, tokens, lanes), lambda j, order_ref: (0, 0, 0, j))
    table = pl.BlockSpec((length, lanes), fixed)
    kernel = attend_back_kernel if back else attend_kernel
    scratch = [pltpu.VMEM((length, lanes), BF16)] * 3
    if back:
        scratch += [pltpu.VMEM((length, lanes), F32)] * 2
    products = 5 if back else 2
    return pl.pallas_call(
        functools.partial(kernel, tokens, blocks, rows_at_once),
        grid_spec=pltpu.PrefetchScalarGridSpec(
            num_scalar_prefetch=1,
            grid=(width // lanes,),
            in_specs=[three] + ([part] if back else []) + [table, table],
            out_specs=three if back else part,
            scratch_shapes=scratch,
        ),
        out_shape=jax.ShapeDtypeStruct(qkv.shape if back else qkv.shape[1:], BF16),
        compiler_params=pltpu.CompilerParams(vmem_limit_bytes=48 * 1024 * 1024),
        cost_estimate=pl.CostEstimate(
            flops=products * 4 * length * length * width,
            bytes_accessed=(7 if back else 4) * length * width * 2,
            transcendentals=length * length * (width // HD),
        ),
    )(order, qkv, *([grad] if back else []), *tables)


def greet():
    masks = [("head", 1)] + [("dp", bit) for bit in bits_of(lax.axis_size("dp"))]
    masks += [("blk", 1)] + [("blk", 2 * r) for r in range(1, head_groups())]
    barrier = pltpu.get_barrier_semaphore()
    for axis, mask in masks:
        pl.semaphore_signal(barrier, inc=1, device_id={axis: flipped(axis, mask)}, device_id_type=MESH)
    pl.semaphore_wait(barrier, len(masks))


def flipped(axis, mask):
    place, other = lax.axis_index(axis), 0
    for bit in bits_of(lax.axis_size(axis)):
        digit = (place // bit) % 2
        other = other + bit * ((1 - digit) if mask & bit else digit)
    return other


class Copies:
    def __init__(self, send, recv, local):
        self.send, self.recv, self.local = send, recv, local
        self.remote_count = self.local_count = 0
        self.sent = []

    def remote(self, source, target, axis, mask):
        k = self.remote_count
        self.remote_count += 1
        copy = pltpu.make_async_remote_copy(
            src_ref=source, dst_ref=target, send_sem=self.send.at[k], recv_sem=self.recv.at[k],
            device_id={axis: flipped(axis, mask)}, device_id_type=MESH,
        )
        copy.start()
        self.sent.append(copy)
        return copy

    def inside(self, source, target):
        copy = pltpu.make_async_copy(source, target, self.local.at[self.local_count])
        self.local_count += 1
        copy.start()
        return copy

    def is_unsent(self, copy):
        return any(copy is other for other in self.sent)

    def wait_sent(self, copy):
        copy.wait_send()
        self.sent = [other for other in self.sent if other is not copy]

    def finish(self):
        for copy in self.sent:
            copy.wait_send()


def halves_turned(rows):
    half = rows.shape[-1] // 2
    return jnp.concatenate([rows[:, half:], rows[:, :half]], 1)


class WeightGather:
    def __init__(self, copies, own, other, full):
        self.copies, self.full, self.stage = copies, full, 0
        self.mine = copies.inside(own, full.at[0, 0])
        self.copy = copies.remote(other, full.at[1, 0], "blk", 1)

    def advance(self):
        if self.mine is not None:
            self.mine.wait()
            self.mine = None
        self.copy.wait_recv()
        stages = replica_stages()
        if self.stage < len(stages):
            held = 1 << self.stage
            self.copy = self.copies.remote(
                self.full.at[:, 0:held], self.full.at[:, held : 2 * held], *stages[self.stage]
            )
        self.stage += 1


class TokenGather:
    def __init__(self, copies, rows, turned_rows, m, head_first=None):
        self.copies, self.rows, self.turned_rows, self.m = copies, rows, turned_rows, m
        self.head_first = m % 2 == 1 if head_first is None else head_first
        if self.head_first:
            self.copy = copies.remote(rows.at[m, 0, 0], rows.at[m, 1, 0], "head", 1)
        else:
            turned_rows[m, 0] = halves_turned(rows[m, 0, 0])
            self.copy = copies.remote(turned_rows.at[m, 0], rows.at[m, 0, 1], "blk", 1)
        self.first = self.copy

    def second(self):
        m, rows, turned_rows = self.m, self.rows, self.turned_rows
        self.copy.wait_recv()
        if self.head_first:
            turned_rows[m, 0] = halves_turned(rows[m, 0, 0])
            turned_rows[m, 1] = halves_turned(rows[m, 1, 0])
            self.copy = self.copies.remote(turned_rows.at[m], rows.at[m, :, 1], "blk", 1)
        else:
            self.copy = self.copies.remote(rows.at[m, 0], rows.at[m, 1], "head", 1)

    def end(self):
        self.copy.wait_recv()

    def release(self):
        self.copies.wait_sent(self.first)
        self.copies.wait_sent(self.copy)


class TokenScatter:
    def __init__(self, copies, partial, leaving, came, passing, last, total, m, head_first=None):
        self.copies, self.partial, self.came, self.passing = copies, partial, came, passing
        self.last, self.total, self.m = last, total, m
        self.head_first = m % 2 == 0 if head_first is None else head_first
        if self.head_first:
            self.copy = copies.remote(partial.at[m, 1], came.at[m], "head", 1)
        else:
            leaving[m, 0] = halves_turned(partial[m, 0, 1])
            leaving[m, 1] = halves_turned(partial[m, 1, 1])
            self.copy = copies.remote(leaving.at[m], came.at[m], "blk", 1)
        self.first = self.copy

    def second(self):
        m, partial = self.m, self.partial
        self.copy.wait_recv()
        kept = partial[m, 0, 1] if self.head_first else partial[m, 1, 0]
        theirs = (kept.astype(F32) + self.came[m, 1].astype(F32)).astype(BF16)
        if self.head_first:
            self.passing[m] = halves_turned(theirs)
            self.copy = self.copies.remote(self.passing.at[m], self.last.at[m], "blk", 1)
        else:
            self.passing[m] = theirs
            self.copy = self.copies.remote(self.passing.at[m], self.last.at[m], "head", 1)
        self.total[m] += partial[m, 0, 0].astype(F32) + self.came[m, 0].astype(F32)

    def end(self):
        self.copy.wait_recv()
        self.total[self.m] += self.last[self.m].astype(F32)

    def release_first(self):
        self.copies.wait_sent(self.first)

    def release_last(self):
        self.copies.wait_sent(self.copy)

    def release(self):
        self.release_first()
        self.release_last()


def place_of(block):
    n_blk = lax.axis_size("blk")
    head, blk = block // n_blk, block % n_blk
    near = (blk + lax.axis_index("blk")) % 2
    return blk // 2, ((head + lax.axis_index("head")) % 2) * 2 + near


def load_heads(seq, m, lane, cosine_ref, sine_ref, held):
    tokens = seq.shape[-2]
    lanes = held[0].shape[1]
    blocks = held[0].shape[0] // tokens

    def one(block, carry):
        upper, group = place_of(block)
        rows = pl.ds(pl.multiple_of(block * tokens, tokens), tokens)
        for part in range(3):
            value = seq[m, upper, part, group, :, pl.ds(lane, lanes)]
            if part < 2:
                value = turned(value.astype(F32), cosine_ref[rows, :], sine_ref[rows, :]).astype(BF16)
            held[part][rows, :] = value
        return carry

    lax.fori_loop(0, blocks, one, 0)


def attend(seq, out, m, cosine_ref, sine_ref, held):
    tokens, width = seq.shape[-2:]
    q_s, k_s, v_s = held
    length, lanes = q_s.shape
    rows_at_once = min(256, length) if length <= 2048 else LANES

    def rows_of(first, last, lane):
        results = []
        for start in range(0, lanes, HD):
            head = slice(start, start + HD)
            weights, inverse = softmax_rows(q_s[pl.ds(first, rows_at_once), head], k_s[:last, head], first)
            results.append(matmul(weights.astype(BF16), v_s[:last, head]) * inverse)
        result = jnp.concatenate(results, 1).astype(BF16)
        for offset in range(0, rows_at_once, tokens):
            upper, group = place_of((first + offset) // tokens)
            out[m, upper, group, :, pl.ds(lane, lanes)] = result[offset : offset + tokens]

    def heads(lane):
        load_heads(seq, m, lane, cosine_ref, sine_ref, held)
        over_rows(length, rows_at_once, lambda first, last: rows_of(first, last, lane))

    over_lanes(width, lanes, heads)


def over_rows(length, rows_at_once, body):
    if length // rows_at_once <= 8:
        for first in range(0, length, rows_at_once):
            body(first, first + rows_at_once)
        return

    def one(j, carry):
        body(pl.multiple_of(j * rows_at_once, rows_at_once), length)
        return carry

    lax.fori_loop(0, length // rows_at_once, one, 0)


def over_lanes(width, lanes, body):
    if width == lanes:
        body(0)
        return

    def one(j, carry):
        body(pl.multiple_of(j * lanes, lanes))
        return carry

    lax.fori_loop(0, width // lanes, one, 0)


def store_normed(values, target, at):
    scale = lax.rsqrt(jnp.mean(values * values, -1, keepdims=True) + EPSILON)
    target[at] = (values * scale).astype(BF16)


def front_kernel(sizes, *refs):
    micros, groups, n_att, n_mlp = sizes
    x_ref, g_in, g_turned, att_in, mlp_in, cosine_ref, sine_ref = refs[:7]
    refs = refs[7:]
    w_att, refs = refs[:n_att], refs[n_att:]
    w_mlp, refs = refs[:n_mlp], refs[n_mlp:]
    xg_out, seq_out, attended_out, mixed_out, x2_out, gg_out = refs[:6]
    (xg, x2, turned_rows, turned_more, w_in, w_out, made, seq, heads_out, attended, partial,
     leaving, came, passing, last, mixed, q_s, k_s, v_s, send, recv, local) = refs[6:]
    held = (q_s, k_s, v_s)
    each = range(micros)
    near = lax.axis_index("blk") % 2
    upper = lax.axis_index("blk") // 2
    width = x_ref.shape[-1]
    tokens = x_ref.shape[-2]
    heads_width = w_in.shape[-1]
    here = heads_width // groups
    copies = Copies(send, recv, local)

    greet()
    att = [WeightGather(copies, att_in.at[i, near], att_in.at[i, 1 - near], w_att[i]) for i in range(n_att)]
    gathers = []
    for m in each:
        store_normed(x_ref[m].astype(F32), xg, (m, 0, 0))
        gathers.append(TokenGather(copies, xg, turned_rows, m))
    for chunk in att:
        chunk.advance()
    per_weight = n_mlp // 3
    order = [(w, j) for j in range(per_weight) for w in range(2)] + [(2, j) for j in range(per_weight)]
    mlp = [
        WeightGather(
            copies, mlp_in.at[w, near * per_weight + j], mlp_in.at[w, (1 - near) * per_weight + j], full
        )
        for (w, j), full in zip(order, w_mlp)
    ]
    for gather in gathers:
        gather.second()
    grad_own = [copies.inside(g_in.at[m], gg_out.at[m, 0, 0]) for m in each]
    grad_rows = [copies.remote(g_turned.at[m], gg_out.at[m, 0, 1], "blk", 1) for m in each]
    stages = len(replica_stages())
    steps = [[] for _ in range(stages + n_att)]
    for s in range(stages):
        for i in range(n_att):
            steps[s + i].append(att[i])
    for step in steps:
        for chunk in step:
            if chunk.stage <= stages:
                chunk.advance()

    background = [[] for _ in range(stages + n_mlp + 1)]
    for i, chunk in enumerate(mlp):
        for s in range(stages + 1):
            background[i + s].append(chunk)
    done = [0]

    def pump(count):
        for step in background[done[0] : done[0] + count]:
            for chunk in reversed(step):
                chunk.advance()
        done[0] += count

    for gather in gathers:
        gather.end()
    writes = [copies.inside(xg, xg_out)]
    loads = [copies.inside(w_att[i], w_in.at[i]) for i in range(3)] + [copies.inside(w_att[3], w_out)]
    crossing = [[] for _ in each]
    mine = [[] for _ in each]
    tile = min(256, heads_width)
    for i in range(3):
        loads[i].wait()
        for m in each:
            rows = xg[m].reshape(4 * tokens, width)
            for start in range(0, heads_width, tile):
                columns = w_in[i, :, :, :, start : start + tile].reshape(width, tile)
                product = matmul(rows, columns).astype(BF16)
                for lane in range(0, tile, min(here, tile)):
                    place = (start + lane) // here
                    inner = (start + lane) % here
                    for group in range(4):
                        made[m, place, i, group, :, inner : inner + min(here, tile)] = product[
                            group * tokens : (group + 1) * tokens, lane : lane + min(here, tile)
                        ]
            mine[m].append(copies.inside(made.at[m, upper, i], seq.at[m, upper, i]))
            for r in range(1, groups):
                crossing[m].append(
                    copies.remote(made.at[m, flipped("blk", 2 * r) // 2, i], seq.at[m, upper, i], "blk", 2 * r)
                )
    for m in each:
        grad_own[m].wait()
        grad_rows[m].wait_recv()
        grad_rows[m] = copies.remote(gg_out.at[m, 0], gg_out.at[m, 1], "head", 1)
    returning = []
    for m in each:
        pump(1)
        for copy in mine[m]:
            copy.wait()
        for copy in crossing[m]:
            copy.wait_recv()
        attend(seq, heads_out, m, cosine_ref, sine_ref, held)
        back = [copies.inside(heads_out.at[m, upper], attended.at[m, upper])]
        for r in range(1, groups):
            back.append(
                copies.remote(heads_out.at[m, flipped("blk", 2 * r) // 2], attended.at[m, upper], "blk", 2 * r)
            )
        returning.append(back)
    writes.append(copies.inside(seq, seq_out))
    pump(1)
    loads[3].wait()
    scatters = []
    rows_tile = min(256, width)
    for m in each:
        returning[m][0].wait()
        for copy in returning[m][1:]:
            copy.wait_recv()
        rows = jnp.concatenate([attended[m, g].reshape(4 * tokens, here) for g in range(groups)], 1)
        _, replicas, piece, _ = w_out.shape
        for start in range(0, width, rows_tile):
            half, first = start // (replicas * piece), start // piece % replicas
            part = w_out[half, first : first + rows_tile // piece].reshape(rows_tile, heads_width)
            product = matmul_nt(rows, part).astype(BF16)
            for group in range(4):
                partial[m, group // 2, group % 2, :, start : start + rows_tile] = product[
                    group * tokens : (group + 1) * tokens
                ]
        mixed[m] = x_ref[m].astype(F32)
        scatters.append(TokenScatter(copies, partial, leaving, came, passing, last, mixed, m))
    writes.append(copies.inside(attended, attended_out))
    pump(1)
    for scatter in scatters:
        scatter.second()
    pump(1)
    gathers = []
    for m in each:
        scatters[m].end()
        store_normed(mixed[m], x2, (m, 0, 0))
        gathers.append(TokenGather(copies, x2, turned_more, m))
    writes.append(copies.inside(mixed, mixed_out))
    pump(1)
    for gather in gathers:
        gather.second()
    pump(1)
    for gather in gathers:
        gather.end()
    writes.append(copies.inside(x2, x2_out))
    pump(len(background) - done[0])
    for copy in grad_rows:
        copy.wait_recv()
    for copy in writes:
        copy.wait()
    copies.finish()


def front(x_rows, grad_rows, grad_turned, att_in, mlp_in, tables):
    micros, tokens, width = x_rows.shape
    n_att, _, piece, heads_width = att_in.shape
    n_weights, parts, _, columns = mlp_in.shape
    n_mlp = n_weights * parts // 2
    groups = head_groups()
    here = heads_width // groups
    replicas = width // piece // 2
    length, lanes = tables[0].shape
    any_space = pl.BlockSpec(memory_space=pl.ANY)
    in_vmem = pl.BlockSpec(memory_space=pltpu.VMEM)

    def bf16(*shape):
        return jax.ShapeDtypeStruct(shape, BF16)

    token_rows = (micros, 2, 2, tokens, width)
    outs = [bf16(2, replicas, piece, heads_width)] * n_att + [bf16(2, replicas, piece, columns)] * n_mlp
    outs += [
        bf16(*token_rows),
        bf16(micros, groups, 3, 4, tokens, here),
        bf16(micros, groups, 4, tokens, here),
        jax.ShapeDtypeStruct((micros, tokens, width), F32),
        bf16(*token_rows),
        bf16(*token_rows),
    ]

    def room(*shape):
        return pltpu.VMEM(shape, BF16)

    scratch = [
        room(*token_rows),
        room(*token_rows),
        room(micros, 2, tokens, width),
        room(micros, 2, tokens, width),
        room(3, 2, replicas, piece, heads_width),
        room(2, replicas, piece, heads_width),
        room(micros, groups, 3, 4, tokens, here),
        room(micros, groups, 3, 4, tokens, here),
        room(micros, groups, 4, tokens, here),
        room(micros, groups, 4, tokens, here),
        room(*token_rows),
        room(micros, 2, tokens, width),
        room(micros, 2, tokens, width),
        room(micros, tokens, width),
        room(micros, tokens, width),
        pltpu.VMEM((micros, tokens, width), F32),
        room(length, lanes),
        room(length, lanes),
        room(length, lanes),
        pltpu.SemaphoreType.DMA((192,)),
        pltpu.SemaphoreType.DMA((192,)),
        pltpu.SemaphoreType.DMA((64,)),
    ]
    results = pl.pallas_call(
        functools.partial(front_kernel, (micros, groups, n_att, n_mlp)),
        out_shape=outs,
        in_specs=[in_vmem] + [any_space] * 4 + [in_vmem, in_vmem],
        out_specs=[any_space] * len(outs),
        scratch_shapes=scratch,
        compiler_params=pltpu.CompilerParams(
            collective_id=0, has_side_effects=True, vmem_limit_bytes=60 * 1024 * 1024
        ),
    )(x_rows, grad_rows, grad_turned, att_in, mlp_in, *tables)
    w_att, results = results[:n_att], results[n_att:]
    w_mlp, results = results[:n_mlp], results[n_mlp:]
    return w_att, [w.reshape(width, -1) for w in w_mlp], results


def absolute_block(place):
    stages = replica_stages()
    n_blk = lax.axis_size("blk")
    bits = [("blk", 1, place >> len(stages) & 1)] + [(a, bit, place >> s & 1) for s, (a, bit) in enumerate(stages)]
    block = 0
    for axis, bit, here in bits:
        digit = (lax.axis_index(axis) // bit) % 2
        block = block + bit * ((1 - digit) if here else digit) * (1 if axis == "blk" else n_blk)
    return block


def feature_lanes(place, piece):
    return pl.ds(pl.multiple_of(absolute_block(place) * piece, piece), piece)


def to_own_order(read, width, piece):
    return jnp.concatenate([read(feature_lanes(j, piece)) for j in range(width // piece)], 1)


def to_absolute_order(rows, target, at, piece):
    for j in range(rows.shape[1] // piece):
        target[at, :, feature_lanes(j, piece)] = rows[:, j * piece : (j + 1) * piece]


def part_of(block):
    n_blk = lax.axis_size("blk")
    head, blk = block // n_blk, block % n_blk
    mine = lax.axis_index("blk")
    near = (blk + mine) % 2
    return (blk // 2 + mine // 2) % 2, ((head + lax.axis_index("head")) % 2) * 2 + near


def load_pair_heads(seq, lane, cosine_ref, sine_ref, held):
    tokens = seq.shape[-2]
    lanes = held[0].shape[1]
    blocks = held[0].shape[0] // tokens

    def one(block, carry):
        part, group = part_of(block)
        rows = pl.ds(pl.multiple_of(block * tokens, tokens), tokens)
        for i in range(3):
            value = seq[i, part, group, :, pl.ds(lane, lanes)]
            if i < 2:
                value = turned(value.astype(F32), cosine_ref[rows, :], sine_ref[rows, :]).astype(BF16)
            held[i][rows, :] = value
        return carry

    lax.fori_loop(0, blocks, one, 0)


def attend_pair(seq, out, lane, cosine_ref, sine_ref, held):
    tokens = seq.shape[-2]
    q_s, k_s, v_s = held
    length, lanes = q_s.shape
    rows_at_once = min(256, length)
    load_pair_heads(seq, lane, cosine_ref, sine_ref, held)
    for first in range(0, length, rows_at_once):
        last = first + rows_at_once
        results = []
        for start in range(0, lanes, HD):
            head = slice(start, start + HD)
            weights, inverse = softmax_rows(q_s[first:last, head], k_s[:last, head], first)
            results.append(matmul(weights.astype(BF16), v_s[:last, head]) * inverse)
        result = jnp.concatenate(results, 1).astype(BF16)
        for offset in range(0, rows_at_once, tokens):
            part, group = part_of((first + offset) // tokens)
            out[part, group, :, pl.ds(lane, lanes)] = result[offset : offset + tokens]


def attend_pair_back(seq, grad, out, lane, cosine_ref, sine_ref, held, sums):
    tokens = seq.shape[-2]
    q_s, k_s, v_s = held
    dk_s, dv_s = sums
    length, lanes = q_s.shape
    rows_at_once = min(256, length)
    load_pair_heads(seq, lane, cosine_ref, sine_ref, held)
    dk_s[...] = jnp.zeros_like(dk_s)
    dv_s[...] = jnp.zeros_like(dv_s)
    for first in range(0, length, rows_at_once):
        last = first + rows_at_once
        places = [part_of((first + offset) // tokens) for offset in range(0, rows_at_once, tokens)]
        grad_rows = jnp.concatenate([grad[p, g, :, pl.ds(lane, lanes)] for p, g in places], 0)
        query_parts, key_parts, value_parts = [], [], []
        for start in range(0, lanes, HD):
            head = slice(start, start + HD)
            query, keys, grad_part = q_s[first:last, head], k_s[:last, head], grad_rows[:, head]
            weights, inverse = softmax_rows(query, keys, first)
            probabilities = weights * inverse
            grad_prob = matmul_nt(grad_part, v_s[:last, head])
            row_delta = jnp.sum(probabilities * grad_prob, 1, keepdims=True)
            grad_scores = (probabilities * (grad_prob - row_delta) * HD ** (-0.5)).astype(BF16)
            query_parts.append(matmul(grad_scores, keys))
            key_parts.append(matmul_tn(grad_scores, query))
            value_parts.append(matmul_tn(probabilities.astype(BF16), grad_part))
        grad_query = jnp.concatenate(query_parts, 1)
        grad_query = turned(grad_query, cosine_ref[first:last, :], -sine_ref[first:last, :]).astype(BF16)
        for i, (p, g) in enumerate(places):
            out[0, p * 4 + g, :, pl.ds(lane, lanes)] = grad_query[i * tokens : (i + 1) * tokens]
        dk_s[:last, :] += jnp.concatenate(key_parts, 1)
        dv_s[:last, :] += jnp.concatenate(value_parts, 1)

    def one(block, carry):
        p, g = part_of(block)
        rows = pl.ds(pl.multiple_of(block * tokens, tokens), tokens)
        grad_key = turned(dk_s[rows, :], cosine_ref[rows, :], -sine_ref[rows, :])
        out[1, p * 4 + g, :, pl.ds(lane, lanes)] = grad_key.astype(BF16)
        out[2, p * 4 + g, :, pl.ds(lane, lanes)] = dv_s[rows, :].astype(BF16)
        return carry

    lax.fori_loop(0, length // tokens, one, 0)


def greet_pairs():
    masks = [("head", 1)] + [(axis, bit) for axis in ("blk", "dp") for bit in bits_of(lax.axis_size(axis))]
    barrier = pltpu.get_barrier_semaphore()
    for axis, mask in masks:
        pl.semaphore_signal(barrier, inc=1, device_id={axis: flipped(axis, mask)}, device_id_type=MESH)
    pl.semaphore_wait(barrier, len(masks))


def up_to(chunk, stage):
    while chunk.stage < stage:
        chunk.advance()


def store_product(product, target, part, columns):
    tokens = target.shape[-2]
    for group in range(4):
        target[part, group // 2, group % 2, :, columns] = product[group * tokens : (group + 1) * tokens]


def pair_front_kernel(sizes, *refs):
    n_att, n_mlp = sizes
    x_in, g_in, att_in, mlp_in, cosine_ref, sine_ref = refs[:6]
    refs = refs[6:]
    w_att, refs = refs[:n_att], refs[n_att:]
    (w_gu, w_down, grads_out, hidden_out), refs = refs[:4], refs[4:]
    xg_out, seq_out, attended_out, mixed_out, x2_out, gg_out, x_out, g_out = refs[:8]
    (x_raw, g_raw, x_own, g_own, g_turned, xg, x2, turned_rows, turned_more, w_in, w_out, seq, attended, partial,
     leaving, came, passing, last, mixed, slopes, activated, q_s, k_s, v_s, send, recv, local) = refs[8:]
    held = (q_s, k_s, v_s)
    near = lax.axis_index("blk") % 2
    upper = lax.axis_index("blk") // 2
    tokens, width = x_own.shape[-2:]
    heads_width = w_in.shape[-1]
    count = 4 * tokens
    piece = w_in.shape[-2]
    copies = Copies(send, recv, local)
    stages = len(replica_stages())

    loads = [copies.inside(x_in.at[upper, 0], x_raw.at[0]), copies.inside(g_in.at[upper, 0], g_raw.at[0])]
    greet_pairs()
    trade = copies.remote(x_in.at[1 - upper, 0], x_raw.at[1], "blk", 2)

    def att_chunk(i):
        return lambda: WeightGather(copies, att_in.at[i, near], att_in.at[i, 1 - near], w_att[i])

    def mlp_chunk(w, j, columns):
        per_weight = n_mlp // 3
        size = mlp_in.shape[-1]
        first = (2 * j + w if w < 2 else j) * size + columns.start
        full = (w_gu if w < 2 else w_down).at[:, :, :, first : first + columns.stop - columns.start]
        own, other = (mlp_in.at[w, at * per_weight + j, :, columns] for at in (near, 1 - near))
        return lambda: WeightGather(copies, own, other, full)

    whole, halves = slice(0, 2 * heads_width), [slice(0, heads_width), slice(heads_width, 2 * heads_width)]
    mlp_order = [(w, j, whole) for j in range(2) for w in range(2)] + [(2, 0, whole)] + [(2, 1, h) for h in halves]
    makers = [att_chunk(i) for i in range(n_att)] + [mlp_chunk(*chunk) for chunk in mlp_order]
    chunks = []

    def reach(k, stage):
        if 0 <= k < len(makers):
            while len(chunks) <= k:
                chunks.append(makers[len(chunks)]())
            up_to(chunks[k], stage)

    def step(k):
        reach(k - 2, stages + 1)
        reach(k - 1, 3)
        reach(k, 2)
        reach(k + ahead[0], 1)
        reach(k + ahead[0] + 1, 0)

    ahead = [1]

    reach(n_att - 1, 0)
    reach(0, 1)

    def own_rows(p):
        x_own[p] = to_own_order(lambda lanes: x_raw[p, :, lanes], width, piece)
        store_normed(x_own[p].astype(F32), xg, (p, 0, 0))
        return TokenGather(copies, xg, turned_rows, p, False)

    loads[0].wait()
    gathers = [own_rows(0)]
    step(0)
    gathers[0].second()
    step(1)
    trade.wait_recv()
    gathers.append(own_rows(1))
    step(2)
    w_loads = []

    def load_weight(i):
        reach(i, stages + 1)
        w_loads.append(copies.inside(w_att[i], w_in.at[i] if i < 3 else w_out))

    def project(i, p):
        rows = xg[p].reshape(count, width)
        for start in range(0, heads_width, 256):
            columns = w_in[i, :, :, :, start : start + 256].reshape(width, 256)
            product = matmul(rows, columns).astype(BF16)
            for group in range(4):
                seq[i, p, group, :, start : start + 256] = product[group * tokens : (group + 1) * tokens]

    gathers[1].second()
    step(3)
    trade = copies.remote(g_in.at[1 - upper, 0], g_raw.at[1], "blk", 2)
    loads[1].wait()
    for i in range(3):
        load_weight(i)
    gathers[0].end()
    for i in range(3):
        w_loads[i].wait()
        project(i, 0)
    gathers[1].end()
    for i in range(3):
        project(i, 1)
    store_xg = copies.inside(xg, xg_out)
    writes = [copies.inside(seq, seq_out), copies.inside(x_own, x_out)]
    first_gathers = gathers
    trade.wait_recv()
    grad_rows = []
    for p in range(2):
        g_own[p] = to_own_order(lambda lanes, p=p: g_raw[p, :, lanes], width, piece)
        g_turned[p] = halves_turned(g_own[p])
        mine = copies.inside(g_own.at[p], gg_out.at[p, 0, 0])
        grad_rows.append((mine, copies.remote(g_turned.at[p], gg_out.at[p, 0, 1], "blk", 1)))
    writes.append(copies.inside(g_own, g_out))
    lanes = q_s.shape[1]
    for at, lane in enumerate(range(0, heads_width, lanes)):
        attend_pair(seq, attended, lane, cosine_ref, sine_ref, held)
    load_weight(3)
    w_loads[3].wait()
    scatters = []
    for p in range(2):
        rows = attended[p].reshape(count, heads_width)
        for start in range(0, width, 256):
            half, first = start // (width // 2), start // piece % (width // piece // 2)
            part = w_out[half, first : first + 256 // piece].reshape(256, heads_width)
            store_product(matmul_nt(rows, part).astype(BF16), partial, p, slice(start, start + 256))
        mixed[p] = x_own[p].astype(F32)
        scatters.append(TokenScatter(copies, partial, leaving, came, passing, last, mixed, p))
    writes.append(copies.inside(attended, attended_out))
    step(4)
    for scatter in scatters:
        scatter.second()
    far = []
    for p, (mine, turned_copy) in enumerate(grad_rows):
        mine.wait()
        turned_copy.wait_recv()
        far.append(copies.remote(gg_out.at[p, 0], gg_out.at[p, 1], "head", 1))
    step(5)
    gathers = []
    for p in range(2):
        scatters[p].end()
        store_normed(mixed[p], x2, (p, 0, 0))
        gathers.append(TokenGather(copies, x2, turned_more, p))
    writes.append(copies.inside(mixed, mixed_out))
    step(6)
    for gather in gathers:
        gather.second()
    step(7)
    for gather in gathers:
        gather.end()
    writes.append(copies.inside(x2, x2_out))
    store_xg.wait()
    for gather in first_gathers:
        gather.release()
    for scatter in scatters:
        scatter.release()
    for copy in far:
        copy.wait_recv()
    load_rows = [copies.inside(gg_out, xg)]
    hidden = partial
    quarters = range(0, 2 * heads_width, heads_width)
    size = 2 * heads_width

    def tiles(body):
        def one(i, carry):
            body(i // 2, i % 2)
            return carry

        lax.fori_loop(0, 4, one, 0)

    def forward(j):
        for lane in quarters:
            sources = [w_gu.at[:, :, :, (2 * j + w) * size + lane : (2 * j + w) * size + lane + heads_width] for w in (0, 1)]
            loads = [copies.inside(source, w_in.at[w]) for w, source in enumerate(sources)]
            for load in loads:
                load.wait()
            lanes = slice(j * size + lane, j * size + lane + heads_width)

            def body(p, head, lanes=lanes):
                rows = x2[p, head].reshape(2 * tokens, width)
                gate = matmul(rows, w_in[0].reshape(width, heads_width))
                up = matmul(rows, w_in[1].reshape(width, heads_width))
                sigmoid = jax.nn.sigmoid(gate)
                active = gate * sigmoid
                slope = up * sigmoid * (1.0 + gate * (1.0 - sigmoid))
                shape = (2, tokens, heads_width)
                slopes[p, head, :, :, lanes] = slope.astype(BF16).reshape(shape)
                activated[p, head, :, :, lanes] = active.astype(BF16).reshape(shape)
                hidden[p, head, :, :, lanes] = (active * up).astype(BF16).reshape(shape)

            tiles(body)
        here = slice(j * size, (j + 1) * size)
        writes.append(copies.inside(hidden.at[:, :, :, :, here], hidden_out.at[:, :, :, :, here]))

    def backward(j, lane):
        lanes = slice(j * size + lane, j * size + lane + heads_width)
        copies.inside(w_down.at[:, :, :, lanes], w_in.at[2]).wait()

        def body(p, head):
            rows = xg[p, head].reshape(2 * tokens, width)
            grad_hidden = matmul(rows, w_in[2].reshape(width, heads_width)).reshape(2, tokens, heads_width)
            slopes[p, head, :, :, lanes] = (grad_hidden * slopes[p, head, :, :, lanes].astype(F32)).astype(BF16)
            activated[p, head, :, :, lanes] = (
                grad_hidden * activated[p, head, :, :, lanes].astype(F32)
            ).astype(BF16)

        tiles(body)
        for w, made in enumerate((slopes, activated)):
            first = (2 * j + w) * size + lane
            there = slice(first, first + heads_width)
            writes.append(copies.inside(made.at[:, :, :, :, lanes], grads_out.at[:, :, :, :, there]))

    reach(n_att + 1, stages + 1)
    forward(0)
    step(8)
    reach(n_att + 3, stages + 1)
    forward(1)
    for load in load_rows:
        load.wait()
    step(9)
    reach(n_att + 4, stages + 1)
    for lane in quarters:
        backward(0, lane)
    step(10)
    reach(n_att + 5, stages + 1)
    backward(1, 0)
    step(11)
    step(12)
    backward(1, heads_width)
    for copy in writes:
        copy.wait()
    copies.finish()


def pair_front(block_input, grad_output, att_in, mlp_in, tables):
    _, _, tokens, width = block_input.shape
    n_att, _, piece, heads_width = att_in.shape
    n_weights, parts, _, columns = mlp_in.shape
    n_mlp = n_weights * parts // 2
    replicas = width // piece // 2
    length, lanes = tables[0].shape
    any_space = pl.BlockSpec(memory_space=pl.ANY)
    in_vmem = pl.BlockSpec(memory_space=pltpu.VMEM)

    def bf16(*shape):
        return jax.ShapeDtypeStruct(shape, BF16)

    def room(*shape):
        return pltpu.VMEM(shape, BF16)

    token_rows = (2, 2, 2, tokens, width)
    outs = [bf16(2, replicas, piece, heads_width)] * n_att
    hidden_width = n_mlp // 3 * columns
    outs += [bf16(2, replicas, piece, 2 * hidden_width), bf16(2, replicas, piece, hidden_width)]
    outs += [bf16(2, 2, 2, tokens, 2 * hidden_width), bf16(2, 2, 2, tokens, hidden_width)]
    outs += [
        bf16(*token_rows),
        bf16(3, 2, 4, tokens, heads_width),
        bf16(2, 4, tokens, heads_width),
        jax.ShapeDtypeStruct((2, tokens, width), F32),
        bf16(*token_rows),
        bf16(*token_rows),
        bf16(2, tokens, width),
        bf16(2, tokens, width),
    ]
    own, pair = (2, tokens, width), (2, 2, tokens, width)
    scratch = [room(*shape) for shape in [own] * 5 + [token_rows] * 2 + [pair] * 2]
    scratch += [
        room(3, 2, replicas, piece, heads_width),
        room(2, replicas, piece, heads_width),
        room(3, 2, 4, tokens, heads_width),
        room(2, 4, tokens, heads_width),
        room(*token_rows),
        room(*pair),
        room(*pair),
        room(*own),
        room(*own),
        pltpu.VMEM(own, F32),
        room(2, 2, 2, tokens, hidden_width),
        room(2, 2, 2, tokens, hidden_width),
        *[room(length, lanes)] * 3,
        pltpu.SemaphoreType.DMA((96,)),
        pltpu.SemaphoreType.DMA((96,)),
        pltpu.SemaphoreType.DMA((64,)),
    ]
    results = pl.pallas_call(
        functools.partial(pair_front_kernel, (n_att, n_mlp)),
        out_shape=outs,
        in_specs=[any_space] * 4 + [in_vmem] * 2,
        out_specs=[any_space] * len(outs),
        scratch_shapes=scratch,
        compiler_params=pltpu.CompilerParams(
            collective_id=2, has_side_effects=True, vmem_limit_bytes=63 * 1024 * 1024
        ),
    )(block_input, grad_output, att_in, mlp_in, *tables)
    w_att, results = results[:n_att], results[n_att:]
    return w_att, results[:2], results[2:4], results[4:]


class GradHalving:
    def __init__(self, copies, held, stored, landed, final, own, other):
        self.copies, self.held, self.stored, self.landed = copies, held, stored, landed
        self.final, self.own, self.other = final, own, other
        self.stages = replica_stages()[::-1][1:]
        self.stage, self.copy = -1, None

    def send(self):
        copies, held = self.copies, self.held
        for store in self.stored:
            store.wait()
        self.stored = []
        self.stage += 1
        if self.stage == len(self.stages):
            self.copy = copies.remote(held.at[1, 0], self.other, "blk", 1)
            return
        count = held.shape[1] >> self.stage
        self.copy = copies.remote(
            held.at[:, count // 2 : count], self.landed[self.stage], *self.stages[self.stage]
        )

    def arrive(self):
        self.copy.wait_recv()

    def load(self, rooms):
        count = self.held.shape[1] >> (self.stage + 1)
        columns = self.held.shape[-1]
        self.mine, self.came = (room.at[:, 0:count, :, 0:columns] for room in rooms)
        self.count = count
        self.loads = [
            self.copies.inside(self.held.at[:, 0:count], self.mine),
            self.copies.inside(self.landed[self.stage], self.came),
        ]

    def combine(self):
        copies, mine, came, count = self.copies, self.mine, self.came, self.count
        columns = self.held.shape[-1]
        for load in self.loads:
            load.wait()
        if self.stage == len(self.stages) - 1:
            self.final[:, 0:columns] = mine[0, 0].astype(F32) + came[0, 0].astype(F32)
            mine[1, 0] = (mine[1, 0].astype(F32) + came[1, 0].astype(F32)).astype(BF16)
            self.stored = [
                copies.inside(self.final.at[:, 0:columns], self.own),
                copies.inside(mine.at[1, 0], self.held.at[1, 0]),
            ]
            return

        def one(i, carry):
            half, row = i // count, i % count
            mine[half, row] = (mine[half, row].astype(F32) + came[half, row].astype(F32)).astype(BF16)
            return carry

        lax.fori_loop(0, 2 * count, one, 0)
        self.stored = [copies.inside(mine, self.held.at[:, 0:count])]


def pair_back_kernel(sizes, *refs):
    n_mlp, n_att = sizes
    stages = len(replica_stages()) - 1

    def take(number):
        nonlocal refs
        taken, refs = refs[:number], refs[number:]
        return taken

    e_in, produced_in, mixed_in, x2_in, gg_in, xg_in, attended_in, seq_in = take(8)
    g_ref, x_ref, cosine_ref, sine_ref = take(4)
    (grads_in, hidden_in), w_att = take(2), take(n_att)
    own_mlp, other_mlp, own_att, other_att = take(n_mlp), take(n_mlp), take(n_att), take(n_att)
    output_out, input_out = take(2)
    far_x2, far_gg, far_xg, far_rows, far_grads, far_hidden, far_attended, far_b = take(8)
    held_mlp, held_att = take(n_mlp), take(n_att)
    landed_mlp = [take(stages) for _ in range(n_mlp)]
    landed_att = [take(stages) for _ in range(n_att)]
    (partial, leaving, came, passing, last, came_o, last_o, came_c, last_c, total, total_c, rows_g,
     staged, room_a, room_b, room_c, room_d, final, grad_heads, rows_b, rows_o,
     acts, weights, seq, ready, q_s, k_s, v_s, dk_s, dv_s, send, recv, local) = refs
    parts = range(2)
    upper = lax.axis_index("blk") // 2
    tokens, width = x_ref.shape[-2:]
    heads_width = rows_o.shape[-1]
    size = 2 * heads_width
    _, held_pieces, piece, _ = held_mlp[0].shape
    copies = Copies(send, recv, local)
    count = 4 * tokens
    tile = 256
    half, quarter = width // 2, width // 4
    core = replica_stages()[-1]

    def to_core(source, target):
        return [
            copies.remote(
                source.at[:, :, :, :, low * half + quarter : (low + 1) * half],
                target.at[:, :, :, :, low * quarter : (low + 1) * quarter],
                *core,
            )
            for low in range(2)
        ]

    load_e = copies.inside(e_in, partial)
    load_mixed = copies.inside(mixed_in, total_c)
    greet_pairs()
    load_e.wait()
    for p in parts:
        total[p] = jnp.zeros_like(total[p])
    scatters = [TokenScatter(copies, partial, leaving, came, passing, last, total, p) for p in parts]
    x2_moves = to_core(x2_in, far_x2)
    mlp_moves = []
    for k in range(n_mlp):
        first = k % (2 * n_mlp // 3) * size
        columns = slice(first, first + size)
        source, target = (grads_in, far_grads) if k < 2 * n_mlp // 3 else (hidden_in, far_hidden)
        if k == 2 * n_mlp // 3:
            gg_moves = to_core(gg_in, far_gg)
        mlp_moves.append(
            copies.remote(source.at[:, :, :, :, columns], target.at[:, :, :, :, columns], *core)
        )
    xg_moves = to_core(xg_in, far_xg)
    attended_move = copies.remote(attended_in, far_attended, *core)

    def load_acts(source, far, moves):
        loads = [
            copies.inside(
                source.at[:, :, :, :, low * half : low * half + quarter],
                acts.at[0, :, :, :, :, low * quarter : (low + 1) * quarter],
            )
            for low in range(2)
        ]
        for move in moves:
            move.wait_recv()
        return loads + [copies.inside(far, acts.at[1])]

    chunks = []
    staging = []

    def weight_grad(lefts, held, landed, own, other):
        part_columns = lefts[0][2][0].shape[-1]
        columns = part_columns * len(lefts[0][2])
        for store in staging:
            store.wait()
        staging.clear()
        pieces = tile // piece
        per_low = quarter // tile

        def one(i, carry):
            low, part = i // per_low, i % per_low
            for j in range(len(lefts[0][2])):
                product = None
                for stride, left, rights in lefts:
                    lanes = pl.ds(pl.multiple_of(low * stride + part * tile, tile), tile)
                    rows = left[:, :, :, :, lanes].reshape(2 * count, tile)
                    term = matmul_tn(rows, rights[j][...].reshape(2 * count, part_columns))
                    product = term if product is None else product + term
                staged[low, pl.ds(part * pieces, pieces), :, j * part_columns : (j + 1) * part_columns] = (
                    product.astype(BF16).reshape(pieces, piece, part_columns)
                )
            return carry

        lax.fori_loop(0, 2 * per_low, one, 0)
        store = copies.inside(staged.at[:, :, :, 0:columns], held)
        staging.append(store)
        chunks.append(GradHalving(copies, held, [], landed, final, own, other))

    def send(k):
        if k < len(chunks) and chunks[k].stage < 0:
            if k == len(chunks) - 1:
                for store in staging:
                    store.wait()
                staging.clear()
            chunks[k].send()

    done = [0]

    def step():
        k = done[0]
        done[0] += 1
        here = []
        for at, rooms in ((k, (room_a, room_b)), (k - 1, (room_c, room_d))):
            if 0 <= at < len(chunks):
                chunks[at].arrive()
                if at == k:
                    send(k + 1)
                chunks[at].load(rooms)
                here.append(chunks[at])
        for chunk in here:
            chunk.combine()
        for chunk in here:
            chunk.send()
        if 0 <= k - 2 < len(chunks):
            chunks[k - 2].arrive()

    def load_grads(k):
        own_source, far_source = (grads_in, far_grads) if k < 2 * n_mlp // 3 else (hidden_in, far_hidden)
        mlp_moves[k].wait_recv()
        loads = []
        for device, source in enumerate((own_source, far_source)):
            for half_of in range(2):
                first = k % (2 * n_mlp // 3) * size + half_of * heads_width
                for row in range(8):
                    part = source.at[row // 4, row // 2 % 2, row % 2, :, first : first + heads_width]
                    loads.append(copies.inside(part, weights.at[2 * (k % 2) + device, half_of, row]))
        return loads

    acts_loads = load_acts(x2_in, far_x2, x2_moves)
    slots = [load_grads(0)]

    def mlp_chunk(k):
        for load in slots[k]:
            load.wait()
        if k + 1 < n_mlp:
            slots.append(load_grads(k + 1))
        lefts = [
            (quarter, acts.at[device], [weights.at[2 * (k % 2) + device, half_of] for half_of in range(2)])
            for device in range(2)
        ]
        weight_grad(lefts, held_mlp[k], landed_mlp[k], own_mlp[k], other_mlp[k])

    for load in acts_loads:
        load.wait()
    mlp_chunk(0)
    send(0)
    mlp_chunk(1)
    for scatter in scatters:
        scatter.second()
    load_mixed.wait()
    mlp_chunk(2)
    gathers = []
    for p in parts:
        scatters[p].end()
        scatters[p].release()
        mixed = total_c[p]
        scale = lax.rsqrt(jnp.mean(mixed * mixed, -1, keepdims=True) + EPSILON)
        total[p] = g_ref[p].astype(F32) + norm_back(total[p], mixed, scale)
        rows_g[p, 0, 0] = total[p].astype(BF16)
    for p in parts:
        gathers.append(TokenGather(copies, rows_g, leaving, p))
    load_produced = copies.inside(produced_in, partial)
    step()
    mlp_chunk(3)
    acts_loads = load_acts(gg_in, far_gg, gg_moves)
    for gather in gathers:
        gather.second()
    for load in acts_loads:
        load.wait()
    mlp_chunk(4)
    mlp_chunk(5)
    step()
    w_loads = [copies.inside(w_att[i], weights.at[slot]) for i, slot in ((3, 0), (0, 1), (1, 2))]
    load_seq = copies.inside(seq_in, seq)
    load_rows_o = [copies.inside(attended_in.at[p], rows_o.at[4 * p : 4 * p + 4]) for p in parts]
    attended_move.wait_recv()
    load_rows_o += [copies.inside(far_attended.at[p], weights.at[3, 0, 4 * p : 4 * p + 4]) for p in parts]
    for gather in gathers:
        gather.end()
        gather.release()
    rows_moves = to_core(rows_g, far_rows)
    load_produced.wait()
    scatters = [TokenScatter(copies, partial, leaving, came_o, passing, last_o, total_c, p) for p in parts]
    w_loads[0].wait()
    for p in parts:
        rows = rows_g[p].reshape(count, width)
        product = matmul(rows, weights[0].reshape(width, heads_width)).astype(BF16)
        for group in range(4):
            grad_heads[p, group] = product[group * tokens : (group + 1) * tokens]
    w_loads.append(copies.inside(w_att[2], weights.at[0]))
    step()
    for move in rows_moves:
        move.wait_recv()
    far_load = copies.inside(far_rows, acts.at[1])
    for load in load_rows_o + [far_load]:
        load.wait()
    lefts = [(half, rows_g, [rows_o]), (quarter, acts.at[1], [weights.at[3, 0]])]
    weight_grad(lefts, held_att[3], landed_att[3], own_att[3], other_att[3])
    acts_loads = load_acts(xg_in, far_xg, xg_moves)
    load_seq.wait()
    lanes = cosine_ref.shape[1]
    for at, lane in enumerate(range(0, heads_width, lanes)):
        attend_pair_back(seq, grad_heads, rows_b, lane, cosine_ref, sine_ref, (q_s, k_s, v_s), (dk_s, dv_s))
        if at == 2:
            for scatter in scatters:
                scatter.second()
        if at % 2:
            step()
    b_moves = [copies.remote(rows_b.at[i], far_b.at[i], *core) for i in range(3)]
    for load in w_loads[1:]:
        load.wait()
    out_scatters, scatters = scatters, []
    for p in parts:
        out_scatters[p].release_first()
        pieces = tile // piece
        for start in range(0, width, tile):
            low, first = start // half, start // piece % (half // piece)
            terms = []
            for i in range(3):
                weight = weights[(i + 1) % 3, low, first : first + pieces].reshape(tile, heads_width)
                terms.append(matmul_nt(rows_b[i, 4 * p : 4 * p + 4].reshape(count, heads_width), weight))
            product = functools.reduce(jnp.add, terms).astype(BF16)
            store_product(product, partial, p, slice(start, start + tile))
        scatters.append(TokenScatter(copies, partial, leaving, came_c, passing, last_c, total_c, p, True))
    step()
    b_loads = []
    for i in range(3):
        b_moves[i].wait_recv()
        b_loads.append(copies.inside(far_b.at[i], weights.at[i, 0]))
    for load in acts_loads:
        load.wait()
    for i in range(3):
        b_loads[i].wait()
        lefts = [(quarter, acts.at[0], [rows_b.at[i]]), (quarter, acts.at[1], [weights.at[i, 0]])]
        weight_grad(lefts, held_att[i], landed_att[i], own_att[i], other_att[i])
    for p in parts:
        out_scatters[p].end()
        out_scatters[p].release_last()
        to_absolute_order(total_c[p].astype(BF16), ready, p, piece)
        total_c[p] = jnp.zeros_like(total_c[p])
    stores = [copies.inside(ready.at[0], output_out.at[upper])]
    for scatter in scatters:
        scatter.second()
    step()
    send(len(chunks) - 2)
    trades = [copies.remote(ready.at[1], output_out.at[upper], "blk", 2)]
    step()
    send(len(chunks) - 1)
    for p in parts:
        scatters[p].end()
        scatters[p].release()
        values = x_ref[p].astype(F32)
        scale = lax.rsqrt(jnp.mean(values * values, -1, keepdims=True) + EPSILON)
        total[p] += norm_back(total_c[p], values, scale)
    stores[0].wait()
    copies.wait_sent(trades[0])
    for p in parts:
        to_absolute_order(total[p].astype(BF16), ready, p, piece)
    stores = [copies.inside(ready.at[0], input_out.at[upper])]
    trades.append(copies.remote(ready.at[1], input_out.at[upper], "blk", 2))
    while done[0] < len(chunks) + 2:
        step()
    for store in stores:
        store.wait()
    for trade in trades:
        trade.wait_recv()
    copies.finish()


def pair_back(partial, produced, held, tables, grads, w_att):
    normed_one, sequences, attended, mixed, normed_two, grad_rows, x_rows, g_rows = held
    _, tokens, width = x_rows.shape
    _, replicas, piece, heads_width = w_att[0].shape
    columns = 2 * heads_width
    n_mlp, n_att = sum(g.shape[-1] for g in grads) // columns, len(w_att)
    stages = len(replica_stages()) - 1
    any_space = pl.BlockSpec(memory_space=pl.ANY)
    in_vmem = pl.BlockSpec(memory_space=pltpu.VMEM)

    def bf16(*shape):
        return jax.ShapeDtypeStruct(shape, BF16)

    def f32(*shape):
        return jax.ShapeDtypeStruct(shape, F32)

    def room(*shape):
        return pltpu.VMEM(shape, BF16)

    widths = [columns] * n_mlp + [heads_width] * n_att
    token_rows, own, pair = (2, 2, 2, tokens, width), (2, tokens, width), (2, 2, tokens, width)
    half_rows = (2, 2, 2, tokens, width // 2)
    outs = [f32(piece, columns)] * n_mlp + [bf16(piece, columns)] * n_mlp
    outs += [f32(piece, heads_width)] * n_att + [bf16(piece, heads_width)] * n_att
    outs += [bf16(2, tokens, width)] * 2
    outs += [bf16(*half_rows)] * 4 + [bf16(*g.shape) for g in grads]
    outs += [bf16(2, 4, tokens, heads_width), bf16(3, 8, tokens, heads_width)]
    outs += [bf16(2, replicas // 2, piece, w) for w in widths]
    outs += [bf16(2, replicas >> (s + 2), piece, w) for w in widths for s in range(stages)]
    scratch = [
        room(*token_rows),
        room(*pair),
        room(*pair),
        room(*own),
        room(*own),
        room(*pair),
        room(*own),
        room(*pair),
        room(*own),
        pltpu.VMEM(own, F32),
        pltpu.VMEM(own, F32),
        room(*token_rows),
        room(2, replicas // 2, piece, columns),
        *[room(2, replicas // 4, piece, columns)] * 2,
        *[room(2, replicas // 8, piece, columns)] * 2,
        pltpu.VMEM((piece, columns), F32),
        room(2, 4, tokens, heads_width),
        room(3, 8, tokens, heads_width),
        room(8, tokens, heads_width),
        room(2, *half_rows),
        room(4, 2, replicas, piece, heads_width),
        room(3, 2, 4, tokens, heads_width),
        room(*own),
        *[room(*tables[0].shape)] * 3,
        *[pltpu.VMEM(tables[0].shape, F32)] * 2,
        pltpu.SemaphoreType.DMA((128,)),
        pltpu.SemaphoreType.DMA((128,)),
        pltpu.SemaphoreType.DMA((448,)),
    ]
    results = pl.pallas_call(
        functools.partial(pair_back_kernel, (n_mlp, n_att)),
        out_shape=outs,
        in_specs=[any_space] * 8 + [in_vmem] * 4 + [any_space] * (2 + n_att),
        out_specs=[any_space] * len(outs),
        scratch_shapes=scratch,
        compiler_params=pltpu.CompilerParams(
            collective_id=3, has_side_effects=True, vmem_limit_bytes=63 * 1024 * 1024
        ),
    )(
        partial, produced, mixed, normed_two, grad_rows, normed_one, attended, sequences, g_rows, x_rows,
        *tables, *grads, *w_att,
    )
    own_mlp, results = results[:n_mlp], results[n_mlp:]
    other_mlp, results = results[:n_mlp], results[n_mlp:]
    own_att, results = results[:n_att], results[n_att:]
    other_att, results = results[:n_att], results[n_att:]
    return list(zip(own_mlp, other_mlp)), list(zip(own_att, other_att)), results[0], results[1]


def scale_of(values):
    return lax.rsqrt(jnp.mean(values * values, -1, keepdims=True) + EPSILON)


def norm_back(grad, values, scale):
    return scale * grad - values * (scale * scale * scale) * jnp.mean(grad * values, -1, keepdims=True)


def on_device(
    block_input,
    attention_gain,
    query_weight,
    key_weight,
    value_weight,
    output_weight,
    mlp_gain,
    gate_weight,
    up_weight,
    down_weight,
    grad_output,
):
    micros, _, tokens, width = block_input.shape
    heads_width = query_weight.shape[1] // 2
    length = tokens * lax.axis_size("blk") * lax.axis_size("head")
    to_own, to_absolute = feature_order()
    order = block_order()
    tables = rope_tables(length, min(LANES, heads_width // head_groups()))
    each = range(micros)
    head_first = [m % 2 == 1 for m in each]

    gain_one = attention_gain.astype(F32)[:, None]
    gain_two = mlp_gain.astype(F32)[:, None]

    def scaled(weight, gain):
        return (weight.astype(F32) * gain).astype(BF16)

    def joined(parts):
        return jnp.concatenate(parts, 0)

    def columns_of(weight, parts):
        rows, columns = weight.shape
        return weight.reshape(rows, parts, columns // parts).swapaxes(0, 1)

    att_in = jnp.stack(
        [columns_of(scaled(w, gain_one), 2) for w in (query_weight, key_weight, value_weight)]
        + [columns_of(output_weight.T, 2)]
    )
    mlp_in = jnp.stack(
        [columns_of(scaled(w, gain_two), 4) for w in (gate_weight, up_weight)] + [columns_of(down_weight.T, 4)]
    )
    paired = micros == 2 and lax.axis_size("blk") == 4 and heads_width % LANES == 0 and 8 * tokens == width // 2
    paired = paired and mlp_in.shape[-1] == 2 * heads_width == width // 2 and mlp_in.shape[-2] == tokens
    hidden, grad_gate, grad_up = [], [], []
    grad_normed = produced = 0.0
    if paired:
        w_att, w_mlp, made, held = pair_front(block_input, grad_output, att_in, mlp_in, tables)
        grad_normed, produced = (
            matmul_nt(rows.reshape(-1, rows.shape[-1]), weight.reshape(width, -1)) for rows, weight in zip(made, w_mlp)
        )
    else:
        block_rows = [array.reshape(micros * tokens, width) for array in (block_input, grad_output)]
        inputs_low, grad_low = (rows.reshape(micros, tokens, width) for rows in reorder(to_own, *block_rows))
        grad_turned = turn_features(grad_low.reshape(micros * tokens, width)).reshape(micros, tokens, width)
        w_att, w_mlp, held = front(inputs_low, grad_low, grad_turned, att_in, mlp_in, tables)
        normed_one, sequences, attended, mixed, normed_two, grad_rows = held
        normed_two_all = normed_two.reshape(-1, width)
        grad_rows_all = grad_rows.reshape(-1, width)
        for gate_full, up_full, down_full in zip(w_mlp[0:4:2], w_mlp[1:4:2], w_mlp[4:]):
            gate = matmul(normed_two_all, gate_full)
            up = matmul(normed_two_all, up_full)
            sigmoid = jax.nn.sigmoid(gate)
            activated = gate * sigmoid
            hidden.append((activated * up).astype(BF16))
            grad_hidden = matmul(grad_rows_all, down_full)
            grad_gate.append((grad_hidden * up * sigmoid * (1.0 + gate * (1.0 - sigmoid))).astype(BF16))
            grad_up.append((grad_hidden * activated).astype(BF16))
            grad_normed += matmul_nt(grad_gate[-1], gate_full) + matmul_nt(grad_up[-1], up_full)
            produced += matmul_nt(hidden[-1], down_full)

    def split(rows):
        size = rows.shape[0] // micros
        return [rows[m * size : (m + 1) * size] for m in each]

    if paired:
        partials = [rows.astype(BF16).reshape(held[4].shape) for rows in (grad_normed, produced)]
        mlp_pairs, att_pairs, block_output, input_grad = pair_back(*partials, held, tables, made, w_att)

        def beside(pairs):
            return tuple(jnp.concatenate(side, 1) for side in zip(*pairs))

        gate_grad, up_grad, down_grad = beside(mlp_pairs[0:4:2]), beside(mlp_pairs[1:4:2]), beside(mlp_pairs[4:])
        output_grad = att_pairs[3]
        qkv_grads = [side_by_side(*pair) for pair in att_pairs[:3]]
    else:
        produced = split(produced)
        outputs = [(mixed[m] + scatter_tokens(produced[m], head_first[m])).astype(BF16) for m in each]
        upper = lax.axis_index("blk") // 2
        w_att = [w.reshape(width, -1) for w in w_att]
        normed_one_all = normed_one.reshape(-1, width)
        sequences = [lax.dynamic_index_in_dim(sequences, upper ^ r, 1, keepdims=False) for r in range(head_groups())]
        sequences = jnp.concatenate(sequences, 2)
        attended = jnp.concatenate([attended[:, g] for g in range(head_groups())], -1)
        attended_all = attended.reshape(micros * 4 * tokens, -1)
        grad_normed = split(grad_normed)
        grad_mixed = []
        for m in each:
            back_rows = norm_back(scatter_tokens(grad_normed[m], head_first[m]), mixed[m], scale_of(mixed[m]))
            grad_mixed.append(grad_low[m].astype(F32) + back_rows)
        gate_grad = scatter_weight_grad(normed_two_all, jnp.concatenate(grad_gate, 1))
        up_grad = scatter_weight_grad(normed_two_all, jnp.concatenate(grad_up, 1))
        down_grad = scatter_weight_grad(grad_rows_all, jnp.concatenate(hidden, 1))
        grad_mixed_rows = [gather_tokens(grad_mixed[m].astype(BF16), head_first[m]) for m in each]
        grad_qkv, input_grads = [], []
        for m in each:
            grad_attended = matmul(grad_mixed_rows[m], w_att[3]).astype(BF16)
            grad_sequences = attention_call(order, sequences[m], tables, to_sequences([grad_attended])[0])
            returned = from_sequences(grad_sequences)
            grad_qkv.append(jnp.concatenate([returned[0], returned[1], returned[2]], 1))
            terms = [matmul_nt(returned[i], w_att[i]) for i in range(3)]
            grad_normed_one = scatter_tokens(functools.reduce(jnp.add, terms), head_first[m])
            inputs = inputs_low[m].astype(F32)
            back_rows = norm_back(grad_normed_one, inputs, scale_of(inputs))
            input_grads.append((grad_mixed[m] + back_rows).astype(BF16))
        output_grad = scatter_weight_grad(joined(grad_mixed_rows), attended_all)
        qkv_grad = scatter_weight_grad(normed_one_all, joined(grad_qkv))
        qkv_grads = [
            side_by_side(*(side[:, i * heads_width : (i + 1) * heads_width] for side in qkv_grad)) for i in range(3)
        ]
        block_output, input_grad = reorder(to_absolute, joined(outputs), joined(input_grads))
    mlp_grads = [side_by_side(*gate_grad), side_by_side(*up_grad)]

    def gain_grad(weights, grads):
        terms = [jnp.sum(w.astype(F32) * g, 1) for w, g in zip(weights, grads)]
        here = functools.reduce(jnp.add, terms)
        return here + swap(here, "head", 1)

    attention_gain_grad = gain_grad((query_weight, key_weight, value_weight), qkv_grads)
    mlp_gain_grad = gain_grad((gate_weight, up_weight), mlp_grads)

    return (
        block_output.reshape(micros, 1, tokens, width),
        input_grad.reshape(micros, 1, tokens, width),
        attention_gain_grad,
        qkv_grads[0] * gain_one,
        qkv_grads[1] * gain_one,
        qkv_grads[2] * gain_one,
        side_by_side(*output_grad).T,
        mlp_gain_grad,
        mlp_grads[0] * gain_two,
        mlp_grads[1] * gain_two,
        side_by_side(*down_grad).T,
    )


def solution(mesh):
    rows, row_split = P(None, "dp", ("head", "blk"), None), P(("dp", "blk"), "head")
    column_split, gain = P("head", ("dp", "blk")), P(("dp", "blk"))
    return jax.shard_map(
        on_device,
        mesh=mesh,
        in_specs=(
            rows, gain, row_split, row_split, row_split, column_split, gain, row_split, row_split, column_split, rows,
        ),
        out_specs=(
            rows, rows, gain, row_split, row_split, row_split, column_split, gain, row_split, row_split, column_split,
        ),
        check_vma=False,
    )
```

```python
import functools

import jax
import jax.numpy as jnp
import numpy as np
from jax import lax
from jax.experimental import pallas as pl
from jax.experimental.pallas import tpu as pltpu
from jax.sharding import PartitionSpec as P

HD = 64
EPSILON = 1e-05
ROPE_BASE = 130000.0
MASKED_SCORE = -1e30
F32 = jnp.float32
BF16 = jnp.bfloat16
LANES = 128
MESH = pl.DeviceIdType.MESH


def swap(value, axis, bit):
    count = lax.axis_size(axis)
    return lax.ppermute(value, axis, [(i, i ^ bit) for i in range(count)])


def bits_of(count):
    return [1 << i for i in range(count.bit_length() - 1)]


def replica_stages():
    upper = [("blk", bit) for bit in bits_of(lax.axis_size("blk"))[1:]]
    return upper + [("dp", bit) for bit in reversed(bits_of(lax.axis_size("dp")))]


def matmul(left_side, right_side):
    return jnp.dot(left_side, right_side, preferred_element_type=F32)


def matmul_nt(left_side, right_side):
    return lax.dot_general(left_side, right_side, (((1,), (1,)), ((), ())), preferred_element_type=F32)


def matmul_tn(left_side, right_side):
    return lax.dot_general(left_side, right_side, (((0,), (0,)), ((), ())), preferred_element_type=F32)


def feature_order():
    n_blk, n_dp = lax.axis_size("blk"), lax.axis_size("dp")
    order = np.zeros((1,), np.int32)
    for axis, bit in replica_stages():
        order = np.concatenate([order, order ^ (bit if axis == "blk" else bit * n_blk)])
    order = np.concatenate([order, order ^ 1])
    assert order.size == n_blk * n_dp
    mine = lax.axis_index("dp") * n_blk + lax.axis_index("blk")
    back = np.argsort(order).astype(np.int32)
    absolute = jnp.arange(order.size, dtype=jnp.int32) ^ mine
    return jnp.asarray(order) ^ mine, jnp.asarray(back)[absolute]


def reorder_kernel(count, order_ref, *refs):
    for source, target in zip(refs[:count], refs[count:]):
        blocks = order_ref.shape[0]
        piece = source.shape[1] // blocks
        for j in range(blocks):
            start = pl.multiple_of(order_ref[j] * piece, piece)
            target[:, j * piece : (j + 1) * piece] = source[:, pl.ds(start, piece)]


def reorder(order, *arrays):
    count, width = arrays[0].shape
    blocks = order.shape[0]
    piece = width // blocks
    if piece % LANES:
        return [jnp.take(rows.reshape(count, blocks, piece), order, axis=1).reshape(count, width) for rows in arrays]
    in_vmem = pl.BlockSpec(memory_space=pltpu.VMEM)
    return pl.pallas_call(
        functools.partial(reorder_kernel, len(arrays)),
        in_specs=[pl.BlockSpec(memory_space=pltpu.SMEM)] + [in_vmem] * len(arrays),
        out_specs=[in_vmem] * len(arrays),
        out_shape=[jax.ShapeDtypeStruct(rows.shape, rows.dtype) for rows in arrays],
    )(order, *arrays)


def turn_features(rows):
    half = rows.shape[1] // 2
    return jnp.concatenate([rows[:, half:], rows[:, :half]], 1)


def gather_tokens(rows, head_first):
    count = rows.shape[0]
    if head_first:
        other = swap(rows, "head", 1)
        far = swap(turn_features(jnp.concatenate([rows, other], 0)), "blk", 1)
        return jnp.concatenate([rows, far[:count], other, far[count:]], 0)
    both = jnp.concatenate([rows, swap(turn_features(rows), "blk", 1)], 0)
    return jnp.concatenate([both, swap(both, "head", 1)], 0)


def scatter_tokens(partial, head_first):
    partial = partial.astype(BF16)
    count = partial.shape[0] // 4
    if head_first:
        came = swap(partial[2 * count :], "head", 1)
        mine = partial[:count].astype(F32) + came[:count].astype(F32)
        theirs = (partial[count : 2 * count].astype(F32) + came[count:].astype(F32)).astype(BF16)
        return mine + swap(turn_features(theirs), "blk", 1).astype(F32)
    leaving = jnp.concatenate([partial[count : 2 * count], partial[3 * count :]], 0)
    came = swap(turn_features(leaving), "blk", 1)
    mine = partial[:count].astype(F32) + came[:count].astype(F32)
    theirs = (partial[2 * count : 3 * count].astype(F32) + came[count:].astype(F32)).astype(BF16)
    return mine + swap(theirs, "head", 1).astype(F32)


def own_and_other(columns):
    width = columns.shape[1] // 2
    place = lax.axis_index("blk") % 2
    return (
        lax.dynamic_slice_in_dim(columns, place * width, width, 1),
        lax.dynamic_slice_in_dim(columns, (1 - place) * width, width, 1),
    )


def gather_weight(own, other):
    streams = [own, swap(other, "blk", 1)]
    stages = replica_stages()
    for axis, bit in stages[:-1]:
        streams = [jnp.concatenate([held, swap(held, axis, bit)], 0) for held in streams]
    pieces = []
    for held in streams:
        pieces += [held, swap(held, *stages[-1])]
    return jnp.concatenate(pieces, 0)


def scatter_weight_grad(acts, grads):
    quarter = acts.shape[1] // 4
    stages = replica_stages()[::-1]

    def piece(place):
        return matmul_tn(acts[:, place * quarter : (place + 1) * quarter], grads).astype(BF16)

    streams = []
    for first in (2, 0):
        came = swap(piece(first + 1), *stages[0])
        held = piece(first).astype(F32) + came.astype(F32)
        for axis, bit in stages[1:]:
            half = held.shape[0] // 2
            held = held.astype(BF16)
            came = swap(held[half:], axis, bit)
            held = held[:half].astype(F32) + came.astype(F32)
        streams.append(held)
    return streams[1], swap(streams[0].astype(BF16), "blk", 1)


def side_by_side(own, other):
    other = other.astype(F32)
    low = lax.axis_index("blk") % 2 == 0
    return jnp.concatenate([jnp.where(low, own, other), jnp.where(low, other, own)], 1)


def head_groups():
    return lax.axis_size("blk") // 2


def to_sequences(parts):
    groups = head_groups()
    upper = lax.axis_index("blk") // 2
    width = parts[0].shape[1] // groups
    arrived = []
    for r in range(groups):
        chosen = jnp.stack([lax.dynamic_slice_in_dim(part, (upper ^ r) * width, width, 1) for part in parts])
        if r:
            chosen = lax.ppermute(chosen, "blk", [(i, i ^ (2 * r)) for i in range(2 * groups)])
        arrived.append(chosen.reshape(len(parts), 4, -1, width))
    return jnp.concatenate(arrived, 1)


def from_sequences(blocks):
    groups = head_groups()
    upper = lax.axis_index("blk") // 2
    count, _, tokens, width = blocks.shape
    arrived = []
    for r in range(groups):
        chosen = blocks[:, 4 * r : 4 * r + 4]
        if r:
            chosen = lax.ppermute(chosen, "blk", [(i, i ^ (2 * r)) for i in range(2 * groups)])
        arrived.append(chosen.reshape(count, 4 * tokens, width))
    stacked = jnp.stack(arrived)
    ordered = [lax.dynamic_index_in_dim(stacked, h ^ upper, 0, keepdims=False) for h in range(groups)]
    return jnp.concatenate(ordered, 2)


def block_order():
    n_blk, n_head = lax.axis_size("blk"), lax.axis_size("head")
    block = np.arange(n_blk * n_head, dtype=np.int32)
    r_head = (block // n_blk) ^ lax.axis_index("head")
    r_blk = (block % n_blk) ^ lax.axis_index("blk")
    return ((r_blk // 2) * 2 + r_head) * 2 + r_blk % 2


def rope_tables(length, lanes):
    half = HD // 2
    frequency = ROPE_BASE ** (-np.arange(half, dtype=np.float32) * np.float32(2.0 / HD))
    angles = np.arange(length, dtype=np.float32)[:, None] * frequency.astype(np.float32)[None, :]
    cosine, sine = np.cos(angles), np.sin(angles)
    return (
        jnp.asarray(np.tile(cosine, (1, lanes // half)), F32),
        jnp.asarray(np.tile(np.concatenate([-sine, sine], 1), (1, lanes // HD)), F32),
    )


def turned(rows, cosine, sine):
    half = HD // 2
    parts = []
    for start in range(0, rows.shape[1], HD):
        parts += [rows[:, start + half : start + HD], rows[:, start : start + half]]
    return rows * cosine + jnp.concatenate(parts, 1) * sine


def load_sequence(order_ref, qkv_ref, cosine_ref, sine_ref, held, tokens, blocks):
    def one(block, carry):
        place = order_ref[block]
        rows = pl.ds(pl.multiple_of(block * tokens, tokens), tokens)
        for part in range(3):
            value = qkv_ref[part, place]
            if part < 2:
                value = turned(value.astype(F32), cosine_ref[rows, :], sine_ref[rows, :]).astype(BF16)
            held[part][rows, :] = value
        return carry

    lax.fori_loop(0, blocks, one, 0)


def softmax_rows(query, keys, first_row):
    scores = matmul_nt(query, keys) * HD ** (-0.5)
    row = first_row + lax.broadcasted_iota(jnp.int32, scores.shape, 0)
    scores = jnp.where(lax.broadcasted_iota(jnp.int32, scores.shape, 1) <= row, scores, MASKED_SCORE)
    weights = jnp.exp(scores - jnp.max(scores, 1, keepdims=True))
    return weights, 1.0 / jnp.sum(weights, 1, keepdims=True)


def attend_kernel(tokens, blocks, rows_at_once, order_ref, qkv_ref, cosine_ref, sine_ref, out_ref, q_s, k_s, v_s):
    lanes = qkv_ref.shape[-1]
    load_sequence(order_ref, qkv_ref, cosine_ref, sine_ref, (q_s, k_s, v_s), tokens, blocks)
    for first in range(0, tokens * blocks, rows_at_once):
        last = first + rows_at_once
        results = []
        for lane in range(0, lanes, HD):
            head = slice(lane, lane + HD)
            weights, inverse = softmax_rows(q_s[first:last, head], k_s[:last, head], first)
            results.append(matmul(weights.astype(BF16), v_s[:last, head]) * inverse)
        result = jnp.concatenate(results, 1).astype(BF16)
        for offset in range(0, rows_at_once, tokens):
            out_ref[order_ref[(first + offset) // tokens]] = result[offset : offset + tokens]


def attend_back_kernel(
    tokens, blocks, rows_at_once, order_ref, qkv_ref, grad_ref, cosine_ref, sine_ref, out_ref,
    q_s, k_s, v_s, dk_s, dv_s,
):
    lanes = qkv_ref.shape[-1]
    load_sequence(order_ref, qkv_ref, cosine_ref, sine_ref, (q_s, k_s, v_s), tokens, blocks)
    dk_s[...] = jnp.zeros_like(dk_s)
    dv_s[...] = jnp.zeros_like(dv_s)
    for first in range(0, tokens * blocks, rows_at_once):
        last = first + rows_at_once
        arrived = [grad_ref[order_ref[row // tokens]] for row in range(first, last, tokens)]
        grad_rows = jnp.concatenate(arrived, 0)
        query_parts, key_parts, value_parts = [], [], []
        for lane in range(0, lanes, HD):
            head = slice(lane, lane + HD)
            query, keys, grad = q_s[first:last, head], k_s[:last, head], grad_rows[:, head]
            weights, inverse = softmax_rows(query, keys, first)
            probabilities = weights * inverse
            grad_prob = matmul_nt(grad, v_s[:last, head])
            row_delta = jnp.sum(probabilities * grad_prob, 1, keepdims=True)
            grad_scores = (probabilities * (grad_prob - row_delta) * HD ** (-0.5)).astype(BF16)
            query_parts.append(matmul(grad_scores, keys))
            key_parts.append(matmul_tn(grad_scores, query))
            value_parts.append(matmul_tn(probabilities.astype(BF16), grad))
        grad_query = jnp.concatenate(query_parts, 1)
        grad_query = turned(grad_query, cosine_ref[first:last, :], -sine_ref[first:last, :]).astype(BF16)
        for offset in range(0, rows_at_once, tokens):
            out_ref[0, order_ref[(first + offset) // tokens]] = grad_query[offset : offset + tokens]
        dk_s[:last, :] += jnp.concatenate(key_parts, 1)
        dv_s[:last, :] += jnp.concatenate(value_parts, 1)

    def one(block, carry):
        place = order_ref[block]
        rows = pl.ds(pl.multiple_of(block * tokens, tokens), tokens)
        out_ref[1, place] = turned(dk_s[rows, :], cosine_ref[rows, :], -sine_ref[rows, :]).astype(BF16)
        out_ref[2, place] = dv_s[rows, :].astype(BF16)
        return carry

    lax.fori_loop(0, blocks, one, 0)


def attention_call(order, qkv, tables, grad=None):
    _, blocks, tokens, width = qkv.shape
    length = blocks * tokens
    lanes = min(LANES, width)
    rows_at_once = min(256, length) if length <= 2048 else LANES
    back = grad is not None

    def fixed(j, order_ref):
        return (0, 0)

    part = pl.BlockSpec((blocks, tokens, lanes), lambda j, order_ref: (0, 0, j))
    three = pl.BlockSpec((3, blocks, tokens, lanes), lambda j, order_ref: (0, 0, 0, j))
    table = pl.BlockSpec((length, lanes), fixed)
    kernel = attend_back_kernel if back else attend_kernel
    scratch = [pltpu.VMEM((length, lanes), BF16)] * 3
    if back:
        scratch += [pltpu.VMEM((length, lanes), F32)] * 2
    products = 5 if back else 2
    return pl.pallas_call(
        functools.partial(kernel, tokens, blocks, rows_at_once),
        grid_spec=pltpu.PrefetchScalarGridSpec(
            num_scalar_prefetch=1,
            grid=(width // lanes,),
            in_specs=[three] + ([part] if back else []) + [table, table],
            out_specs=three if back else part,
            scratch_shapes=scratch,
        ),
        out_shape=jax.ShapeDtypeStruct(qkv.shape if back else qkv.shape[1:], BF16),
        compiler_params=pltpu.CompilerParams(vmem_limit_bytes=48 * 1024 * 1024),
        cost_estimate=pl.CostEstimate(
            flops=products * 4 * length * length * width,
            bytes_accessed=(7 if back else 4) * length * width * 2,
            transcendentals=length * length * (width // HD),
        ),
    )(order, qkv, *([grad] if back else []), *tables)


def greet():
    masks = [("head", 1)] + [("dp", bit) for bit in bits_of(lax.axis_size("dp"))]
    masks += [("blk", 1)] + [("blk", 2 * r) for r in range(1, head_groups())]
    barrier = pltpu.get_barrier_semaphore()
    for axis, mask in masks:
        pl.semaphore_signal(barrier, inc=1, device_id={axis: flipped(axis, mask)}, device_id_type=MESH)
    pl.semaphore_wait(barrier, len(masks))


def flipped(axis, mask):
    place, other = lax.axis_index(axis), 0
    for bit in bits_of(lax.axis_size(axis)):
        digit = (place // bit) % 2
        other = other + bit * ((1 - digit) if mask & bit else digit)
    return other


class Copies:
    def __init__(self, send, recv, local):
        self.send, self.recv, self.local = send, recv, local
        self.remote_count = self.local_count = 0
        self.sent = []

    def remote(self, source, target, axis, mask):
        k = self.remote_count
        self.remote_count += 1
        copy = pltpu.make_async_remote_copy(
            src_ref=source, dst_ref=target, send_sem=self.send.at[k], recv_sem=self.recv.at[k],
            device_id={axis: flipped(axis, mask)}, device_id_type=MESH,
        )
        copy.start()
        self.sent.append(copy)
        return copy

    def inside(self, source, target):
        copy = pltpu.make_async_copy(source, target, self.local.at[self.local_count])
        self.local_count += 1
        copy.start()
        return copy

    def is_unsent(self, copy):
        return any(copy is other for other in self.sent)

    def wait_sent(self, copy):
        copy.wait_send()
        self.sent = [other for other in self.sent if other is not copy]

    def finish(self):
        for copy in self.sent:
            copy.wait_send()


def halves_turned(rows):
    half = rows.shape[-1] // 2
    return jnp.concatenate([rows[:, half:], rows[:, :half]], 1)


class WeightGather:
    def __init__(self, copies, own, other, full):
        self.copies, self.full, self.stage = copies, full, 0
        self.mine = copies.inside(own, full.at[0, 0])
        self.copy = copies.remote(other, full.at[1, 0], "blk", 1)

    def advance(self):
        if self.mine is not None:
            self.mine.wait()
            self.mine = None
        self.copy.wait_recv()
        stages = replica_stages()
        if self.stage < len(stages):
            held = 1 << self.stage
            self.copy = self.copies.remote(
                self.full.at[:, 0:held], self.full.at[:, held : 2 * held], *stages[self.stage]
            )
        self.stage += 1


def lane_halves(width):
    return [slice(0, width // 2), slice(width // 2, width)]


class TokenGather:
    def __init__(self, copies, rows, turned_rows, m, head_first=None):
        self.copies, self.rows, self.turned_rows, self.m = copies, rows, turned_rows, m
        self.head_first = m % 2 == 1 if head_first is None else head_first
        self.halves = lane_halves(rows.shape[-1])
        self.first, self.last = [], []
        for here, there in zip(self.halves, self.halves[::-1]):
            if self.head_first:
                copy = copies.remote(rows.at[m, 0, 0, :, here], rows.at[m, 1, 0, :, here], "head", 1)
            else:
                turned_rows[m, 0, :, there] = rows[m, 0, 0, :, here]
                copy = copies.remote(turned_rows.at[m, 0, :, there], rows.at[m, 0, 1, :, there], "blk", 1)
            self.first.append(copy)

    def second_half(self, h):
        m, rows, turned_rows = self.m, self.rows, self.turned_rows
        here, there = self.halves[h], self.halves[1 - h]
        self.first[h].wait_recv()
        if self.head_first:
            turned_rows[m, 0, :, there] = rows[m, 0, 0, :, here]
            turned_rows[m, 1, :, there] = rows[m, 1, 0, :, here]
            copy = self.copies.remote(turned_rows.at[m, :, :, there], rows.at[m, :, 1, :, there], "blk", 1)
        else:
            copy = self.copies.remote(rows.at[m, 0, :, :, there], rows.at[m, 1, :, :, there], "head", 1)
        self.last.append(copy)

    def second(self):
        seconds([self])

    def end(self):
        for copy in self.last:
            copy.wait_recv()

    def release(self):
        for copy in self.first + self.last:
            self.copies.wait_sent(copy)


class TokenScatter:
    def __init__(self, copies, partial, leaving, came, passing, last, total, m, head_first=None):
        self.copies, self.partial, self.came, self.passing = copies, partial, came, passing
        self.arrived, self.total, self.m = last, total, m
        self.head_first = m % 2 == 0 if head_first is None else head_first
        self.halves = lane_halves(partial.shape[-1])
        self.first, self.last = [], []
        for here, there in zip(self.halves, self.halves[::-1]):
            if self.head_first:
                copy = copies.remote(partial.at[m, 1, :, :, here], came.at[m, :, :, here], "head", 1)
            else:
                leaving[m, 0, :, there] = partial[m, 0, 1, :, here]
                leaving[m, 1, :, there] = partial[m, 1, 1, :, here]
                copy = copies.remote(leaving.at[m, :, :, there], came.at[m, :, :, there], "blk", 1)
            self.first.append(copy)

    def second_half(self, h):
        m, partial, came = self.m, self.partial, self.came
        self.first[h].wait_recv()
        here = self.halves[h] if self.head_first else self.halves[1 - h]
        there = self.halves[1 - h] if self.head_first else here
        kept = partial[m, 0, 1, :, here] if self.head_first else partial[m, 1, 0, :, here]
        self.passing[m, :, there] = (kept.astype(F32) + came[m, 1, :, here].astype(F32)).astype(BF16)
        axis = "blk" if self.head_first else "head"
        self.last.append(self.copies.remote(self.passing.at[m, :, there], self.arrived.at[m, :, there], axis, 1))
        self.total[m, :, here] += partial[m, 0, 0, :, here].astype(F32) + came[m, 0, :, here].astype(F32)

    def second(self):
        seconds([self])

    def end(self):
        for copy in self.last:
            copy.wait_recv()
        self.total[self.m] += self.arrived[self.m].astype(F32)

    def release_first(self):
        for copy in self.first:
            self.copies.wait_sent(copy)

    def release_last(self):
        for copy in self.last:
            self.copies.wait_sent(copy)

    def release(self):
        self.release_first()
        self.release_last()


def seconds(ways):
    for h in range(2):
        for way in ways:
            way.second_half(h)


def place_of(block):
    n_blk = lax.axis_size("blk")
    head, blk = block // n_blk, block % n_blk
    near = (blk + lax.axis_index("blk")) % 2
    return blk // 2, ((head + lax.axis_index("head")) % 2) * 2 + near


def load_heads(seq, m, lane, cosine_ref, sine_ref, held):
    tokens = seq.shape[-2]
    lanes = held[0].shape[1]
    blocks = held[0].shape[0] // tokens

    def one(block, carry):
        upper, group = place_of(block)
        rows = pl.ds(pl.multiple_of(block * tokens, tokens), tokens)
        for part in range(3):
            value = seq[m, upper, part, group, :, pl.ds(lane, lanes)]
            if part < 2:
                value = turned(value.astype(F32), cosine_ref[rows, :], sine_ref[rows, :]).astype(BF16)
            held[part][rows, :] = value
        return carry

    lax.fori_loop(0, blocks, one, 0)


def attend(seq, out, m, cosine_ref, sine_ref, held):
    tokens, width = seq.shape[-2:]
    q_s, k_s, v_s = held
    length, lanes = q_s.shape
    rows_at_once = min(256, length) if length <= 2048 else LANES

    def rows_of(first, last, lane):
        results = []
        for start in range(0, lanes, HD):
            head = slice(start, start + HD)
            weights, inverse = softmax_rows(q_s[pl.ds(first, rows_at_once), head], k_s[:last, head], first)
            results.append(matmul(weights.astype(BF16), v_s[:last, head]) * inverse)
        result = jnp.concatenate(results, 1).astype(BF16)
        for offset in range(0, rows_at_once, tokens):
            upper, group = place_of((first + offset) // tokens)
            out[m, upper, group, :, pl.ds(lane, lanes)] = result[offset : offset + tokens]

    def heads(lane):
        load_heads(seq, m, lane, cosine_ref, sine_ref, held)
        over_rows(length, rows_at_once, lambda first, last: rows_of(first, last, lane))

    over_lanes(width, lanes, heads)


def over_rows(length, rows_at_once, body):
    if length // rows_at_once <= 8:
        for first in range(0, length, rows_at_once):
            body(first, first + rows_at_once)
        return

    def one(j, carry):
        body(pl.multiple_of(j * rows_at_once, rows_at_once), length)
        return carry

    lax.fori_loop(0, length // rows_at_once, one, 0)


def over_lanes(width, lanes, body):
    if width == lanes:
        body(0)
        return

    def one(j, carry):
        body(pl.multiple_of(j * lanes, lanes))
        return carry

    lax.fori_loop(0, width // lanes, one, 0)


def store_normed(values, target, at):
    scale = lax.rsqrt(jnp.mean(values * values, -1, keepdims=True) + EPSILON)
    target[at] = (values * scale).astype(BF16)


def front_kernel(sizes, *refs):
    micros, groups, n_att, n_mlp = sizes
    x_ref, g_in, g_turned, att_in, mlp_in, cosine_ref, sine_ref = refs[:7]
    refs = refs[7:]
    w_att, refs = refs[:n_att], refs[n_att:]
    w_mlp, refs = refs[:n_mlp], refs[n_mlp:]
    xg_out, seq_out, attended_out, mixed_out, x2_out, gg_out = refs[:6]
    (xg, x2, turned_rows, turned_more, w_in, w_out, made, seq, heads_out, attended, partial,
     leaving, came, passing, last, mixed, q_s, k_s, v_s, send, recv, local) = refs[6:]
    held = (q_s, k_s, v_s)
    each = range(micros)
    near = lax.axis_index("blk") % 2
    upper = lax.axis_index("blk") // 2
    width = x_ref.shape[-1]
    tokens = x_ref.shape[-2]
    heads_width = w_in.shape[-1]
    here = heads_width // groups
    copies = Copies(send, recv, local)

    greet()
    att = [WeightGather(copies, att_in.at[i, near], att_in.at[i, 1 - near], w_att[i]) for i in range(n_att)]
    gathers = []
    for m in each:
        store_normed(x_ref[m].astype(F32), xg, (m, 0, 0))
        gathers.append(TokenGather(copies, xg, turned_rows, m))
    for chunk in att:
        chunk.advance()
    per_weight = n_mlp // 3
    order = [(w, j) for j in range(per_weight) for w in range(2)] + [(2, j) for j in range(per_weight)]
    mlp = [
        WeightGather(
            copies, mlp_in.at[w, near * per_weight + j], mlp_in.at[w, (1 - near) * per_weight + j], full
        )
        for (w, j), full in zip(order, w_mlp)
    ]
    for gather in gathers:
        gather.second()
    grad_own = [copies.inside(g_in.at[m], gg_out.at[m, 0, 0]) for m in each]
    grad_rows = [copies.remote(g_turned.at[m], gg_out.at[m, 0, 1], "blk", 1) for m in each]
    stages = len(replica_stages())
    steps = [[] for _ in range(stages + n_att)]
    for s in range(stages):
        for i in range(n_att):
            steps[s + i].append(att[i])
    for step in steps:
        for chunk in step:
            if chunk.stage <= stages:
                chunk.advance()

    background = [[] for _ in range(stages + n_mlp + 1)]
    for i, chunk in enumerate(mlp):
        for s in range(stages + 1):
            background[i + s].append(chunk)
    done = [0]

    def pump(count):
        for step in background[done[0] : done[0] + count]:
            for chunk in reversed(step):
                chunk.advance()
        done[0] += count

    for gather in gathers:
        gather.end()
    writes = [copies.inside(xg, xg_out)]
    loads = [copies.inside(w_att[i], w_in.at[i]) for i in range(3)] + [copies.inside(w_att[3], w_out)]
    crossing = [[] for _ in each]
    mine = [[] for _ in each]
    tile = min(256, heads_width)
    for i in range(3):
        loads[i].wait()
        for m in each:
            rows = xg[m].reshape(4 * tokens, width)
            for start in range(0, heads_width, tile):
                columns = w_in[i, :, :, :, start : start + tile].reshape(width, tile)
                product = matmul(rows, columns).astype(BF16)
                for lane in range(0, tile, min(here, tile)):
                    place = (start + lane) // here
                    inner = (start + lane) % here
                    for group in range(4):
                        made[m, place, i, group, :, inner : inner + min(here, tile)] = product[
                            group * tokens : (group + 1) * tokens, lane : lane + min(here, tile)
                        ]
            mine[m].append(copies.inside(made.at[m, upper, i], seq.at[m, upper, i]))
            for r in range(1, groups):
                crossing[m].append(
                    copies.remote(made.at[m, flipped("blk", 2 * r) // 2, i], seq.at[m, upper, i], "blk", 2 * r)
                )
    for m in each:
        grad_own[m].wait()
        grad_rows[m].wait_recv()
        grad_rows[m] = copies.remote(gg_out.at[m, 0], gg_out.at[m, 1], "head", 1)
    returning = []
    for m in each:
        pump(1)
        for copy in mine[m]:
            copy.wait()
        for copy in crossing[m]:
            copy.wait_recv()
        attend(seq, heads_out, m, cosine_ref, sine_ref, held)
        back = [copies.inside(heads_out.at[m, upper], attended.at[m, upper])]
        for r in range(1, groups):
            back.append(
                copies.remote(heads_out.at[m, flipped("blk", 2 * r) // 2], attended.at[m, upper], "blk", 2 * r)
            )
        returning.append(back)
    writes.append(copies.inside(seq, seq_out))
    pump(1)
    loads[3].wait()
    scatters = []
    rows_tile = min(256, width)
    for m in each:
        returning[m][0].wait()
        for copy in returning[m][1:]:
            copy.wait_recv()
        rows = jnp.concatenate([attended[m, g].reshape(4 * tokens, here) for g in range(groups)], 1)
        _, replicas, piece, _ = w_out.shape
        for start in range(0, width, rows_tile):
            half, first = start // (replicas * piece), start // piece % replicas
            part = w_out[half, first : first + rows_tile // piece].reshape(rows_tile, heads_width)
            product = matmul_nt(rows, part).astype(BF16)
            for group in range(4):
                partial[m, group // 2, group % 2, :, start : start + rows_tile] = product[
                    group * tokens : (group + 1) * tokens
                ]
        mixed[m] = x_ref[m].astype(F32)
        scatters.append(TokenScatter(copies, partial, leaving, came, passing, last, mixed, m))
    writes.append(copies.inside(attended, attended_out))
    pump(1)
    for scatter in scatters:
        scatter.second()
    pump(1)
    gathers = []
    for m in each:
        scatters[m].end()
        store_normed(mixed[m], x2, (m, 0, 0))
        gathers.append(TokenGather(copies, x2, turned_more, m))
    writes.append(copies.inside(mixed, mixed_out))
    pump(1)
    for gather in gathers:
        gather.second()
    pump(1)
    for gather in gathers:
        gather.end()
    writes.append(copies.inside(x2, x2_out))
    pump(len(background) - done[0])
    for copy in grad_rows:
        copy.wait_recv()
    for copy in writes:
        copy.wait()
    copies.finish()


def front(x_rows, grad_rows, grad_turned, att_in, mlp_in, tables):
    micros, tokens, width = x_rows.shape
    n_att, _, piece, heads_width = att_in.shape
    n_weights, parts, _, columns = mlp_in.shape
    n_mlp = n_weights * parts // 2
    groups = head_groups()
    here = heads_width // groups
    replicas = width // piece // 2
    length, lanes = tables[0].shape
    any_space = pl.BlockSpec(memory_space=pl.ANY)
    in_vmem = pl.BlockSpec(memory_space=pltpu.VMEM)

    def bf16(*shape):
        return jax.ShapeDtypeStruct(shape, BF16)

    token_rows = (micros, 2, 2, tokens, width)
    outs = [bf16(2, replicas, piece, heads_width)] * n_att + [bf16(2, replicas, piece, columns)] * n_mlp
    outs += [
        bf16(*token_rows),
        bf16(micros, groups, 3, 4, tokens, here),
        bf16(micros, groups, 4, tokens, here),
        jax.ShapeDtypeStruct((micros, tokens, width), F32),
        bf16(*token_rows),
        bf16(*token_rows),
    ]

    def room(*shape):
        return pltpu.VMEM(shape, BF16)

    scratch = [
        room(*token_rows),
        room(*token_rows),
        room(micros, 2, tokens, width),
        room(micros, 2, tokens, width),
        room(3, 2, replicas, piece, heads_width),
        room(2, replicas, piece, heads_width),
        room(micros, groups, 3, 4, tokens, here),
        room(micros, groups, 3, 4, tokens, here),
        room(micros, groups, 4, tokens, here),
        room(micros, groups, 4, tokens, here),
        room(*token_rows),
        room(micros, 2, tokens, width),
        room(micros, 2, tokens, width),
        room(micros, tokens, width),
        room(micros, tokens, width),
        pltpu.VMEM((micros, tokens, width), F32),
        room(length, lanes),
        room(length, lanes),
        room(length, lanes),
        pltpu.SemaphoreType.DMA((192,)),
        pltpu.SemaphoreType.DMA((192,)),
        pltpu.SemaphoreType.DMA((64,)),
    ]
    results = pl.pallas_call(
        functools.partial(front_kernel, (micros, groups, n_att, n_mlp)),
        out_shape=outs,
        in_specs=[in_vmem] + [any_space] * 4 + [in_vmem, in_vmem],
        out_specs=[any_space] * len(outs),
        scratch_shapes=scratch,
        compiler_params=pltpu.CompilerParams(
            collective_id=0, has_side_effects=True, vmem_limit_bytes=60 * 1024 * 1024
        ),
    )(x_rows, grad_rows, grad_turned, att_in, mlp_in, *tables)
    w_att, results = results[:n_att], results[n_att:]
    w_mlp, results = results[:n_mlp], results[n_mlp:]
    return w_att, [w.reshape(width, -1) for w in w_mlp], results


def absolute_block(place):
    stages = replica_stages()
    n_blk = lax.axis_size("blk")
    bits = [("blk", 1, place >> len(stages) & 1)] + [(a, bit, place >> s & 1) for s, (a, bit) in enumerate(stages)]
    block = 0
    for axis, bit, here in bits:
        digit = (lax.axis_index(axis) // bit) % 2
        block = block + bit * ((1 - digit) if here else digit) * (1 if axis == "blk" else n_blk)
    return block


def feature_lanes(place, piece):
    return pl.ds(pl.multiple_of(absolute_block(place) * piece, piece), piece)


def to_own_order(read, width, piece):
    return jnp.concatenate([read(feature_lanes(j, piece)) for j in range(width // piece)], 1)


def to_absolute_order(rows, target, at, piece):
    for j in range(rows.shape[1] // piece):
        target[at, :, feature_lanes(j, piece)] = rows[:, j * piece : (j + 1) * piece]


def part_of(block):
    n_blk = lax.axis_size("blk")
    head, blk = block // n_blk, block % n_blk
    mine = lax.axis_index("blk")
    near = (blk + mine) % 2
    return (blk // 2 + mine // 2) % 2, ((head + lax.axis_index("head")) % 2) * 2 + near


def load_pair_heads(seq, lane, cosine_ref, sine_ref, held):
    tokens = seq.shape[-2]
    lanes = held[0].shape[1]
    blocks = held[0].shape[0] // tokens

    def one(block, carry):
        part, group = part_of(block)
        rows = pl.ds(pl.multiple_of(block * tokens, tokens), tokens)
        for i in range(3):
            value = seq[i, part, group, :, pl.ds(lane, lanes)]
            if i < 2:
                value = turned(value.astype(F32), cosine_ref[rows, :], sine_ref[rows, :]).astype(BF16)
            held[i][rows, :] = value
        return carry

    lax.fori_loop(0, blocks, one, 0)


def attend_pair(seq, out, lane, cosine_ref, sine_ref, held):
    tokens = seq.shape[-2]
    q_s, k_s, v_s = held
    length, lanes = q_s.shape
    rows_at_once = min(256, length)
    load_pair_heads(seq, lane, cosine_ref, sine_ref, held)
    for first in range(0, length, rows_at_once):
        last = first + rows_at_once
        results = []
        for start in range(0, lanes, HD):
            head = slice(start, start + HD)
            weights, inverse = softmax_rows(q_s[first:last, head], k_s[:last, head], first)
            results.append(matmul(weights.astype(BF16), v_s[:last, head]) * inverse)
        result = jnp.concatenate(results, 1).astype(BF16)
        for offset in range(0, rows_at_once, tokens):
            part, group = part_of((first + offset) // tokens)
            out[part, group, :, pl.ds(lane, lanes)] = result[offset : offset + tokens]


def attend_pair_back(seq, grad, out, lane, cosine_ref, sine_ref, held, sums):
    tokens = seq.shape[-2]
    q_s, k_s, v_s = held
    dk_s, dv_s = sums
    length, lanes = q_s.shape
    rows_at_once = min(256, length)
    load_pair_heads(seq, lane, cosine_ref, sine_ref, held)
    dk_s[...] = jnp.zeros_like(dk_s)
    dv_s[...] = jnp.zeros_like(dv_s)
    for first in range(0, length, rows_at_once):
        last = first + rows_at_once
        places = [part_of((first + offset) // tokens) for offset in range(0, rows_at_once, tokens)]
        grad_rows = jnp.concatenate([grad[p, g, :, pl.ds(lane, lanes)] for p, g in places], 0)
        query_parts, key_parts, value_parts = [], [], []
        for start in range(0, lanes, HD):
            head = slice(start, start + HD)
            query, keys, grad_part = q_s[first:last, head], k_s[:last, head], grad_rows[:, head]
            weights, inverse = softmax_rows(query, keys, first)
            probabilities = weights * inverse
            grad_prob = matmul_nt(grad_part, v_s[:last, head])
            row_delta = jnp.sum(probabilities * grad_prob, 1, keepdims=True)
            grad_scores = (probabilities * (grad_prob - row_delta) * HD ** (-0.5)).astype(BF16)
            query_parts.append(matmul(grad_scores, keys))
            key_parts.append(matmul_tn(grad_scores, query))
            value_parts.append(matmul_tn(probabilities.astype(BF16), grad_part))
        grad_query = jnp.concatenate(query_parts, 1)
        grad_query = turned(grad_query, cosine_ref[first:last, :], -sine_ref[first:last, :]).astype(BF16)
        for i, (p, g) in enumerate(places):
            out[0, p * 4 + g, :, pl.ds(lane, lanes)] = grad_query[i * tokens : (i + 1) * tokens]
        dk_s[:last, :] += jnp.concatenate(key_parts, 1)
        dv_s[:last, :] += jnp.concatenate(value_parts, 1)

    def one(block, carry):
        p, g = part_of(block)
        rows = pl.ds(pl.multiple_of(block * tokens, tokens), tokens)
        grad_key = turned(dk_s[rows, :], cosine_ref[rows, :], -sine_ref[rows, :])
        out[1, p * 4 + g, :, pl.ds(lane, lanes)] = grad_key.astype(BF16)
        out[2, p * 4 + g, :, pl.ds(lane, lanes)] = dv_s[rows, :].astype(BF16)
        return carry

    lax.fori_loop(0, length // tokens, one, 0)


def greet_pairs():
    masks = [("head", 1)] + [(axis, bit) for axis in ("blk", "dp") for bit in bits_of(lax.axis_size(axis))]
    barrier = pltpu.get_barrier_semaphore()
    for axis, mask in masks:
        pl.semaphore_signal(barrier, inc=1, device_id={axis: flipped(axis, mask)}, device_id_type=MESH)
    pl.semaphore_wait(barrier, len(masks))


def up_to(chunk, stage):
    while chunk.stage < stage:
        chunk.advance()


def store_product(product, target, part, columns):
    tokens = target.shape[-2]
    for group in range(4):
        target[part, group // 2, group % 2, :, columns] = product[group * tokens : (group + 1) * tokens]


def pair_front_kernel(sizes, *refs):
    n_att, n_mlp = sizes
    (x_in, g_in), refs = refs[:2], refs[2:]
    att_in, mlp_in, refs = refs[:n_att], refs[n_att : n_att + 3], refs[n_att + 3 :]
    (cosine_ref, sine_ref), refs = refs[:2], refs[2:]
    w_att, refs = refs[:n_att], refs[n_att:]
    (w_gu, w_down, grads_out, hidden_out), refs = refs[:4], refs[4:]
    xg_out, seq_out, attended_out, mixed_out, x2_out, gg_out, x_out, g_out = refs[:8]
    (x_raw, g_raw, x_own, g_own, g_turned, xg, x2, turned_rows, turned_more, w_in, w_out, seq, attended, partial,
     leaving, came, passing, last, mixed, slopes, activated, q_s, k_s, v_s, send, recv, local) = refs[8:]
    held = (q_s, k_s, v_s)
    near = lax.axis_index("blk") % 2
    upper = lax.axis_index("blk") // 2
    tokens, width = x_own.shape[-2:]
    heads_width = w_in.shape[-1]
    count = 4 * tokens
    piece = w_in.shape[-2]
    copies = Copies(send, recv, local)
    stages = len(replica_stages())

    loads = [copies.inside(x_in.at[upper, 0], x_raw.at[0]), copies.inside(g_in.at[upper, 0], g_raw.at[0])]
    greet_pairs()
    trade = copies.remote(x_in.at[1 - upper, 0], x_raw.at[1], "blk", 2)

    def att_chunk(i):
        return lambda: WeightGather(copies, att_in[i].at[near], att_in[i].at[1 - near], w_att[i])

    def mlp_chunk(w, j, columns):
        per_weight = n_mlp // 3
        size = mlp_in[w].shape[-1]
        first = (2 * j + w if w < 2 else j) * size + columns.start
        full = (w_gu if w < 2 else w_down).at[:, :, :, first : first + columns.stop - columns.start]
        own, other = (mlp_in[w].at[at * per_weight + j, :, columns] for at in (near, 1 - near))
        return lambda: WeightGather(copies, own, other, full)

    whole, halves = slice(0, 2 * heads_width), [slice(0, heads_width), slice(heads_width, 2 * heads_width)]
    mlp_order = [(w, j, whole) for j in range(2) for w in range(2)] + [(2, 0, whole)] + [(2, 1, h) for h in halves]
    makers = [att_chunk(i) for i in range(n_att)] + [mlp_chunk(*chunk) for chunk in mlp_order]
    chunks = []

    def reach(k, stage):
        if 0 <= k < len(makers):
            while len(chunks) <= k:
                chunks.append(makers[len(chunks)]())
            up_to(chunks[k], stage)

    def step(k):
        reach(k - 2, stages + 1)
        reach(k - 1, 3)
        reach(k, 2)
        reach(k + ahead[0], 1)
        reach(k + ahead[0] + 1, 0)

    ahead = [1]

    reach(n_att - 1, 0)
    reach(0, 1)

    def own_rows(p):
        x_own[p] = to_own_order(lambda lanes: x_raw[p, :, lanes], width, piece)
        store_normed(x_own[p].astype(F32), xg, (p, 0, 0))
        return TokenGather(copies, xg, turned_rows, p, False)

    loads[0].wait()
    gathers = [own_rows(0)]
    step(0)
    gathers[0].second()
    step(1)
    trade.wait_recv()
    gathers.append(own_rows(1))
    step(2)
    w_loads = []

    def load_weight(i):
        reach(i, stages + 1)
        w_loads.append(copies.inside(w_att[i], w_in.at[i] if i < 3 else w_out))

    def project(i, p):
        rows = xg[p].reshape(count, width)
        for start in range(0, heads_width, 256):
            columns = w_in[i, :, :, :, start : start + 256].reshape(width, 256)
            product = matmul(rows, columns).astype(BF16)
            for group in range(4):
                seq[i, p, group, :, start : start + 256] = product[group * tokens : (group + 1) * tokens]

    gathers[1].second()
    step(3)
    trade = copies.remote(g_in.at[1 - upper, 0], g_raw.at[1], "blk", 2)
    loads[1].wait()
    for i in range(3):
        load_weight(i)
    gathers[0].end()
    for i in range(3):
        w_loads[i].wait()
        project(i, 0)
    gathers[1].end()
    for i in range(3):
        project(i, 1)
    store_xg = copies.inside(xg, xg_out)
    writes = [copies.inside(seq, seq_out), copies.inside(x_own, x_out)]
    first_gathers = gathers
    trade.wait_recv()
    grad_rows = []
    for p in range(2):
        g_own[p] = to_own_order(lambda lanes, p=p: g_raw[p, :, lanes], width, piece)
        g_turned[p] = halves_turned(g_own[p])
        mine = copies.inside(g_own.at[p], gg_out.at[p, 0, 0])
        grad_rows.append((mine, copies.remote(g_turned.at[p], gg_out.at[p, 0, 1], "blk", 1)))
    writes.append(copies.inside(g_own, g_out))
    lanes = q_s.shape[1]
    for at, lane in enumerate(range(0, heads_width, lanes)):
        attend_pair(seq, attended, lane, cosine_ref, sine_ref, held)
    load_weight(3)
    w_loads[3].wait()
    scatters = []
    for p in range(2):
        rows = attended[p].reshape(count, heads_width)
        for start in range(0, width, 256):
            half, first = start // (width // 2), start // piece % (width // piece // 2)
            part = w_out[half, first : first + 256 // piece].reshape(256, heads_width)
            store_product(matmul_nt(rows, part).astype(BF16), partial, p, slice(start, start + 256))
        mixed[p] = x_own[p].astype(F32)
        scatters.append(TokenScatter(copies, partial, leaving, came, passing, last, mixed, p))
    writes.append(copies.inside(attended, attended_out))
    step(4)
    seconds(scatters)
    far = []
    for p, (mine, turned_copy) in enumerate(grad_rows):
        mine.wait()
        turned_copy.wait_recv()
        far.append(copies.remote(gg_out.at[p, 0], gg_out.at[p, 1], "head", 1))
    step(5)
    gathers = []
    for p in range(2):
        scatters[p].end()
        store_normed(mixed[p], x2, (p, 0, 0))
        gathers.append(TokenGather(copies, x2, turned_more, p))
    writes.append(copies.inside(mixed, mixed_out))
    step(6)
    seconds(gathers)
    step(7)
    for gather in gathers:
        gather.end()
    writes.append(copies.inside(x2, x2_out))
    store_xg.wait()
    for gather in first_gathers:
        gather.release()
    for scatter in scatters:
        scatter.release()
    for copy in far:
        copy.wait_recv()
    load_rows = [copies.inside(gg_out, xg)]
    hidden = partial
    quarters = range(0, 2 * heads_width, heads_width)
    size = 2 * heads_width

    def tiles(body):
        def one(i, carry):
            body(i // 2, i % 2)
            return carry

        lax.fori_loop(0, 4, one, 0)

    def forward(j):
        for lane in quarters:
            sources = [w_gu.at[:, :, :, (2 * j + w) * size + lane : (2 * j + w) * size + lane + heads_width] for w in (0, 1)]
            loads = [copies.inside(source, w_in.at[w]) for w, source in enumerate(sources)]
            for load in loads:
                load.wait()
            lanes = slice(j * size + lane, j * size + lane + heads_width)

            def body(p, head, lanes=lanes):
                rows = x2[p, head].reshape(2 * tokens, width)
                gate = matmul(rows, w_in[0].reshape(width, heads_width))
                up = matmul(rows, w_in[1].reshape(width, heads_width))
                sigmoid = jax.nn.sigmoid(gate)
                active = gate * sigmoid
                slope = up * sigmoid * (1.0 + gate * (1.0 - sigmoid))
                shape = (2, tokens, heads_width)
                slopes[p, head, :, :, lanes] = slope.astype(BF16).reshape(shape)
                activated[p, head, :, :, lanes] = active.astype(BF16).reshape(shape)
                hidden[p, head, :, :, lanes] = (active * up).astype(BF16).reshape(shape)

            tiles(body)
        here = slice(j * size, (j + 1) * size)
        writes.append(copies.inside(hidden.at[:, :, :, :, here], hidden_out.at[:, :, :, :, here]))

    def backward(j, lane):
        lanes = slice(j * size + lane, j * size + lane + heads_width)
        copies.inside(w_down.at[:, :, :, lanes], w_in.at[2]).wait()

        def body(p, head):
            rows = xg[p, head].reshape(2 * tokens, width)
            grad_hidden = matmul(rows, w_in[2].reshape(width, heads_width)).reshape(2, tokens, heads_width)
            slopes[p, head, :, :, lanes] = (grad_hidden * slopes[p, head, :, :, lanes].astype(F32)).astype(BF16)
            activated[p, head, :, :, lanes] = (
                grad_hidden * activated[p, head, :, :, lanes].astype(F32)
            ).astype(BF16)

        tiles(body)
        for w, made in enumerate((slopes, activated)):
            first = (2 * j + w) * size + lane
            there = slice(first, first + heads_width)
            writes.append(copies.inside(made.at[:, :, :, :, lanes], grads_out.at[:, :, :, :, there]))

    reach(n_att + 1, stages + 1)
    forward(0)
    step(8)
    reach(n_att + 3, stages + 1)
    forward(1)
    for load in load_rows:
        load.wait()
    step(9)
    reach(n_att + 4, stages + 1)
    for lane in quarters:
        backward(0, lane)
    step(10)
    reach(n_att + 5, stages + 1)
    backward(1, 0)
    step(11)
    step(12)
    backward(1, heads_width)
    for copy in writes:
        copy.wait()
    copies.finish()


def pair_front(block_input, grad_output, att_in, mlp_in, tables):
    _, _, tokens, width = block_input.shape
    n_att, (_, piece, heads_width) = len(att_in), att_in[0].shape
    parts, _, columns = mlp_in[0].shape
    n_mlp = len(mlp_in) * parts // 2
    replicas = width // piece // 2
    length, lanes = tables[0].shape
    any_space = pl.BlockSpec(memory_space=pl.ANY)
    in_vmem = pl.BlockSpec(memory_space=pltpu.VMEM)

    def bf16(*shape):
        return jax.ShapeDtypeStruct(shape, BF16)

    def room(*shape):
        return pltpu.VMEM(shape, BF16)

    token_rows = (2, 2, 2, tokens, width)
    outs = [bf16(2, replicas, piece, heads_width)] * n_att
    hidden_width = n_mlp // 3 * columns
    outs += [bf16(2, replicas, piece, 2 * hidden_width), bf16(2, replicas, piece, hidden_width)]
    outs += [bf16(2, 2, 2, tokens, 2 * hidden_width), bf16(2, 2, 2, tokens, hidden_width)]
    outs += [
        bf16(*token_rows),
        bf16(3, 2, 4, tokens, heads_width),
        bf16(2, 4, tokens, heads_width),
        jax.ShapeDtypeStruct((2, tokens, width), F32),
        bf16(*token_rows),
        bf16(*token_rows),
        bf16(2, tokens, width),
        bf16(2, tokens, width),
    ]
    own, pair = (2, tokens, width), (2, 2, tokens, width)
    scratch = [room(*shape) for shape in [own] * 5 + [token_rows] * 2 + [pair] * 2]
    scratch += [
        room(3, 2, replicas, piece, heads_width),
        room(2, replicas, piece, heads_width),
        room(3, 2, 4, tokens, heads_width),
        room(2, 4, tokens, heads_width),
        room(*token_rows),
        room(*pair),
        room(*pair),
        room(*own),
        room(*own),
        pltpu.VMEM(own, F32),
        room(2, 2, 2, tokens, hidden_width),
        room(2, 2, 2, tokens, hidden_width),
        *[room(length, lanes)] * 3,
        pltpu.SemaphoreType.DMA((96,)),
        pltpu.SemaphoreType.DMA((96,)),
        pltpu.SemaphoreType.DMA((64,)),
    ]
    results = pl.pallas_call(
        functools.partial(pair_front_kernel, (n_att, n_mlp)),
        out_shape=outs,
        in_specs=[any_space] * (2 + len(att_in) + len(mlp_in)) + [in_vmem] * 2,
        out_specs=[any_space] * len(outs),
        scratch_shapes=scratch,
        compiler_params=pltpu.CompilerParams(
            collective_id=2, has_side_effects=True, vmem_limit_bytes=63 * 1024 * 1024
        ),
    )(block_input, grad_output, *att_in, *mlp_in, *tables)
    w_att, results = results[:n_att], results[n_att:]
    return w_att, results[:2], results[2:4], results[4:]


class GradHalving:
    def __init__(self, copies, held, stored, landed, final, own, other):
        self.copies, self.held, self.stored, self.landed = copies, held, stored, landed
        self.final, self.own, self.other = final, own, other
        self.stages = replica_stages()[::-1][1:]
        self.stage, self.copy = -1, None

    def send(self):
        copies, held = self.copies, self.held
        for store in self.stored:
            store.wait()
        self.stored = []
        self.stage += 1
        if self.stage == len(self.stages):
            self.copy = copies.remote(held.at[1, 0], self.other, "blk", 1)
            return
        count = held.shape[1] >> self.stage
        self.copy = copies.remote(
            held.at[:, count // 2 : count], self.landed[self.stage], *self.stages[self.stage]
        )

    def arrive(self):
        self.copy.wait_recv()

    def load(self, rooms):
        count = self.held.shape[1] >> (self.stage + 1)
        columns = self.held.shape[-1]
        self.mine, self.came = (room.at[:, 0:count, :, 0:columns] for room in rooms)
        self.count = count
        self.loads = [
            self.copies.inside(self.held.at[:, 0:count], self.mine),
            self.copies.inside(self.landed[self.stage], self.came),
        ]

    def combine(self):
        copies, mine, came, count = self.copies, self.mine, self.came, self.count
        columns = self.held.shape[-1]
        for load in self.loads:
            load.wait()
        if self.stage == len(self.stages) - 1:
            self.final[:, 0:columns] = mine[0, 0].astype(F32) + came[0, 0].astype(F32)
            mine[1, 0] = (mine[1, 0].astype(F32) + came[1, 0].astype(F32)).astype(BF16)
            self.stored = [
                copies.inside(self.final.at[:, 0:columns], self.own),
                copies.inside(mine.at[1, 0], self.held.at[1, 0]),
            ]
            return

        def one(i, carry):
            half, row = i // count, i % count
            mine[half, row] = (mine[half, row].astype(F32) + came[half, row].astype(F32)).astype(BF16)
            return carry

        lax.fori_loop(0, 2 * count, one, 0)
        self.stored = [copies.inside(mine, self.held.at[:, 0:count])]


def pair_back_kernel(sizes, *refs):
    n_mlp, n_att = sizes
    stages = len(replica_stages()) - 1

    def take(number):
        nonlocal refs
        taken, refs = refs[:number], refs[number:]
        return taken

    e_in, produced_in, mixed_in, x2_in, gg_in, xg_in, attended_in, seq_in = take(8)
    g_ref, x_ref, cosine_ref, sine_ref = take(4)
    (grads_in, hidden_in), w_att = take(2), take(n_att)
    own_mlp, other_mlp, own_att, other_att = take(n_mlp), take(n_mlp), take(n_att), take(n_att)
    output_out, input_out = take(2)
    far_x2, far_gg, far_xg, far_rows, far_grads, far_hidden, far_attended, far_b = take(8)
    held_mlp, held_att = take(n_mlp), take(n_att)
    landed_mlp = [take(stages) for _ in range(n_mlp)]
    landed_att = [take(stages) for _ in range(n_att)]
    (partial, leaving, came, passing, last, came_o, last_o, came_c, last_c, total, total_c, rows_g,
     staged, room_a, room_b, room_c, room_d, final, grad_heads, rows_b, rows_o,
     acts, weights, seq, ready, q_s, k_s, v_s, dk_s, dv_s, send, recv, local) = refs
    parts = range(2)
    upper = lax.axis_index("blk") // 2
    tokens, width = x_ref.shape[-2:]
    heads_width = rows_o.shape[-1]
    size = 2 * heads_width
    _, held_pieces, piece, _ = held_mlp[0].shape
    copies = Copies(send, recv, local)
    count = 4 * tokens
    tile = 256
    half, quarter = width // 2, width // 4
    core = replica_stages()[-1]

    def to_core(source, target):
        return [
            copies.remote(
                source.at[:, :, :, :, low * half + quarter : (low + 1) * half],
                target.at[:, :, :, :, low * quarter : (low + 1) * quarter],
                *core,
            )
            for low in range(2)
        ]

    load_e = copies.inside(e_in, partial)
    load_mixed = copies.inside(mixed_in, total_c)
    greet_pairs()
    load_e.wait()
    for p in parts:
        total[p] = jnp.zeros_like(total[p])
    scatters = [TokenScatter(copies, partial, leaving, came, passing, last, total, p) for p in parts]
    x2_moves = to_core(x2_in, far_x2)
    mlp_moves = []
    for k in range(n_mlp):
        first = k % (2 * n_mlp // 3) * size
        columns = slice(first, first + size)
        source, target = (grads_in, far_grads) if k < 2 * n_mlp // 3 else (hidden_in, far_hidden)
        if k == 2 * n_mlp // 3:
            gg_moves = to_core(gg_in, far_gg)
        mlp_moves.append(
            copies.remote(source.at[:, :, :, :, columns], target.at[:, :, :, :, columns], *core)
        )
    xg_moves = to_core(xg_in, far_xg)
    attended_move = copies.remote(attended_in, far_attended, *core)

    def load_acts(source, far, moves):
        loads = [
            copies.inside(
                source.at[:, :, :, :, low * half : low * half + quarter],
                acts.at[0, :, :, :, :, low * quarter : (low + 1) * quarter],
            )
            for low in range(2)
        ]
        for move in moves:
            move.wait_recv()
        return loads + [copies.inside(far, acts.at[1])]

    chunks = []
    staging = []

    def weight_grad(lefts, held, landed, own, other):
        part_columns = lefts[0][2][0].shape[-1]
        columns = part_columns * len(lefts[0][2])
        for store in staging:
            store.wait()
        staging.clear()
        pieces = tile // piece
        per_low = quarter // tile

        def one(i, carry):
            low, part = i // per_low, i % per_low
            for j in range(len(lefts[0][2])):
                product = None
                for stride, left, rights in lefts:
                    lanes = pl.ds(pl.multiple_of(low * stride + part * tile, tile), tile)
                    rows = left[:, :, :, :, lanes].reshape(2 * count, tile)
                    term = matmul_tn(rows, rights[j][...].reshape(2 * count, part_columns))
                    product = term if product is None else product + term
                staged[low, pl.ds(part * pieces, pieces), :, j * part_columns : (j + 1) * part_columns] = (
                    product.astype(BF16).reshape(pieces, piece, part_columns)
                )
            return carry

        lax.fori_loop(0, 2 * per_low, one, 0)
        store = copies.inside(staged.at[:, :, :, 0:columns], held)
        staging.append(store)
        chunks.append(GradHalving(copies, held, [], landed, final, own, other))

    def send(k):
        if k < len(chunks) and chunks[k].stage < 0:
            if k == len(chunks) - 1:
                for store in staging:
                    store.wait()
                staging.clear()
            chunks[k].send()

    done = [0]

    def step():
        k = done[0]
        done[0] += 1
        here = []
        for at, rooms in ((k, (room_a, room_b)), (k - 1, (room_c, room_d))):
            if 0 <= at < len(chunks):
                chunks[at].arrive()
                if at == k:
                    send(k + 1)
                chunks[at].load(rooms)
                here.append(chunks[at])
        for chunk in here:
            chunk.combine()
        for chunk in here:
            chunk.send()
        if 0 <= k - 2 < len(chunks):
            chunks[k - 2].arrive()

    def load_grads(k):
        own_source, far_source = (grads_in, far_grads) if k < 2 * n_mlp // 3 else (hidden_in, far_hidden)
        mlp_moves[k].wait_recv()
        loads = []
        for device, source in enumerate((own_source, far_source)):
            for half_of in range(2):
                first = k % (2 * n_mlp // 3) * size + half_of * heads_width
                for row in range(8):
                    part = source.at[row // 4, row // 2 % 2, row % 2, :, first : first + heads_width]
                    loads.append(copies.inside(part, weights.at[2 * (k % 2) + device, half_of, row]))
        return loads

    acts_loads = load_acts(x2_in, far_x2, x2_moves)
    slots = [load_grads(0)]

    def mlp_chunk(k):
        for load in slots[k]:
            load.wait()
        if k + 1 < n_mlp:
            slots.append(load_grads(k + 1))
        lefts = [
            (quarter, acts.at[device], [weights.at[2 * (k % 2) + device, half_of] for half_of in range(2)])
            for device in range(2)
        ]
        weight_grad(lefts, held_mlp[k], landed_mlp[k], own_mlp[k], other_mlp[k])

    for load in acts_loads:
        load.wait()
    mlp_chunk(0)
    send(0)
    mlp_chunk(1)
    seconds(scatters)
    load_mixed.wait()
    mlp_chunk(2)
    gathers = []
    for p in parts:
        scatters[p].end()
        scatters[p].release()
        mixed = total_c[p]
        scale = lax.rsqrt(jnp.mean(mixed * mixed, -1, keepdims=True) + EPSILON)
        total[p] = g_ref[p].astype(F32) + norm_back(total[p], mixed, scale)
        rows_g[p, 0, 0] = total[p].astype(BF16)
    for p in parts:
        gathers.append(TokenGather(copies, rows_g, leaving, p))
    load_produced = copies.inside(produced_in, partial)
    step()
    mlp_chunk(3)
    acts_loads = load_acts(gg_in, far_gg, gg_moves)
    seconds(gathers)
    for load in acts_loads:
        load.wait()
    mlp_chunk(4)
    mlp_chunk(5)
    step()
    w_loads = [copies.inside(w_att[i], weights.at[slot]) for i, slot in ((3, 0), (0, 1), (1, 2))]
    load_seq = copies.inside(seq_in, seq)
    load_rows_o = [copies.inside(attended_in.at[p], rows_o.at[4 * p : 4 * p + 4]) for p in parts]
    attended_move.wait_recv()
    load_rows_o += [copies.inside(far_attended.at[p], weights.at[3, 0, 4 * p : 4 * p + 4]) for p in parts]
    for gather in gathers:
        gather.end()
        gather.release()
    rows_moves = to_core(rows_g, far_rows)
    load_produced.wait()
    scatters = [TokenScatter(copies, partial, leaving, came_o, passing, last_o, total_c, p) for p in parts]
    w_loads[0].wait()
    for p in parts:
        rows = rows_g[p].reshape(count, width)
        product = matmul(rows, weights[0].reshape(width, heads_width)).astype(BF16)
        for group in range(4):
            grad_heads[p, group] = product[group * tokens : (group + 1) * tokens]
    w_loads.append(copies.inside(w_att[2], weights.at[0]))
    step()
    for move in rows_moves:
        move.wait_recv()
    far_load = copies.inside(far_rows, acts.at[1])
    for load in load_rows_o + [far_load]:
        load.wait()
    lefts = [(half, rows_g, [rows_o]), (quarter, acts.at[1], [weights.at[3, 0]])]
    weight_grad(lefts, held_att[3], landed_att[3], own_att[3], other_att[3])
    acts_loads = load_acts(xg_in, far_xg, xg_moves)
    load_seq.wait()
    lanes = cosine_ref.shape[1]
    for at, lane in enumerate(range(0, heads_width, lanes)):
        attend_pair_back(seq, grad_heads, rows_b, lane, cosine_ref, sine_ref, (q_s, k_s, v_s), (dk_s, dv_s))
        if at == 2:
            seconds(scatters)
        if at % 2:
            step()
    b_moves = [copies.remote(rows_b.at[i], far_b.at[i], *core) for i in range(3)]
    for load in w_loads[1:]:
        load.wait()
    out_scatters, scatters = scatters, []
    for p in parts:
        out_scatters[p].release_first()
        pieces = tile // piece
        for start in range(0, width, tile):
            low, first = start // half, start // piece % (half // piece)
            terms = []
            for i in range(3):
                weight = weights[(i + 1) % 3, low, first : first + pieces].reshape(tile, heads_width)
                terms.append(matmul_nt(rows_b[i, 4 * p : 4 * p + 4].reshape(count, heads_width), weight))
            product = functools.reduce(jnp.add, terms).astype(BF16)
            store_product(product, partial, p, slice(start, start + tile))
        scatters.append(TokenScatter(copies, partial, leaving, came_c, passing, last_c, total_c, p, True))
    step()
    b_loads = []
    for i in range(3):
        b_moves[i].wait_recv()
        b_loads.append(copies.inside(far_b.at[i], weights.at[i, 0]))
    for load in acts_loads:
        load.wait()
    for i in range(3):
        b_loads[i].wait()
        lefts = [(quarter, acts.at[0], [rows_b.at[i]]), (quarter, acts.at[1], [weights.at[i, 0]])]
        weight_grad(lefts, held_att[i], landed_att[i], own_att[i], other_att[i])
    for p in parts:
        out_scatters[p].end()
        out_scatters[p].release_last()
        to_absolute_order(total_c[p].astype(BF16), ready, p, piece)
        total_c[p] = jnp.zeros_like(total_c[p])
    stores = [copies.inside(ready.at[0], output_out.at[upper])]
    seconds(scatters)
    step()
    send(len(chunks) - 2)
    trades = [copies.remote(ready.at[1], output_out.at[upper], "blk", 2)]
    step()
    send(len(chunks) - 1)
    for p in parts:
        scatters[p].end()
        scatters[p].release()
        values = x_ref[p].astype(F32)
        scale = lax.rsqrt(jnp.mean(values * values, -1, keepdims=True) + EPSILON)
        total[p] += norm_back(total_c[p], values, scale)
    stores[0].wait()
    copies.wait_sent(trades[0])
    for p in parts:
        to_absolute_order(total[p].astype(BF16), ready, p, piece)
    stores = [copies.inside(ready.at[0], input_out.at[upper])]
    trades.append(copies.remote(ready.at[1], input_out.at[upper], "blk", 2))
    while done[0] < len(chunks) + 2:
        step()
    for store in stores:
        store.wait()
    for trade in trades:
        trade.wait_recv()
    copies.finish()


def pair_back(partial, produced, held, tables, grads, w_att):
    normed_one, sequences, attended, mixed, normed_two, grad_rows, x_rows, g_rows = held
    _, tokens, width = x_rows.shape
    _, replicas, piece, heads_width = w_att[0].shape
    columns = 2 * heads_width
    n_mlp, n_att = sum(g.shape[-1] for g in grads) // columns, len(w_att)
    stages = len(replica_stages()) - 1
    any_space = pl.BlockSpec(memory_space=pl.ANY)
    in_vmem = pl.BlockSpec(memory_space=pltpu.VMEM)

    def bf16(*shape):
        return jax.ShapeDtypeStruct(shape, BF16)

    def f32(*shape):
        return jax.ShapeDtypeStruct(shape, F32)

    def room(*shape):
        return pltpu.VMEM(shape, BF16)

    widths = [columns] * n_mlp + [heads_width] * n_att
    token_rows, own, pair = (2, 2, 2, tokens, width), (2, tokens, width), (2, 2, tokens, width)
    half_rows = (2, 2, 2, tokens, width // 2)
    outs = [f32(piece, columns)] * n_mlp + [bf16(piece, columns)] * n_mlp
    outs += [f32(piece, heads_width)] * n_att + [bf16(piece, heads_width)] * n_att
    outs += [bf16(2, tokens, width)] * 2
    outs += [bf16(*half_rows)] * 4 + [bf16(*g.shape) for g in grads]
    outs += [bf16(2, 4, tokens, heads_width), bf16(3, 8, tokens, heads_width)]
    outs += [bf16(2, replicas // 2, piece, w) for w in widths]
    outs += [bf16(2, replicas >> (s + 2), piece, w) for w in widths for s in range(stages)]
    scratch = [
        room(*token_rows),
        room(*pair),
        room(*pair),
        room(*own),
        room(*own),
        room(*pair),
        room(*own),
        room(*pair),
        room(*own),
        pltpu.VMEM(own, F32),
        pltpu.VMEM(own, F32),
        room(*token_rows),
        room(2, replicas // 2, piece, columns),
        *[room(2, replicas // 4, piece, columns)] * 2,
        *[room(2, replicas // 8, piece, columns)] * 2,
        pltpu.VMEM((piece, columns), F32),
        room(2, 4, tokens, heads_width),
        room(3, 8, tokens, heads_width),
        room(8, tokens, heads_width),
        room(2, *half_rows),
        room(4, 2, replicas, piece, heads_width),
        room(3, 2, 4, tokens, heads_width),
        room(*own),
        *[room(*tables[0].shape)] * 3,
        *[pltpu.VMEM(tables[0].shape, F32)] * 2,
        pltpu.SemaphoreType.DMA((128,)),
        pltpu.SemaphoreType.DMA((128,)),
        pltpu.SemaphoreType.DMA((448,)),
    ]
    results = pl.pallas_call(
        functools.partial(pair_back_kernel, (n_mlp, n_att)),
        out_shape=outs,
        in_specs=[any_space] * 8 + [in_vmem] * 4 + [any_space] * (2 + n_att),
        out_specs=[any_space] * len(outs),
        scratch_shapes=scratch,
        compiler_params=pltpu.CompilerParams(
            collective_id=3, has_side_effects=True, vmem_limit_bytes=63 * 1024 * 1024
        ),
    )(
        partial, produced, mixed, normed_two, grad_rows, normed_one, attended, sequences, g_rows, x_rows,
        *tables, *grads, *w_att,
    )
    own_mlp, results = results[:n_mlp], results[n_mlp:]
    other_mlp, results = results[:n_mlp], results[n_mlp:]
    own_att, results = results[:n_att], results[n_att:]
    other_att, results = results[:n_att], results[n_att:]
    return list(zip(own_mlp, other_mlp)), list(zip(own_att, other_att)), results[0], results[1]


def scale_of(values):
    return lax.rsqrt(jnp.mean(values * values, -1, keepdims=True) + EPSILON)


def norm_back(grad, values, scale):
    return scale * grad - values * (scale * scale * scale) * jnp.mean(grad * values, -1, keepdims=True)


def on_device(
    block_input,
    attention_gain,
    query_weight,
    key_weight,
    value_weight,
    output_weight,
    mlp_gain,
    gate_weight,
    up_weight,
    down_weight,
    grad_output,
):
    micros, _, tokens, width = block_input.shape
    heads_width = query_weight.shape[1] // 2
    length = tokens * lax.axis_size("blk") * lax.axis_size("head")
    to_own, to_absolute = feature_order()
    order = block_order()
    tables = rope_tables(length, min(LANES, heads_width // head_groups()))
    each = range(micros)
    head_first = [m % 2 == 1 for m in each]

    gain_one = attention_gain.astype(F32)[:, None]
    gain_two = mlp_gain.astype(F32)[:, None]

    def scaled(weight, gain):
        return (weight.astype(F32) * gain).astype(BF16)

    def joined(parts):
        return jnp.concatenate(parts, 0)

    def columns_of(weight, parts):
        rows, columns = weight.shape
        return weight.reshape(rows, parts, columns // parts).swapaxes(0, 1)

    att_in = [columns_of(scaled(w, gain_one), 2) for w in (query_weight, key_weight, value_weight)]
    att_in.append(columns_of(output_weight.T, 2))
    mlp_in = [columns_of(scaled(w, gain_two), 4) for w in (gate_weight, up_weight)] + [columns_of(down_weight.T, 4)]
    part_rows, part_columns = mlp_in[0].shape[1:]
    paired = micros == 2 and lax.axis_size("blk") == 4 and heads_width % LANES == 0 and 8 * tokens == width // 2
    paired = paired and part_columns == 2 * heads_width == width // 2 and part_rows == tokens
    hidden, grad_gate, grad_up = [], [], []
    grad_normed = produced = 0.0
    if paired:
        w_att, w_mlp, made, held = pair_front(block_input, grad_output, att_in, mlp_in, tables)
        grad_normed, produced = (
            matmul_nt(rows.reshape(-1, rows.shape[-1]), weight.reshape(width, -1)) for rows, weight in zip(made, w_mlp)
        )
    else:
        block_rows = [array.reshape(micros * tokens, width) for array in (block_input, grad_output)]
        inputs_low, grad_low = (rows.reshape(micros, tokens, width) for rows in reorder(to_own, *block_rows))
        grad_turned = turn_features(grad_low.reshape(micros * tokens, width)).reshape(micros, tokens, width)
        w_att, w_mlp, held = front(inputs_low, grad_low, grad_turned, jnp.stack(att_in), jnp.stack(mlp_in), tables)
        normed_one, sequences, attended, mixed, normed_two, grad_rows = held
        normed_two_all = normed_two.reshape(-1, width)
        grad_rows_all = grad_rows.reshape(-1, width)
        for gate_full, up_full, down_full in zip(w_mlp[0:4:2], w_mlp[1:4:2], w_mlp[4:]):
            gate = matmul(normed_two_all, gate_full)
            up = matmul(normed_two_all, up_full)
            sigmoid = jax.nn.sigmoid(gate)
            activated = gate * sigmoid
            hidden.append((activated * up).astype(BF16))
            grad_hidden = matmul(grad_rows_all, down_full)
            grad_gate.append((grad_hidden * up * sigmoid * (1.0 + gate * (1.0 - sigmoid))).astype(BF16))
            grad_up.append((grad_hidden * activated).astype(BF16))
            grad_normed += matmul_nt(grad_gate[-1], gate_full) + matmul_nt(grad_up[-1], up_full)
            produced += matmul_nt(hidden[-1], down_full)

    def split(rows):
        size = rows.shape[0] // micros
        return [rows[m * size : (m + 1) * size] for m in each]

    if paired:
        partials = [rows.astype(BF16).reshape(held[4].shape) for rows in (grad_normed, produced)]
        mlp_pairs, att_pairs, block_output, input_grad = pair_back(*partials, held, tables, made, w_att)

        def beside(pairs):
            return tuple(jnp.concatenate(side, 1) for side in zip(*pairs))

        gate_grad, up_grad, down_grad = beside(mlp_pairs[0:4:2]), beside(mlp_pairs[1:4:2]), beside(mlp_pairs[4:])
        output_grad = att_pairs[3]
        qkv_grads = [side_by_side(*pair) for pair in att_pairs[:3]]
    else:
        produced = split(produced)
        outputs = [(mixed[m] + scatter_tokens(produced[m], head_first[m])).astype(BF16) for m in each]
        upper = lax.axis_index("blk") // 2
        w_att = [w.reshape(width, -1) for w in w_att]
        normed_one_all = normed_one.reshape(-1, width)
        sequences = [lax.dynamic_index_in_dim(sequences, upper ^ r, 1, keepdims=False) for r in range(head_groups())]
        sequences = jnp.concatenate(sequences, 2)
        attended = jnp.concatenate([attended[:, g] for g in range(head_groups())], -1)
        attended_all = attended.reshape(micros * 4 * tokens, -1)
        grad_normed = split(grad_normed)
        grad_mixed = []
        for m in each:
            back_rows = norm_back(scatter_tokens(grad_normed[m], head_first[m]), mixed[m], scale_of(mixed[m]))
            grad_mixed.append(grad_low[m].astype(F32) + back_rows)
        gate_grad = scatter_weight_grad(normed_two_all, jnp.concatenate(grad_gate, 1))
        up_grad = scatter_weight_grad(normed_two_all, jnp.concatenate(grad_up, 1))
        down_grad = scatter_weight_grad(grad_rows_all, jnp.concatenate(hidden, 1))
        grad_mixed_rows = [gather_tokens(grad_mixed[m].astype(BF16), head_first[m]) for m in each]
        grad_qkv, input_grads = [], []
        for m in each:
            grad_attended = matmul(grad_mixed_rows[m], w_att[3]).astype(BF16)
            grad_sequences = attention_call(order, sequences[m], tables, to_sequences([grad_attended])[0])
            returned = from_sequences(grad_sequences)
            grad_qkv.append(jnp.concatenate([returned[0], returned[1], returned[2]], 1))
            terms = [matmul_nt(returned[i], w_att[i]) for i in range(3)]
            grad_normed_one = scatter_tokens(functools.reduce(jnp.add, terms), head_first[m])
            inputs = inputs_low[m].astype(F32)
            back_rows = norm_back(grad_normed_one, inputs, scale_of(inputs))
            input_grads.append((grad_mixed[m] + back_rows).astype(BF16))
        output_grad = scatter_weight_grad(joined(grad_mixed_rows), attended_all)
        qkv_grad = scatter_weight_grad(normed_one_all, joined(grad_qkv))
        qkv_grads = [
            side_by_side(*(side[:, i * heads_width : (i + 1) * heads_width] for side in qkv_grad)) for i in range(3)
        ]
        block_output, input_grad = reorder(to_absolute, joined(outputs), joined(input_grads))
    mlp_grads = [side_by_side(*gate_grad), side_by_side(*up_grad)]

    def gain_grad(weights, grads):
        terms = [jnp.sum(w.astype(F32) * g, 1) for w, g in zip(weights, grads)]
        here = functools.reduce(jnp.add, terms)
        return here + swap(here, "head", 1)

    attention_gain_grad = gain_grad((query_weight, key_weight, value_weight), qkv_grads)
    mlp_gain_grad = gain_grad((gate_weight, up_weight), mlp_grads)

    return (
        block_output.reshape(micros, 1, tokens, width),
        input_grad.reshape(micros, 1, tokens, width),
        attention_gain_grad,
        qkv_grads[0] * gain_one,
        qkv_grads[1] * gain_one,
        qkv_grads[2] * gain_one,
        side_by_side(*output_grad).T,
        mlp_gain_grad,
        mlp_grads[0] * gain_two,
        mlp_grads[1] * gain_two,
        side_by_side(*down_grad).T,
    )


def solution(mesh):
    rows, row_split = P(None, "dp", ("head", "blk"), None), P(("dp", "blk"), "head")
    column_split, gain = P("head", ("dp", "blk")), P(("dp", "blk"))
    return jax.shard_map(
        on_device,
        mesh=mesh,
        in_specs=(
            rows, gain, row_split, row_split, row_split, column_split, gain, row_split, row_split, column_split, rows,
        ),
        out_specs=(
            rows, rows, gain, row_split, row_split, row_split, column_split, gain, row_split, row_split, column_split,
        ),
        check_vma=False,
    )
```
